256 devices in a mesh: section: 8 (over x, core), vocab: 32 (over z, y).
Axes of the slice: x: 4, y: 4, z: 8, core: 2. Of those that a mesh axis runs over, the one named last changes fastest.
Arguments:
- hidden: bfloat16 [640, 8192], P('section')
- gain: float32 [4, 8192], replicated, may hold values from 0.5 to 1.5
- exit_scale: float32 [4], replicated, may hold values from 0.25 to 2
- head_weight: bfloat16 [8192, 65536], P(None, ('section', 'vocab'))
- targets: int32 [640], replicated, may hold values from 0 to 65535
- exit_ids: int32 [640], replicated, may hold values from 0 to 3
- counts: int32 [8], replicated, may hold values from 1 to 80, 512 in all
Outputs:
- loss: float32 [], replicated
- grad_weight: bfloat16 [8192, 65536], P(None, ('section', 'vocab'))
- grad_hidden: bfloat16 [640, 8192], P('section', 'vocab')
The draws below stay inside these ranges and needn't reach their ends.
Inputs may be any that keep to these rules, and one draw needn't show every extreme that they name: Section s holds its live rows in its first counts[s] slots; the counts sum to 512 and some section holds exactly 80.
All inputs are finite; a program needn't handle non-finite values.
Results may differ from the reference program's by a relative error of at most 0.0085.
Values may be sent and summed in bfloat16 or wider, within the bound.
A program may use at most 128 MiB of HBM per device.

```python
import math
import jax
import jax.numpy as jnp
import numpy as np
from jax import lax

D = 8192
EXITS = 4
CAP = 80
ROWS_PAD = 640
TOTAL = 512
VOCAB = 65536
N_SECTION = 8


def draw_hidden(key, part):
    key = jax.random.fold_in(key, 1)
    first, second = jax.random.split(key, 2)
    scales = jnp.exp(jax.random.uniform(first, (ROWS_PAD, 1), jnp.float32, 0.0, math.log(10.0)))
    values = scales * jax.random.normal(second, (ROWS_PAD, D), jnp.float32)
    return values.astype(jnp.bfloat16)


def draw_head_weight(key, part):
    key = jax.random.fold_in(key, 2)
    values = jax.random.normal(key, (D, VOCAB), jnp.float32) * (3.0 / math.sqrt(D))
    return values.astype(jnp.bfloat16)


def set_ends(entries, key, smallest, top_value):
    dims = entries.shape
    index_at = [jax.random.randint(jax.random.fold_in(key, axis), (), 0, dims[axis]) for axis in range(len(dims))]
    entries = entries.at[tuple(index_at)].set(smallest)
    longest = dims.index(max(dims))
    index_at[longest] = (index_at[longest] + 1) % dims[longest]
    return entries.at[tuple(index_at)].set(top_value)


def rank_table(amount, slope):
    loads = [(1 << 20) // math.isqrt(rank ** slope) + 1 for rank in range(1, amount + 1)]
    width = 1 + sum(loads) // (1 << 30)
    return np.cumsum(np.array([max(1, weight // width) for weight in loads]))


def skewed_ids(rng, shape, amount, slope):
    grid = rank_table(amount, slope)
    ticket = jax.random.randint(jax.random.fold_in(rng, 1), shape, 0, int(grid[amount - 1]))
    standing = jnp.searchsorted(jnp.asarray(grid, jnp.int32), ticket, side="right")
    return jax.random.permutation(jax.random.fold_in(rng, 2), amount)[standing].astype(jnp.int32)


def split_up(number_of, total, limit, lean):
    weights = [(1 << 20) // math.isqrt(rank ** lean) + 1 for rank in range(2, number_of + 1)]
    surplus, holding = total - limit - (number_of - 1), [1] * (number_of - 1)
    while surplus > 0:
        candidates = [i for i in range(number_of - 1) if holding[i] < limit]
        pool, remaining = sum([weights[i] for i in candidates]), surplus
        for i in candidates:
            more = min(limit - holding[i], max(1, remaining * weights[i] // pool), surplus)
            holding[i] = holding[i] + more
            surplus = surplus - more
    return np.array([limit] + holding)


def ragged(key, amount, total, bound, lean):
    if amount == 2:
        one = jax.random.randint(key, (), max(1, total - bound), min(bound, total - 1) + 1)
        return jnp.stack([one, total - one])
    sizes = jnp.asarray(split_up(amount, total, bound, lean), jnp.int32)
    twos = (amount - 1) // 2
    donor, taker = sizes[1:1 + 2 * twos:2], sizes[2:2 + 2 * twos:2]
    room = jnp.minimum(donor - 1, bound - taker)
    passed = jax.random.randint(jax.random.fold_in(key, 1), (twos,), 0, 1 << 20) % (room + 1)
    sizes = sizes.at[1:1 + 2 * twos:2].set(donor - passed).at[2:2 + 2 * twos:2].set(taker + passed)
    return sizes[jax.random.permutation(jax.random.fold_in(key, 2), amount)]


def setup_inputs(seed: int = 0) -> dict:
    key_list = jax.random.split(jax.random.key(seed), 8)
    return {
        "hidden": draw_hidden(jax.random.fold_in(key_list[7], 71), 0),
        "gain": jnp.clip(1.0 + 0.1 * jax.random.normal(key_list[1], (EXITS, D), jnp.float32), 0.5, 1.5),
        "exit_scale": jnp.clip(jnp.exp(jax.random.uniform(key_list[2], (EXITS,), jnp.float32, math.log(0.25), math.log(2.0))), 0.25, 2.0),
        "head_weight": draw_head_weight(jax.random.fold_in(key_list[7], 71), 0),
        "targets": set_ends(skewed_ids(key_list[4], (ROWS_PAD,), VOCAB, 2), jax.random.fold_in(key_list[4], 3), 0, VOCAB - 1).astype(jnp.int32),
        "exit_ids": set_ends(jax.random.randint(key_list[5], (ROWS_PAD,), 0, EXITS), jax.random.fold_in(key_list[5], 1), 0, EXITS - 1).astype(jnp.int32),
        "counts": ragged(key_list[6], N_SECTION, TOTAL, CAP, 2).astype(jnp.int32),
    }


def reference(hidden, gain, exit_scale, head_weight, targets, exit_ids, counts):
    xf = hidden.astype(jnp.float32)
    rinv = lax.rsqrt(lax.optimization_barrier(jnp.mean(xf * xf, axis=1)) + 1e-05)
    g_rows = gain[exit_ids]
    normed = (xf * rinv[:, None] * g_rows).astype(jnp.bfloat16)
    slots = jnp.arange(ROWS_PAD, dtype=jnp.int32)
    valid = slots % CAP < counts[slots // CAP]
    row_weight = jnp.where(valid, exit_scale[exit_ids], jnp.float32(0.0))
    logits = jnp.dot(normed, head_weight, preferred_element_type=jnp.float32)
    peak = lax.optimization_barrier(jnp.max(logits, axis=1))
    total = lax.optimization_barrier(jnp.sum(jnp.exp(logits - peak[:, None]), axis=1))
    lse = peak + jnp.log(total)
    chosen = jnp.take_along_axis(logits, targets[:, None].astype(jnp.int32), axis=1)[:, 0]
    loss = jnp.sum(row_weight * (lse - chosen)) / TOTAL
    hit = (jnp.arange(VOCAB, dtype=jnp.int32)[None, :] == targets[:, None]).astype(jnp.float32)
    dlogits = (row_weight[:, None] * (jnp.exp(logits - lse[:, None]) - hit)).astype(jnp.bfloat16)
    grad_weight = jnp.dot(normed.T, dlogits, preferred_element_type=jnp.float32).astype(jnp.bfloat16)
    dnormed = jnp.dot(dlogits, head_weight.T, preferred_element_type=jnp.float32)
    unit = xf * rinv[:, None]
    scaled = g_rows * dnormed
    inner = lax.optimization_barrier(jnp.sum(scaled * unit, axis=1)) / D
    grad_hidden = (rinv[:, None] * (scaled - unit * inner[:, None])).astype(jnp.bfloat16)
    return (loss, grad_weight, grad_hidden)
```

```python
import jax
import jax.numpy as jnp
from jax import lax
from jax.experimental import pallas as pl
from jax.experimental.pallas import tpu as pltpu
from jax.sharding import PartitionSpec as P

MESH = pl.DeviceIdType.MESH
NX, NZ, NY = 4, 8, 4
CAP = 80
D = 8192
VW = 256
ROWS = NX * CAP
EXITS = 4
F32 = jnp.float32
BF16 = jnp.bfloat16
ZW, YW = 384, 768
XB0, XA0 = NZ * ZW + NY * YW, NZ * ZW + NY * YW + 512
ZORD = (4, 3, 5, 2, 6, 1, 7, 0)
ZPOS = {d: k for k, d in enumerate(ZORD)}
N_SEM = 176


def kernel(
    hidden, gain, head, meta, counts, scale, loss_out, gw_out, gh_out,
    n_all, w_all, logit, dl, s1, s2, st, loss_x, px, pz, py,
    rx1a, rx1b, rx2a, rx2b, rz1a, rz1b, rz2a, rz2b, ry1a, ry1b, ry2a, ry2b,
    qx1, qx2, qz1, qz2, qy1, qy2, tx, tz, ty, dn, gs, gr, cols_f, ssem, rsem, lsem,
):
    s = lax.axis_index("section")
    v = lax.axis_index("vocab")
    x, c = lax.div(s, 2), lax.rem(s, 2)
    z, y = lax.div(v, NY), lax.rem(v, NY)

    def dev(dx=0, dc=0, dz=0, dy=0):
        return (
            lax.rem(x + dx + NX, NX) * 2 + lax.rem(c + dc, 2),
            lax.rem(z + dz + NZ, NZ) * NY + lax.rem(y + dy + NY, NY),
        )

    used = [0]
    started = []

    def send(src, dst, device):
        i = used[0]
        used[0] += 1
        cp = pltpu.make_async_remote_copy(
            src_ref=src, dst_ref=dst, send_sem=ssem.at[i], recv_sem=rsem.at[i],
            device_id=device, device_id_type=MESH,
        )
        cp.start()
        started.append(cp)
        return cp

    barrier = pltpu.get_barrier_semaphore()
    friends = [dict(dc=1)]
    friends += [dict(dz=i) for i in range(1, NZ)]
    friends += [dict(dx=i, dy=j) for i in range(NX) for j in range(NY) if i or j]
    for f in friends:
        pl.semaphore_signal(barrier, inc=1, device_id=dev(**f), device_id_type=MESH)
    own_w = pltpu.make_async_copy(head, w_all.at[c], lsem.at[0])
    own_w.start()

    diag = lax.broadcasted_iota(jnp.int32, (CAP, 128), 0) == lax.broadcasted_iota(
        jnp.int32, (CAP, 128), 1
    )
    lane = lax.broadcasted_iota(jnp.int32, (1, 128), 1)
    sub8 = lax.broadcasted_iota(jnp.int32, (8, 128), 0)

    def to_col(row):
        return jnp.sum(jnp.where(diag, jnp.broadcast_to(row, (CAP, 128)), 0.0), axis=1, keepdims=True)

    def to_row(col):
        return jnp.sum(jnp.where(diag, jnp.broadcast_to(col, (CAP, 128)), 0.0), axis=0, keepdims=True)

    own_exit = to_col(meta[1, pl.ds(s, 1), :].astype(F32))

    def gain_rows(cols, e):
        g = jnp.broadcast_to(gain[0:1, cols], (CAP, cols.size))
        for i in range(1, EXITS):
            g = jnp.where(e == float(i), gain[i : i + 1, cols], g)
        return g

    def squares(i, acc):
        xs = hidden[:, pl.ds(pl.multiple_of(i * 512, 512), 512)].astype(F32)
        xs = xs * xs
        for j in range(4):
            acc = acc + xs[:, j * 128 : (j + 1) * 128]
        return acc

    total = lax.fori_loop(0, D // 512, squares, jnp.zeros((CAP, 128), F32))
    rinv = lax.rsqrt(jnp.sum(total, axis=1, keepdims=True) / D + 1e-05)

    def norm_chunk(i, carry):
        cols = pl.ds(pl.multiple_of(i * 512, 512), 512)
        xs = hidden[:, cols].astype(F32)
        n_all[0, :, cols] = (xs * rinv * gain_rows(cols, own_exit)).astype(BF16)
        return carry

    lax.fori_loop(0, D // 512, norm_chunk, 0)

    pl.semaphore_wait(barrier, len(friends))

    def zc(d):
        return pl.ds(pl.multiple_of(lax.rem(z + d + NZ, NZ) * ZW, ZW), ZW)

    def yc(d):
        return pl.ds(pl.multiple_of(NZ * ZW + lax.rem(y + d + NY, NY) * YW, YW), YW)

    xb, xa = pl.ds(XB0, 512), pl.ds(XA0, D - XA0)
    low, high, full = pl.ds(0, 48), pl.ds(48, 32), pl.ds(0, CAP)
    events = []
    cps = {}

    def at(time, fn):
        events.append((time, len(events), fn))

    def run():
        for _, _, fn in sorted(events, key=lambda e: (e[0], e[1])):
            fn()
        events.clear()

    def own_x(tag, cols):
        cps[tag + "+"] = send(n_all.at[0, :, cols], n_all.at[3, :, cols], dev(dx=1))
        cps[tag + "-"] = send(n_all.at[0, :, cols], n_all.at[1, :, cols], dev(dx=-1))

    def forward_x(tag, cols, right):
        if right:
            cps[tag + "2"] = send(n_all.at[3, :, cols], n_all.at[2, :, cols], dev(dx=1))
        else:
            cps[tag + "2"] = send(n_all.at[1, :, cols], n_all.at[2, :, cols], dev(dx=-1))

    def chain(tag, n, cols, axis, rel, t0, step):
        half = n // 2

        def begin():
            for sign in (1, -1):
                ref = n_all.at[rel, :, cols(0)]
                cps[tag, sign, 1] = send(ref, ref, dev(**{axis: sign}))

        def arrive(sign, k):
            cps[tag, sign, k].wait_recv()
            if k < half:
                rows = full if k < half - 1 else (low if sign == 1 else high)
                ref = n_all.at[rel, rows, cols(-sign * k)]
                cps[tag, sign, k + 1] = send(ref, ref, dev(**{axis: sign}))

        for k in range(1, half + 1):
            for sign in (1, -1):
                at(t0 + step * k, lambda sign=sign, k=k: arrive(sign, k))
        return begin

    own_x("z", zc(0))
    own_x("y", yc(0))
    z1 = chain("z1", NZ, zc, "dz", 1, 3.0, 4.0)
    z3 = chain("z3", NZ, zc, "dz", 3, 3.5, 4.0)
    z2 = chain("z2", NZ, zc, "dz", 2, 5.5, 4.0)
    y1 = chain("y1", NY, yc, "dy", 1, 5.0, 5.2)
    y3 = chain("y3", NY, yc, "dy", 3, 5.5, 5.2)
    y2 = chain("y2", NY, yc, "dy", 2, 8.0, 5.2)

    def got(tag, sign, then):
        def fn():
            cps[tag + sign].wait_recv()
            then()
        return fn

    def ready_z1():
        z1()
        forward_x("z", zc(0), False)
        own_x("a", xa)
        own_x("b", xb)

    def ready_y1():
        y1()
        forward_x("y", yc(0), False)

    at(3.0, got("z", "-", ready_z1))
    at(3.1, got("z", "+", z3))
    at(5.0, got("y", "-", ready_y1))
    at(5.1, got("y", "+", y3))
    at(5.5, got("z", "2", z2))
    at(8.0, got("y", "2", y2))
    at(11.0, got("b", "-", lambda: forward_x("b", xb, False)))
    at(11.1, got("b", "+", lambda: None))
    at(12.0, got("a", "+", lambda: forward_x("a", xa, True)))
    at(12.1, got("a", "-", lambda: None))
    at(16.0, got("b", "2", lambda: None))
    at(18.0, got("a", "2", lambda: None))

    def swap_w():
        own_w.wait()
        cps["w"] = send(w_all.at[c], w_all.at[c], dev(dc=1))

    at(3.2, swap_w)
    run()
    cps["w"].wait_recv()

    def logit_chunk(i, carry):
        k = pl.multiple_of(i * 512, 512)
        n = n_all[:, :, pl.ds(k, 512)].reshape(ROWS, 512)
        for h in range(2):
            part = jnp.dot(n, w_all[h, pl.ds(k, 512), :], preferred_element_type=F32)
            logit[h] += part
        return carry

    logit[...] = jnp.zeros_like(logit)
    lax.fori_loop(0, D // 512, logit_chunk, 0)

    def section_of(rel):
        return lax.rem(x + rel, NX) * 2 + c

    def first_entry(h):
        return (((x * 2 + h) * NZ * NY + v) * VW).astype(F32)

    entry = lax.broadcasted_iota(jnp.int32, (CAP, VW), 1).astype(F32)

    def hits(rel, h):
        target = to_col(meta[0, pl.ds(section_of(rel), 1), :].astype(F32))
        return entry == target - first_entry(h)

    stats = [jnp.zeros((8, 128), F32)] * 4
    for rel in range(NX):
        rows = pl.ds(rel * CAP, CAP)
        part = [logit[h, rows, :] for h in range(2)]
        m = jnp.maximum(*[jnp.max(l, axis=1, keepdims=True) for l in part])
        e = [jnp.exp(l - m) for l in part]
        values = (
            m,
            sum(jnp.sum(p, axis=1, keepdims=True) for p in e),
            sum(jnp.sum(p * l, axis=1, keepdims=True) for p, l in zip(e, part)),
            sum(
                jnp.sum(jnp.where(hits(rel, h), l, 0.0), axis=1, keepdims=True)
                for h, l in enumerate(part)
            ),
        )
        here = sub8 == lax.rem(x + rel, NX)
        for i in range(4):
            stats[i] = jnp.where(here, jnp.broadcast_to(to_row(values[i]), (8, 128)), stats[i])

    def merge(parts):
        peak = parts[0][0]
        for p in parts[1:]:
            peak = jnp.maximum(peak, p[0])
        f = [jnp.exp(p[0] - peak) for p in parts]
        return (
            peak,
            sum(p[1] * g for p, g in zip(parts, f)),
            sum(p[2] * g for p, g in zip(parts, f)),
            sum(p[3] for p in parts),
        )

    for i in range(4):
        s1[z, i] = stats[i]
    swaps = [send(s1.at[z], s1.at[z], dev(dz=i)) for i in range(1, NZ)]
    for cp in swaps:
        cp.wait_recv()
    stats = merge([[s1[q, i] for i in range(4)] for q in range(NZ)])
    own = x * NY + y
    for i in range(4):
        s2[own, i] = stats[i]
    swaps = [
        send(s2.at[own], s2.at[own], dev(dx=i, dy=j))
        for i in range(NX) for j in range(NY) if i or j
    ]
    for cp in swaps:
        cp.wait_recv()
    peak, total, mean, chosen = merge([[s2[q, i] for i in range(4)] for q in range(NX * NY)])
    lse = peak + jnp.log(total)

    weight = jnp.zeros((8, 128), F32)
    for q in range(NX):
        sec = q * 2 + c
        ids = meta[1, pl.ds(sec, 1), :]
        w_row = jnp.zeros((1, 128), F32)
        for i in range(EXITS):
            w_row = jnp.where(ids == i, scale[i], w_row)
        w_row = jnp.where(lane < counts[sec], w_row, 0.0)
        weight = jnp.where(sub8 == q, jnp.broadcast_to(w_row, (8, 128)), weight)
    live = weight != 0.0
    st[0] = lse
    st[1] = weight
    st[2] = jnp.where(live, weight * (mean / total - chosen), 0.0)
    loss_rows = jnp.where(live, weight * (lse - chosen), 0.0)
    own_loss = jnp.sum(jnp.sum(loss_rows, axis=1, keepdims=True), axis=0, keepdims=True)
    loss_x[0] = jnp.broadcast_to(own_loss, (8, 128))
    loss_swap = send(loss_x.at[0], loss_x.at[1], dev(dc=1))

    for rel in range(NX):
        rows = pl.ds(rel * CAP, CAP)
        at_row = pl.ds(lax.rem(x + rel, NX), 1)
        lse_c, w_c = to_col(st[0, at_row, :]), to_col(st[1, at_row, :])
        for h in range(2):
            hit = jnp.where(hits(rel, h), 1.0, 0.0)
            dl[h, rows, :] = (w_c * (jnp.exp(logit[h, rows, :] - lse_c) - hit)).astype(BF16)

    nt = (((1,), (1,)), ((), ()))

    def grad_block(k):
        zz = lax.rem(z + ZORD[k], NZ)

        def one(ry, carry):
            at_f = pl.ds(pl.multiple_of((zz * NY + lax.rem(y + ry, NY)) * VW, VW), VW)
            out = lax.dot_general(dl[0], w_all[0, at_f, :], nt, preferred_element_type=F32)
            out += lax.dot_general(dl[1], w_all[1, at_f, :], nt, preferred_element_type=F32)
            out = out.astype(BF16)
            for rx in range(NX):
                px[rx, k, ry] = out[rx * CAP : rx * CAP + 32]
                pz[k, rx, ry] = out[rx * CAP + 32 : rx * CAP + 64]
                py[ry, rx, k] = out[rx * CAP + 64 : rx * CAP + 80]
            return carry

        lax.fori_loop(0, NY, one, 0)

    def add_into(dst, srcs):
        def one(i, carry):
            acc = dst[i].astype(F32)
            for r in srcs:
                acc = acc + r[i].astype(F32)
            dst[i] = acc.astype(BF16)
            return carry

        lax.fori_loop(0, dst.shape[0], one, 0)

    def ring(tag, n, axis, block, halves, bufs, times, done):
        half = n // 2
        h_a, h_b = halves

        def begin(sign):
            src = h_a(block(half)) if sign == 1 else h_b(block(half))
            cps[tag, sign, 1] = send(src, bufs[sign][0], dev(**{axis: sign}))

        def arrive(sign, k):
            cps[tag, sign, k].wait_recv()
            d = (sign * (half - k)) % n
            if k == 1:
                part = h_a(block(d)) if sign == 1 else h_b(block(d))
                add_into(part, [bufs[sign][0]])
            else:
                add_into(block(d), [bufs[sign][1].at[k - 2]])
            cps[tag, sign, k + 1] = send(block(d), bufs[sign][1].at[k - 1], dev(**{axis: sign}))

        def finish():
            for sign in (1, -1):
                cps[tag, sign, half].wait_recv()
            add_into(block(0), [bufs[sign][1].at[half - 2] for sign in (1, -1)])
            done()

        for k in range(1, half):
            for sign in (1, -1):
                at(times[k - 1], lambda sign=sign, k=k: arrive(sign, k))
        at(times[half - 1], finish)
        return begin

    def direct(tag, n, axis, block, buf, time, done):
        def begin():
            for d in range(1, n):
                cps[tag, d] = send(block(d), buf.at[d - 1], dev(**{axis: d}))

        def finish():
            for d in range(1, n):
                cps[tag, d].wait_recv()
            acc = block(0)[...].astype(F32)
            for d in range(1, n):
                acc = acc + buf[d - 1].astype(F32)
            done(acc)

        at(time, finish)
        return begin

    def first(m):
        return lambda r: r.at[0:m]

    def last(m):
        return lambda r: r.at[m : 2 * m]

    def put(r0, r1):
        def fn(acc):
            dn[r0:r1] = acc
        return fn

    both = lambda begin: lambda: (begin(1), begin(-1))
    x3 = direct("x3", NZ, "dz", lambda d: px.at[0, ZPOS[d], 0], tx, 28.0, put(0, 32))
    x2 = ring("x2", NY, "dy", lambda d: px.at[0, :, d], (first(4), last(4)),
              {1: (qx1.at[0], rx2a), -1: (qx1.at[1], rx2b)}, (20.0, 22.5), x3)
    x1 = ring("x1", NX, "dx", lambda d: px.at[d], (first(4), last(4)),
              {1: (rx1a, qx2.at[0:1]), -1: (rx1b, qx2.at[1:2])}, (7.0, 17.5), both(x2))
    z3r = direct("w3", NY, "dy", lambda d: pz.at[7, 0, d], tz, 28.1, put(32, 64))
    z2r = ring("w2", NX, "dx", lambda d: pz.at[7, d], (first(2), last(2)),
               {1: (qz1.at[0], rz2a), -1: (qz1.at[1], rz2b)}, (22.0, 24.5), z3r)
    z1r = ring("w1", NZ, "dz", lambda d: pz.at[ZPOS[d]], (first(2), last(2)),
               {1: (rz1a, qz2.at[0]), -1: (rz1b, qz2.at[1])}, (3.5, 9.0, 14.5, 20.0), both(z2r))
    y3r = direct("v3", NX, "dx", lambda d: py.at[0, d, 7], ty, 24.0, put(64, 80))
    y2r = ring("v2", NZ, "dz", lambda d: py.at[0, :, ZPOS[d]], (first(2), last(2)),
               {1: (qy1.at[0], ry2a), -1: (qy1.at[1], ry2b)}, (12.5, 14.6, 16.5, 18.5), y3r)
    y1r = ring("v1", NY, "dy", lambda d: py.at[d], (first(2), last(2)),
               {1: (ry1a, qy2.at[0:1]), -1: (ry1b, qy2.at[1:2])}, (5.0, 10.5), both(y2r))

    tn = (((0,), (0,)), ((), ()))

    def head_rows(j, h, store):
        def one(i, carry):
            f = pl.ds(pl.multiple_of(j * 1024 + i * VW, VW), VW)
            n = n_all[:, :, f].reshape(ROWS, VW)
            store(f, lax.dot_general(n, dl[h], tn, preferred_element_type=F32))
            return carry

        lax.fori_loop(0, 4, one, 0)

    def partner_chunk(j):
        def store(f, value):
            gs[f, :] = value.astype(BF16)

        head_rows(j, 1 - c, store)
        f = pl.ds(j * 1024, 1024)
        cps["g", j] = send(gs.at[f], gr.at[f], dev(dc=1))

    outs = []

    def own_chunk(j):
        cps["g", j].wait_recv()

        def store(f, value):
            gr[f, :] = (value + gr[f, :].astype(F32)).astype(BF16)

        head_rows(j, c, store)
        f = pl.ds(j * 1024, 1024)
        cp = pltpu.make_async_copy(gr.at[f], gw_out.at[f], lsem.at[1 + j])
        cp.start()
        outs.append(cp)

    for j in range(8):
        at(4.0 + j * 1.0, lambda j=j: partner_chunk(j))
        at(12.1 + j * 1.0, lambda j=j: own_chunk(j))

    grad_block(0)
    z1r(1)
    z1r(-1)
    for k in range(1, 4):
        grad_block(k)
    x1(1)
    for k in range(4, 8):
        grad_block(k)
    x1(-1)
    y1r(1)
    y1r(-1)
    run()

    f = pl.ds(pl.multiple_of(v * VW, VW), VW)
    inner = to_col(st[2, pl.ds(x, 1), :])
    unit = hidden[:, f].astype(F32) * rinv
    scaled = gain_rows(f, own_exit) * dn[...]
    gh_out[...] = (rinv * (scaled - unit * (inner / D))).astype(BF16)

    loss_swap.wait_recv()
    loss_out[...] = (loss_x[0, 0:1, 0:1] + loss_x[1, 0:1, 0:1]) / 512.0
    for cp in outs:
        cp.wait()
    for cp in started:
        cp.wait_send()


def body(hidden, gain, exit_scale, head_weight, targets, exit_ids, counts):
    meta = jnp.stack([targets, exit_ids]).reshape(2, 2 * NX, CAP)
    meta = jnp.pad(meta, ((0, 0), (0, 0), (0, 128 - CAP)))
    vmem = pl.BlockSpec(memory_space=pltpu.VMEM)
    smem = pl.BlockSpec(memory_space=pltpu.SMEM)
    hbm = pl.BlockSpec(memory_space=pl.ANY)
    b = lambda *shape: pltpu.VMEM(shape, BF16)
    f = lambda *shape: pltpu.VMEM(shape, F32)
    scratch = [
        b(NX, CAP, D), b(2, D, VW), f(2, ROWS, VW), b(2, ROWS, VW),
        f(NZ, 4, 8, 128), f(NX * NY, 4, 8, 128), f(3, 8, 128), f(2, 8, 128),
        b(NX, NZ, NY, 32, VW), b(NZ, NX, NY, 32, VW), b(NY, NX, NZ, 16, VW),
        b(4, NY, 32, VW), b(4, NY, 32, VW), b(1, NZ, 32, VW), b(1, NZ, 32, VW),
        b(2, NY, 32, VW), b(2, NY, 32, VW), b(1, NY, 32, VW), b(1, NY, 32, VW),
        b(2, NZ, 16, VW), b(2, NZ, 16, VW), b(3, NX, 16, VW), b(3, NX, 16, VW),
        b(2, 4, 32, VW), b(2, NZ, NY, 32, VW),
        b(2, 2, 32, VW), b(2, 3, NX, NY, 32, VW),
        b(2, 2, 16, VW), b(2, NX, NZ, 16, VW),
        b(NZ - 1, 32, VW), b(NY - 1, 32, VW), b(NX - 1, 16, VW),
        f(CAP, VW), b(D, VW), b(D, VW), f(8, 128),
        pltpu.SemaphoreType.DMA((N_SEM,)), pltpu.SemaphoreType.DMA((N_SEM,)),
        pltpu.SemaphoreType.DMA((9,)),
    ]
    loss, grad_weight, grad_hidden = pl.pallas_call(
        kernel,
        out_shape=(
            jax.ShapeDtypeStruct((1, 1), F32),
            jax.ShapeDtypeStruct((D, VW), BF16),
            jax.ShapeDtypeStruct((CAP, VW), BF16),
        ),
        in_specs=[vmem, vmem, hbm, vmem, smem, smem],
        out_specs=(vmem, hbm, vmem),
        scratch_shapes=scratch,
        compiler_params=pltpu.CompilerParams(
            collective_id=0, has_side_effects=True, vmem_limit_bytes=58 * 2**20
        ),
        name="exit_head",
    )(hidden, gain, head_weight, meta, counts, exit_scale)
    return (loss[0, 0], grad_weight, grad_hidden)


def solution(mesh):
    in_specs = (P("section", None), P(), P(), P(None, ("section", "vocab")), P(), P(), P())
    out_specs = (P(), P(None, ("section", "vocab")), P("section", "vocab"))
    return jax.shard_map(body, mesh=mesh, in_specs=in_specs, out_specs=out_specs, check_vma=False)
```

```python
import jax
import jax.numpy as jnp
from jax import lax
from jax.experimental import pallas as pl
from jax.experimental.pallas import tpu as pltpu
from jax.sharding import PartitionSpec as P

MESH = pl.DeviceIdType.MESH
NX, NZ, NY = 4, 8, 4
CAP = 80
D = 8192
VW = 256
ROWS = NX * CAP
EXITS = 4
F32 = jnp.float32
BF16 = jnp.bfloat16
ZW, YW = 384, 768
XB0 = NZ * ZW + NY * YW
XBW = 512
XA0 = XB0 + XBW
ZORD = (4, 3, 5, 2, 6, 1, 7, 0)
ZPOS = {d: k for k, d in enumerate(ZORD)}
N_SEM = 320
HALVES = ((0, 48, 32), (48, 32, 16))
PARTS = (((0, 0, 256), (16, 0, 256), (32, 0, 256)), ((48, 0, 256), (64, 0, 128), (64, 128, 128)))
NT = (((1,), (1,)), ((), ()))
TN = (((0,), (0,)), ((), ()))


def scratch():
    out = dict(
        hid=((CAP, D), BF16), gain=((EXITS, D), F32), n_all=((NX, CAP, D), BF16), w_all=((D, 2 * VW), BF16),
        logit=((NX, CAP, 2 * VW), F32), dl=((NX, CAP, 2 * VW), BF16),
        s1=((2, NZ, 4, 8, 128), F32), s2=((2, NX * NY, 4, 8, 128), F32),
        st=((2, 3, 8, 128), F32), ids=((2, 8, 128), F32), loss=((2, 8, 128), F32), dn=((CAP, VW), F32),
        mine=((D, VW), F32), gs=((D, VW), BF16), gr=((D, VW), BF16),
    )
    for h in range(2):
        lx, lz, ly = [p[2] for p in PARTS[h]]
        out[f"px{h}"] = ((NX, NZ, NY, 16, lx), BF16)
        out[f"pz{h}"] = ((NZ, NX, NY, 16, lz), BF16)
        out[f"py{h}"] = ((NY, NX, NZ, 16, ly), BF16)
        out[f"ax{h}"] = ((2, 2, 4, 2, 16, lx), BF16)
        out[f"bx{h}"] = ((2, 2, 1, NZ, 2, 16, lx), BF16)
        out[f"az{h}"] = ((2, 2, 2, 2, 16, lz), BF16)
        out[f"bz{h}"] = ((2, 2, 3, NX, 2, 16, lz), BF16)
        out[f"ay{h}"] = ((2, 2, 2, 4, 16, ly), BF16)
        out[f"by{h}"] = ((2, 2, 1, NX, 4, 16, ly), BF16)
        out[f"cx{h}"] = ((NY - 1, NZ, 16, lx), BF16)
        out[f"cz{h}"] = ((NX - 1, NY, 16, lz), BF16)
        out[f"cy{h}"] = ((NX - 1, NZ, 16, ly), BF16)
        out[f"ex{h}"] = ((NZ - 1, 16, lx), BF16)
        out[f"ez{h}"] = ((NY - 1, 16, lz), BF16)
        out[f"ey{h}"] = ((NZ - 1, 16, ly), BF16)
    return out


SCRATCH = scratch()


def kernel(hidden, gain_in, head, targets, exit_ids, counts, scale, loss_out, gw_out, gh_out, *refs):
    b = dict(zip(SCRATCH, refs))
    ssem, rsem, lsem = refs[len(SCRATCH) :]
    hid, gain, n_all, w_all = b["hid"], b["gain"], b["n_all"], b["w_all"]
    logit, dl, s1, s2, st, ids = b["logit"], b["dl"], b["s1"], b["s2"], b["st"], b["ids"]
    dn, mine, gs, gr, loss_x = b["dn"], b["mine"], b["gs"], b["gr"], b["loss"]
    s = lax.axis_index("section")
    v = lax.axis_index("vocab")
    x, c = lax.div(s, 2), lax.rem(s, 2)
    z, y = lax.div(v, NY), lax.rem(v, NY)

    def dev(dx=0, dc=0, dz=0, dy=0):
        return (
            lax.rem(x + dx + NX, NX) * 2 + lax.rem(c + dc, 2),
            lax.rem(z + dz + NZ, NZ) * NY + lax.rem(y + dy + NY, NY),
        )

    used = [0]
    started = []
    outs = []
    cps = {}
    events = []

    def send(src, dst, device):
        i = used[0]
        used[0] += 1
        cp = pltpu.make_async_remote_copy(
            src_ref=src, dst_ref=dst, send_sem=ssem.at[i], recv_sem=rsem.at[i],
            device_id=device, device_id_type=MESH,
        )
        cp.start()
        started.append(cp)
        return cp

    def at(time, fn, *args):
        events.append((time, len(events), lambda: fn(*args)))

    def run():
        for _, _, fn in sorted(events, key=lambda e: (e[0], e[1])):
            fn()
        events.clear()

    barrier = pltpu.get_barrier_semaphore()
    friends = [dict(dc=1)]
    friends += [dict(dz=i) for i in range(1, NZ)]
    friends += [dict(dx=i, dy=j) for i in range(NX) for j in range(NY) if i or j]
    for f in friends:
        pl.semaphore_signal(barrier, inc=1, device_id=dev(**f), device_id_type=MESH)
    own_w = pl.ds(pl.multiple_of(c * VW, VW), VW)
    loads = [
        pltpu.make_async_copy(hidden, hid, lsem.at[0]),
        pltpu.make_async_copy(gain_in, gain, lsem.at[1]),
        pltpu.make_async_copy(head, w_all.at[:, own_w], lsem.at[2]),
    ]
    for cp in loads:
        cp.start()

    diag = lax.broadcasted_iota(jnp.int32, (CAP, 128), 0) == lax.broadcasted_iota(
        jnp.int32, (CAP, 128), 1
    )
    lane = lax.broadcasted_iota(jnp.int32, (8, 128), 1)
    sub8 = lax.broadcasted_iota(jnp.int32, (8, 128), 0)
    flat = sub8 * 128 + lane

    def to_col(row):
        return jnp.sum(jnp.where(diag, jnp.broadcast_to(row, (CAP, 128)), 0.0), axis=1, keepdims=True)

    def to_row(col, r0):
        n = col.shape[0]
        return jnp.sum(
            jnp.where(diag[r0 : r0 + n], jnp.broadcast_to(col, (n, 128)), 0.0), axis=0, keepdims=True
        )

    def spread(slot, ref):
        def one(r, acc):
            for q in range(NX):
                acc = jnp.where(flat == q * 128 + r, ref[(q * 2 + c) * CAP + r], acc)
            return acc

        acc = lax.fori_loop(0, CAP, one, jnp.zeros((8, 128), jnp.int32), unroll=4)
        ids[slot] = acc.astype(F32)

    spread(0, exit_ids)
    own_exit = to_col(ids[0, pl.ds(x, 1), :])

    def gain_rows(cols, e):
        g = jnp.broadcast_to(gain[0:1, cols], (CAP, cols.size))
        for i in range(1, EXITS):
            g = jnp.where(e == float(i), gain[i : i + 1, cols], g)
        return g

    def squares(i, acc):
        xs = hid[:, pl.ds(pl.multiple_of(i * 512, 512), 512)].astype(F32)
        xs = xs * xs
        for j in range(4):
            acc = acc + xs[:, j * 128 : (j + 1) * 128]
        return acc

    loads[0].wait()
    total_sq = lax.fori_loop(0, D // 512, squares, jnp.zeros((CAP, 128), F32))
    rinv = lax.rsqrt(jnp.sum(total_sq, axis=1, keepdims=True) / D + 1e-05)

    def norm_chunk(i, carry):
        cols = pl.ds(pl.multiple_of(i * 512, 512), 512)
        xs = hid[:, cols].astype(F32)
        n_all[0, :, cols] = (xs * rinv * gain_rows(cols, own_exit)).astype(BF16)
        return carry

    loads[1].wait()
    lax.fori_loop(0, D // 512, norm_chunk, 0)
    pl.semaphore_wait(barrier, len(friends))

    def zc(d):
        return pl.ds(pl.multiple_of(lax.rem(z + d + NZ, NZ) * ZW, ZW), ZW)

    def yc(d):
        return pl.ds(pl.multiple_of(NZ * ZW + lax.rem(y + d + NY, NY) * YW, YW), YW)

    xb, xa = pl.ds(XB0, XBW), pl.ds(XA0, D - XA0)

    def own_x(tag, h, cols):
        rows = pl.ds(*HALVES[h][:2])
        cps[tag, h, 1] = send(n_all.at[0, rows, cols], n_all.at[3, rows, cols], dev(dx=1))
        cps[tag, h, -1] = send(n_all.at[0, rows, cols], n_all.at[1, rows, cols], dev(dx=-1))

    def forward_x(tag, h, cols, right):
        rows = pl.ds(*HALVES[h][:2])
        rel, dx = (3, 1) if right else (1, -1)
        cps[tag, h, 2] = send(n_all.at[rel, rows, cols], n_all.at[2, rows, cols], dev(dx=dx))

    def chain(tag, h, n, cols, axis, rel, t0, step):
        half = n // 2
        r0, n_rows, n_low = HALVES[h]
        full, low, high = pl.ds(r0, n_rows), pl.ds(r0, n_low), pl.ds(r0 + n_low, n_rows - n_low)

        def begin():
            for sign in (1, -1):
                ref = n_all.at[rel, full, cols(0)]
                cps[tag, h, rel, sign, 1] = send(ref, ref, dev(**{axis: sign}))

        def arrive(sign, k):
            cps[tag, h, rel, sign, k].wait_recv()
            if k < half:
                rows = full if k < half - 1 else (low if sign == 1 else high)
                ref = n_all.at[rel, rows, cols(-sign * k)]
                cps[tag, h, rel, sign, k + 1] = send(ref, ref, dev(**{axis: sign}))

        for k in range(1, half + 1):
            for sign in (1, -1):
                at(t0 + step * k, arrive, sign, k)
        return begin

    def gather(h, tz, ty, tb, ta, dz, dy, fwd, zstep, ystep, more):
        z1 = chain("cz", h, NZ, zc, "dz", 1, tz, zstep)
        z3 = chain("cz", h, NZ, zc, "dz", 3, tz + 0.1, zstep)
        z2 = chain("cz", h, NZ, zc, "dz", 2, tz + dz, zstep)
        y1 = chain("cy", h, NY, yc, "dy", 1, ty, ystep)
        y3 = chain("cy", h, NY, yc, "dy", 3, ty + 0.1, ystep)
        y2 = chain("cy", h, NY, yc, "dy", 2, ty + dy, ystep)

        def got(tag, sign, *then):
            cps[tag, h, sign].wait_recv()
            for fn in then:
                fn()

        at(tz, got, "z", -1, z1, lambda: forward_x("z", h, zc(0), False))
        at(tz, got, "z", 1, z3, *more)
        at(tz + dz, got, "z", 2, z2)
        at(ty, got, "y", -1, y1, lambda: forward_x("y", h, yc(0), False))
        at(ty, got, "y", 1, y3)
        at(ty + dy, got, "y", 2, y2)
        at(tb, got, "b", -1, lambda: forward_x("b", h, xb, False))
        at(tb, got, "b", 1)
        at(ta, got, "a", 1, lambda: forward_x("a", h, xa, True))
        at(ta, got, "a", -1)
        at(tb + fwd, got, "b", 2)
        at(ta + fwd, got, "a", 2)
        return max(e[0] for e in events) + 0.01

    def own_group(h):
        own_x("b", h, xb)
        own_x("a", h, xa)

    for h in range(2):
        own_x("z", h, zc(0))
        own_x("y", h, yc(0))

    here0 = gather(0, 3.0, 4.5, 7.0, 9.0, 1.6, 2.2, 4.0, 3.0, 4.0, (lambda: own_group(0),))
    here1 = gather(1, 4.6, 6.5, 12.0, 14.0, 1.6, 2.2, 4.0, 3.6, 4.6, (lambda: own_group(1),))

    def swap_w():
        loads[2].wait()
        cps["w"] = send(w_all.at[:, own_w], w_all.at[:, own_w], dev(dc=1))

    at(3.2, swap_w)
    at(3.3, spread, 1, targets)

    def weights():
        weight = jnp.zeros((8, 128), F32)
        exits = ids[0]
        for i in range(EXITS):
            weight = jnp.where(exits == float(i), scale[i], weight)
        for q in range(NX):
            weight = jnp.where((sub8 == q) & (lane >= counts[q * 2 + c]), 0.0, weight)
        for h in range(2):
            r0, n_rows, _ = HALVES[h]
            st[h, 1] = jnp.where((sub8 < NX) & (lane >= r0) & (lane < r0 + n_rows), weight, 0.0)

    at(3.4, weights)

    def logits(h, first, last):
        r0, n_rows, _ = HALVES[h]

        def one(i, carry):
            k = pl.ds(pl.multiple_of(i * 2048, 2048), 2048)
            n = n_all[:, r0 : r0 + n_rows, k].reshape(NX * n_rows, 2048)
            part = jnp.dot(n, w_all[k, :], preferred_element_type=F32)
            logit[:, r0 : r0 + n_rows, :] += part.reshape(NX, n_rows, 2 * VW)
            return carry

        lax.fori_loop(first, last, one, 0)

    def clear():
        logit[...] = jnp.zeros_like(logit)
        cps["w"].wait_recv()

    entry = lax.broadcasted_iota(jnp.int32, (CAP, 2 * VW), 1)
    base = (x * 2 * NZ * NY + v) * VW
    entry = jnp.where(entry < VW, entry + base, entry + (base + (NZ * NY - 1) * VW)).astype(F32)

    def column(ref, rel, r0, n):
        return to_col(ref[pl.ds(lax.rem(x + rel, NX), 1), :])[r0 : r0 + n]

    def local_stats(h):
        r0, n, _ = HALVES[h]
        stats = [jnp.zeros((8, 128), F32)] * 4
        for rel in range(NX):
            l = logit[rel, r0 : r0 + n, :]
            hit = entry[:n] == column(ids.at[1], rel, r0, n)
            m = jnp.max(l, axis=1, keepdims=True)
            e = jnp.exp(l - m)
            values = (
                m,
                jnp.sum(e, axis=1, keepdims=True),
                jnp.sum(e * l, axis=1, keepdims=True),
                jnp.sum(jnp.where(hit, l, 0.0), axis=1, keepdims=True),
            )
            here = sub8 == lax.rem(x + rel, NX)
            for i in range(4):
                row = jnp.broadcast_to(to_row(values[i], r0), (8, 128))
                stats[i] = jnp.where(here, row, stats[i])
        for i in range(4):
            s1[h, z, i] = stats[i]
        cps["s1", h] = [send(s1.at[h, z], s1.at[h, z], dev(dz=i)) for i in range(1, NZ)]

    def merge(parts):
        peak = parts[0][0]
        for p in parts[1:]:
            peak = jnp.maximum(peak, p[0])
        f = [jnp.exp(p[0] - peak) for p in parts]
        return (
            peak,
            sum(p[1] * g for p, g in zip(parts, f)),
            sum(p[2] * g for p, g in zip(parts, f)),
            sum(p[3] for p in parts),
        )

    own = x * NY + y

    def stats_z(h):
        for cp in cps["s1", h]:
            cp.wait_recv()
        stats = merge([[s1[h, q, i] for i in range(4)] for q in range(NZ)])
        for i in range(4):
            s2[h, own, i] = stats[i]
        cps["s2", h] = [
            send(s2.at[h, own], s2.at[h, own], dev(dx=i, dy=j))
            for i in range(NX) for j in range(NY) if i or j
        ]

    losses = []

    def stats_xy(h):
        for cp in cps["s2", h]:
            cp.wait_recv()
        peak, total, mean, chosen = merge([[s2[h, q, i] for i in range(4)] for q in range(NX * NY)])
        lse = peak + jnp.log(total)
        weight = st[h, 1]
        live = weight != 0.0
        st[h, 0] = lse
        st[h, 2] = jnp.where(live, weight * (mean / total - chosen), 0.0)
        losses.append(jnp.where(live, weight * (lse - chosen), 0.0))
        if h == 1:
            own_loss = losses[0] + losses[1]
            own_loss = jnp.sum(jnp.sum(own_loss, axis=1, keepdims=True), axis=0, keepdims=True)
            loss_x[0] = jnp.broadcast_to(own_loss, (8, 128))
            cps["loss"] = send(loss_x.at[0], loss_x.at[1], dev(dc=1))
        r0, n, _ = HALVES[h]
        for rel in range(NX):
            lse_c, w_c = column(st.at[h, 0], rel, r0, n), column(st.at[h, 1], rel, r0, n)
            hit = jnp.where(entry[:n] == column(ids.at[1], rel, r0, n), 1.0, 0.0)
            p = jnp.exp(logit[rel, r0 : r0 + n, :] - lse_c)
            dl[rel, r0 : r0 + n, :] = (w_c * (p - hit)).astype(BF16)

    def grad_block(h, k, *then):
        r0, n, _ = HALVES[h]
        zz = lax.rem(z + ZORD[k], NZ)
        rows = dl[:, r0 : r0 + n, :].reshape(NX * n, 2 * VW)
        f = pl.ds(pl.multiple_of(zz * NY * VW, NY * VW), NY * VW)
        out = lax.dot_general(rows, w_all[f, :], NT, preferred_element_type=F32).astype(BF16)
        for yy in range(NY):
            ry = lax.rem(yy - y + NY, NY)
            for rx in range(NX):
                block = out[rx * n : (rx + 1) * n, yy * VW : (yy + 1) * VW]
                cut = [block[p[0] - r0 : p[0] - r0 + 16, p[1] : p[1] + p[2]] for p in PARTS[h]]
                b[f"px{h}"][rx, k, ry] = cut[0]
                b[f"pz{h}"][k, rx, ry] = cut[1]
                b[f"py{h}"][ry, rx, k] = cut[2]
        for fn in then:
            fn()

    def add_into(dst, srcs):
        def one(i, carry):
            acc = dst[i].astype(F32)
            for r in srcs:
                acc = acc + r[i].astype(F32)
            dst[i] = acc.astype(BF16)
            return carry

        lax.fori_loop(0, dst.shape[0], one, 0)

    def ring(tag, h, n, axis, block, one_way, buf_a, buf_b, times, done):
        half = n // 2
        side = {1: 0, -1: 1}
        left = [2]

        def begin(sign):
            for i in range(2):
                src = one_way(block(half, i), sign)
                cps[tag, h, sign, 1, i] = send(src, buf_a.at[side[sign], i], dev(**{axis: sign}))

        def arrive(sign, k, i):
            cps[tag, h, sign, k, i].wait_recv()
            d = (sign * (half - k)) % n
            if k == 1:
                add_into(one_way(block(d, i), sign), [buf_a.at[side[sign], i]])
            else:
                add_into(block(d, i), [buf_b.at[side[sign], i, k - 2]])
            cps[tag, h, sign, k + 1, i] = send(
                block(d, i), buf_b.at[side[sign], i, k - 1], dev(**{axis: sign})
            )

        def finish(i):
            for sign in (1, -1):
                cps[tag, h, sign, half, i].wait_recv()
            add_into(block(0, i), [buf_b.at[side[sign], i, half - 2] for sign in (1, -1)])
            left[0] -= 1
            if left[0] == 0:
                done()

        for k in range(1, half):
            for i in range(2):
                for sign in (1, -1):
                    at(times[k - 1] + i * times[-1], arrive, sign, k, i)
        for i in range(2):
            at(times[half - 1] + i * times[-1], finish, i)
        return begin

    def direct(tag, h, n, axis, block, buf, time, done):
        def begin():
            for d in range(1, n):
                cps[tag, h, d] = send(block(d), buf.at[d - 1], dev(**{axis: d}))

        def finish():
            for d in range(1, n):
                cps[tag, h, d].wait_recv()
            acc = block(0)[...].astype(F32)
            for d in range(1, n):
                acc = acc + buf[d - 1].astype(F32)
            done(acc)

        at(time, finish)
        return begin

    def reduce(h, t):
        px, pz, py = b[f"px{h}"], b[f"pz{h}"], b[f"py{h}"]

        def put(i):
            r, l, w = PARTS[h][i]
            def fn(acc):
                dn[r : r + 16, l : l + w] = acc
            return fn

        def back(ref, begin):
            def fn(acc):
                ref[...] = acc.astype(BF16)
                begin()
            return fn

        def cut(m):
            return lambda r, sign: r.at[0:m] if sign == 1 else r.at[m : 2 * m]

        x3 = direct("x3", h, NZ, "dz", lambda d: px.at[0, ZPOS[d], 0], b[f"ex{h}"], t["x3"], put(0))
        x2 = direct("x2", h, NY, "dy", lambda d: px.at[0, :, d], b[f"cx{h}"], t["x2"],
                    back(px.at[0, :, 0], x3))
        x1 = ring("x1", h, NX, "dx", lambda d, i: px.at[d, :, 2 * i : 2 * i + 2], cut(4),
                  b[f"ax{h}"], b[f"bx{h}"], t["x1"], x2)
        z3 = direct("z3", h, NY, "dy", lambda d: pz.at[7, 0, d], b[f"ez{h}"], t["z3"], put(1))
        z2 = direct("z2", h, NX, "dx", lambda d: pz.at[7, d], b[f"cz{h}"], t["z2"],
                    back(pz.at[7, 0], z3))
        z1 = ring("z1", h, NZ, "dz", lambda d, i: pz.at[ZPOS[d], :, 2 * i : 2 * i + 2], cut(2),
                  b[f"az{h}"], b[f"bz{h}"], t["z1"], z2)
        y3 = direct("y3", h, NZ, "dz", lambda d: py.at[0, 0, ZPOS[d]], b[f"ey{h}"], t["y3"], put(2))
        y2 = direct("y2", h, NX, "dx", lambda d: py.at[0, d], b[f"cy{h}"], t["y2"],
                    back(py.at[0, 0], y3))
        y1 = ring("y1", h, NY, "dy", lambda d, i: py.at[d, :, 4 * i : 4 * i + 4], cut(2),
                  b[f"ay{h}"], b[f"by{h}"], t["y1"], y2)
        then = {
            0: (lambda: z1(1), lambda: z1(-1)),
            3: (lambda: x1(1),),
            7: (lambda: x1(-1), lambda: y1(1), lambda: y1(-1)),
        }
        for k in range(NZ):
            at(t["g"] + t["gstep"] * k, grad_block, h, k, *then.get(k, ()))

    def head_chunk(j):
        f = pl.ds(j * 1024, 1024)
        n = n_all[:, :, f].reshape(ROWS, 1024)
        both = lax.dot_general(n, dl[...].reshape(ROWS, 2 * VW), TN, preferred_element_type=F32)
        first, second = both[:, :VW], both[:, VW:]
        mine[f, :] = jnp.where(c == 0, first, second)
        gs[f, :] = jnp.where(c == 0, second, first).astype(BF16)
        cps["g", j] = send(gs.at[f], gr.at[f], dev(dc=1))

    def head_sum(j):
        cps["g", j].wait_recv()

        def one(i, carry):
            f = pl.ds(pl.multiple_of(j * 1024 + i * 256, 256), 256)
            gr[f, :] = (mine[f, :] + gr[f, :].astype(F32)).astype(BF16)
            return carry

        lax.fori_loop(0, 4, one, 0)
        f = pl.ds(j * 1024, 1024)
        cp = pltpu.make_async_copy(gr.at[f], gw_out.at[f], lsem.at[3 + j])
        cp.start()
        outs.append(cp)

    at(12.0, clear)
    at(here0, logits, 0, 0, 4)
    at(here0, local_stats, 0)
    at(here1, logits, 1, 0, 4)
    at(here1, local_stats, 1)
    at(24.0, stats_z, 0)
    at(28.0, stats_z, 1)
    at(30.5, stats_xy, 0)
    at(34.4, stats_xy, 1)
    reduce(0, dict(
        g=31.0, gstep=0.5, z1=(34.5, 38.5, 42.5, 46.5, 0.8), x1=(38.7, 44.5, 1.5), y1=(38.8, 44.6, 1.5),
        x2=50.0, z2=50.1, y2=50.2, x3=55.0, z3=55.1, y3=55.2,
    ))
    reduce(1, dict(
        g=36.0, gstep=0.8, z1=(40.0, 44.0, 48.0, 52.0, 0.8), x1=(45.5, 52.5, 1.5), y1=(45.6, 51.6, 1.0),
        x2=57.0, z2=57.1, y2=56.0, x3=62.0, z3=62.1, y3=61.0,
    ))
    for j in range(8):
        at(42.0 + j * 1.2, head_chunk, j)
        at(53.0 + j * 0.5, head_sum, j)
    run()

    f = pl.ds(pl.multiple_of(v * VW, VW), VW)
    inner = to_col(st[0, 2, pl.ds(x, 1), :] + st[1, 2, pl.ds(x, 1), :])
    unit = hid[:, f].astype(F32) * rinv
    scaled = gain_rows(f, own_exit) * dn[...]
    gh_out[...] = (rinv * (scaled - unit * (inner / D))).astype(BF16)

    cps["loss"].wait_recv()
    loss_out[...] = (loss_x[0] + loss_x[1]) / 512.0
    for cp in outs:
        cp.wait()
    for cp in started:
        cp.wait_send()


def handover(loss, grad_weight, grad_hidden, loss_out, gw_out, gh_out, buf, sem):
    n = D // 4
    parts = [pl.ds(i * n, n) for i in range(4)]
    reads = [pltpu.make_async_copy(grad_weight.at[p], buf.at[p], sem.at[i]) for i, p in enumerate(parts)]
    writes = [pltpu.make_async_copy(buf.at[p], gw_out.at[p], sem.at[4 + i]) for i, p in enumerate(parts)]
    for r in reads:
        r.start()
    gh_out[...] = grad_hidden[...]
    loss_out[...] = loss[0:1, 0:1]
    for r, w in zip(reads, writes):
        r.wait()
        w.start()
    for w in writes:
        w.wait()


def body(hidden, gain, exit_scale, head_weight, targets, exit_ids, counts):
    vmem = pl.BlockSpec(memory_space=pltpu.VMEM)
    smem = pl.BlockSpec(memory_space=pltpu.SMEM)
    hbm = pl.BlockSpec(memory_space=pl.ANY)
    dma = pltpu.SemaphoreType.DMA
    big = jax.ShapeDtypeStruct((D, VW), BF16)
    small = jax.ShapeDtypeStruct((CAP, VW), BF16)
    results = pl.pallas_call(
        kernel,
        out_shape=(jax.ShapeDtypeStruct((8, 128), F32), big, small),
        in_specs=[hbm, hbm, hbm, smem, smem, smem, smem],
        out_specs=(vmem, hbm, vmem),
        scratch_shapes=[pltpu.VMEM(*v) for v in SCRATCH.values()] + [dma((N_SEM,)), dma((N_SEM,)), dma((11,))],
        compiler_params=pltpu.CompilerParams(
            collective_id=0, has_side_effects=True, vmem_limit_bytes=60 * 2**20
        ),
        name="exit_head",
    )(hidden, gain, head_weight, targets, exit_ids, counts, exit_scale)
    loss, grad_weight, grad_hidden = pl.pallas_call(
        handover,
        out_shape=(jax.ShapeDtypeStruct((1, 1), F32), big, small),
        in_specs=[vmem, hbm, vmem],
        out_specs=(vmem, hbm, vmem),
        scratch_shapes=[pltpu.VMEM((D, VW), BF16), dma((8,))],
        compiler_params=pltpu.CompilerParams(vmem_limit_bytes=16 * 2**20),
        name="handover",
    )(*results)
    return (loss.reshape(()), grad_weight, grad_hidden)


def solution(mesh):
    in_specs = (P("section", None), P(), P(), P(None, ("section", "vocab")), P(), P(), P())
    out_specs = (P(), P(None, ("section", "vocab")), P("section", "vocab"))
    return jax.shard_map(body, mesh=mesh, in_specs=in_specs, out_specs=out_specs, check_vma=False)
```

```python
import jax
import jax.numpy as jnp
from jax import lax
from jax.experimental import pallas as pl
from jax.experimental.pallas import tpu as pltpu
from jax.sharding import PartitionSpec as P

MESH = pl.DeviceIdType.MESH
NX, NZ, NY = 4, 8, 4
CAP = 80
D = 8192
VW = 256
ROWS = NX * CAP
EXITS = 4
F32 = jnp.float32
BF16 = jnp.bfloat16
ZW, YW = 384, 896
XB0 = NZ * ZW + NY * YW
XBW = 768
SHIFT = 0
XA0 = XB0 + XBW
ZORD = (4, 3, 5, 2, 6, 1, 7, 0)
ZPOS = {d: k for k, d in enumerate(ZORD)}
N_SEND = 40
N_RECV = 174
HALVES = ((0, 48, 32), (48, 32, 16))
PARTS = (((0, 0, 256), (16, 0, 256), (32, 0, 256)), ((48, 0, 256), (64, 0, 128), (64, 128, 128)))
TN = (((0,), (0,)), ((), ()))


def scratch():
    out = dict(
        hid=((CAP, D), BF16), gain=((EXITS, D), F32), n_all=((NX, CAP, D), BF16), w_all=((D, 2 * VW), BF16), w_t=((2 * VW, D), BF16),
        logit=((NX, CAP, 2 * VW), F32), dl=((NX, CAP, 2 * VW), BF16),
        s1=((2, NZ, 2, 8, 128), F32), s2=((2, NX * NY, 2, 8, 128), F32),
        st=((2, 3, 8, 128), F32), ids=((2, 8, 128), F32), loss=((2, 8, 128), F32), dn=((CAP, VW), F32),
        mine=((D, VW), F32), gs=((D, VW), BF16), gr=((D, VW), BF16),
    )
    for h in range(2):
        lx, lz, ly = [p[2] for p in PARTS[h]]
        out[f"px{h}"] = ((NX, NZ, NY, 16, lx), BF16)
        out[f"pz{h}"] = ((NZ, NX, NY, 16, lz), BF16)
        out[f"py{h}"] = ((NY, NX, NZ, 16, ly), BF16)
        out[f"ax{h}"] = ((2, 2, 4, 2, 16, lx), BF16)
        out[f"bx{h}"] = ((2, 2, 1, NZ, 2, 16, lx), BF16)
        out[f"az{h}"] = ((2, 2, 2, 2, 16, lz), BF16)
        out[f"bz{h}"] = ((2, 2, 3, NX, 2, 16, lz), BF16)
        out[f"ay{h}"] = ((2, 2, 2, 4, 16, ly), BF16)
        out[f"by{h}"] = ((2, 2, 1, NX, 4, 16, ly), BF16)
        out[f"cx{h}"] = ((NY - 1, NZ, 16, lx), BF16)
        out[f"cz{h}"] = ((NX - 1, NY, 16, lz), BF16)
        out[f"cy{h}"] = ((NX - 1, NZ, 16, ly), BF16)
        out[f"ex{h}"] = ((NZ - 1, 16, lx), BF16)
        out[f"ez{h}"] = ((NY - 1, 16, lz), BF16)
        out[f"ey{h}"] = ((NZ - 1, 16, ly), BF16)
    return out


SCRATCH = scratch()


def kernel(hidden, gain_in, head, targets, exit_ids, counts, scale, loss_out, gw_out, gh_out, *refs):
    b = dict(zip(SCRATCH, refs))
    ssem, rsem, lsem = refs[len(SCRATCH) :]
    hid, gain, n_all, w_all, w_t = b["hid"], b["gain"], b["n_all"], b["w_all"], b["w_t"]
    logit, dl, s1, s2, st, ids = b["logit"], b["dl"], b["s1"], b["s2"], b["st"], b["ids"]
    dn, mine, gs, gr, loss_x = b["dn"], b["mine"], b["gs"], b["gr"], b["loss"]
    s = lax.axis_index("section")
    v = lax.axis_index("vocab")
    x, c = lax.div(s, 2), lax.rem(s, 2)
    z, y = lax.div(v, NY), lax.rem(v, NY)

    def dev(dx=0, dc=0, dz=0, dy=0):
        return (
            lax.rem(x + dx + NX, NX) * 2 + lax.rem(c + dc, 2),
            lax.rem(z + dz + NZ, NZ) * NY + lax.rem(y + dy + NY, NY),
        )

    slots = [0]
    pool = [None] * N_SEND
    count = [0]
    pending = {}
    outs = []
    cps = {}
    events = []

    def slot():
        slots[0] += 1
        return slots[0] - 1

    def send(src, dst, device, at_slot=None):
        at_slot = slot() if at_slot is None else at_slot
        i = count[0] % N_SEND
        count[0] += 1
        if pool[i] is not None:
            pool[i].wait_send()
        cp = pltpu.make_async_remote_copy(
            src_ref=src, dst_ref=dst, send_sem=ssem.at[i], recv_sem=rsem.at[at_slot],
            device_id=device, device_id_type=MESH,
        )
        cp.start()
        pool[i] = cp
        pending.setdefault(at_slot, []).append(cp)
        return at_slot

    def arrived(at_slot, ref):
        pltpu.make_async_copy(ref, ref, rsem.at[at_slot]).wait()
        del pending[at_slot]

    def at(time, fn, *args):
        events.append((time, len(events), lambda: fn(*args)))

    def run():
        for _, _, fn in sorted(events, key=lambda e: (e[0], e[1])):
            fn()
        events.clear()

    barrier = pltpu.get_barrier_semaphore()
    friends = [dict(dc=1)]
    friends += [dict(dz=i) for i in range(1, NZ)]
    friends += [dict(dx=i, dy=j) for i in range(NX) for j in range(NY) if i or j]
    for f in friends:
        pl.semaphore_signal(barrier, inc=1, device_id=dev(**f), device_id_type=MESH)
    own_w = pl.ds(pl.multiple_of(c * VW, VW), VW)
    loads = [
        pltpu.make_async_copy(hidden, hid, lsem.at[0]),
        pltpu.make_async_copy(gain_in, gain, lsem.at[1]),
        pltpu.make_async_copy(head, w_all.at[:, own_w], lsem.at[2]),
    ]
    for cp in loads:
        cp.start()

    diag = lax.broadcasted_iota(jnp.int32, (CAP, 128), 0) == lax.broadcasted_iota(
        jnp.int32, (CAP, 128), 1
    )
    lane = lax.broadcasted_iota(jnp.int32, (8, 128), 1)
    sub8 = lax.broadcasted_iota(jnp.int32, (8, 128), 0)
    flat = sub8 * 128 + lane
    upper = sub8 < 4

    def to_col(row):
        return jnp.sum(jnp.where(diag, jnp.broadcast_to(row, (CAP, 128)), 0.0), axis=1, keepdims=True)

    def to_row(col, r0):
        n = col.shape[0]
        return jnp.sum(
            jnp.where(diag[r0 : r0 + n], jnp.broadcast_to(col, (n, 128)), 0.0), axis=0, keepdims=True
        )

    def spread(slot, ref):
        def one(r, acc):
            for q in range(NX):
                acc = jnp.where(flat == q * 128 + r, ref[(q * 2 + c) * CAP + r], acc)
            return acc

        acc = lax.fori_loop(0, CAP, one, jnp.zeros((8, 128), jnp.int32), unroll=4)
        ids[slot] = acc.astype(F32)

    spread(0, exit_ids)
    own_exit = to_col(ids[0, pl.ds(x, 1), :])

    def gain_rows(cols, e):
        g = jnp.broadcast_to(gain[0:1, cols], (CAP, cols.size))
        for i in range(1, EXITS):
            g = jnp.where(e == float(i), gain[i : i + 1, cols], g)
        return g

    def squares(i, acc):
        xs = hid[:, pl.ds(pl.multiple_of(i * 512, 512), 512)].astype(F32)
        xs = xs * xs
        for j in range(4):
            acc = acc + xs[:, j * 128 : (j + 1) * 128]
        return acc

    loads[0].wait()
    total_sq = lax.fori_loop(0, D // 512, squares, jnp.zeros((CAP, 128), F32))
    rinv = lax.rsqrt(jnp.sum(total_sq, axis=1, keepdims=True) / D + 1e-05)

    def norm_chunk(i, carry):
        cols = pl.ds(pl.multiple_of(i * 512, 512), 512)
        xs = hid[:, cols].astype(F32)
        n_all[0, :, cols] = (xs * rinv * gain_rows(cols, own_exit)).astype(BF16)
        return carry

    loads[1].wait()
    lax.fori_loop(0, D // 512, norm_chunk, 0)
    pl.semaphore_wait(barrier, len(friends))

    def zc(d):
        return pl.ds(pl.multiple_of(lax.rem(z + d + NZ, NZ) * ZW, ZW), ZW)

    def yc(d):
        return pl.ds(pl.multiple_of(NZ * ZW + lax.rem(y + d + NY, NY) * YW, 128), YW)

    xb, xa = pl.ds(XB0, XBW), pl.ds(XA0, D - XA0)

    def own_x(tag, h, cols, far):
        rows = pl.ds(*HALVES[h][:2])
        src = n_all.at[0, rows, cols]
        k = slot()
        send(src, n_all.at[3, rows, cols], dev(dx=1), k)
        send(src, n_all.at[1, rows, cols], dev(dx=-1), k)
        if far:
            send(src, n_all.at[2, rows, cols], dev(dx=2), k)
        cps[tag, h] = k, n_all.at[0 : 3 if far else 2, rows, cols]

    def forward_x(tag, h, cols, right):
        rows = pl.ds(*HALVES[h][:2])
        rel, dx = (3, 1) if right else (1, -1)
        dst = n_all.at[2, rows, cols]
        cps[tag, h, 2] = send(n_all.at[rel, rows, cols], dst, dev(dx=dx)), dst

    def chain(tag, h, n, cols, axis, rel, t0, step):
        half = n // 2
        r0, n_rows, n_low = HALVES[h]
        full, low, high = pl.ds(r0, n_rows), pl.ds(r0, n_low), pl.ds(r0 + n_low, n_rows - n_low)

        def begin():
            for sign in (1, -1):
                ref = n_all.at[rel, full, cols(0)]
                cps[tag, h, rel, sign, 1] = send(ref, ref, dev(**{axis: sign})), ref

        def arrive(sign, k):
            arrived(*cps[tag, h, rel, sign, k])
            if k < half:
                rows = full if k < half - 1 else (low if sign == 1 else high)
                ref = n_all.at[rel, rows, cols(-sign * k)]
                cps[tag, h, rel, sign, k + 1] = send(ref, ref, dev(**{axis: sign})), ref

        for k in range(1, half + 1):
            for sign in (1, -1):
                at(t0 + step * k, arrive, sign, k)
        return begin

    def gather(h, tz, ty, tb, ta, fwd, zstep, ystep, after_z, after_y):
        chains = {}
        for rel in (1, 3, 2):
            chains["z", rel] = chain("cz", h, NZ, zc, "dz", rel, tz + 0.1 * rel, zstep)
            chains["y", rel] = chain("cy", h, NY, yc, "dy", rel, ty + 0.1 * rel, ystep)

        def got(key, *then):
            arrived(*cps[key])
            for fn in then:
                fn()

        for tag, t, then in (("z", tz, after_z), ("y", ty, after_y)):
            at(t, got, (tag, h), chains[tag, 1], chains[tag, 3], chains[tag, 2], then)
        at(tb, got, ("b", h), lambda: forward_x("b", h, xb, False))
        at(ta, got, ("a", h), lambda: forward_x("a", h, xa, True))
        at(tb + fwd, got, ("b", h, 2))
        at(ta + fwd, got, ("a", h, 2))
        return max(e[0] for e in events) + 0.01

    def own_group(h):
        own_x("b", h, xb, False)
        own_x("a", h, xa, False)

    nop = lambda: None
    own_x("z", 0, zc(0), True)
    own_x("y", 0, yc(0), True)
    own_x("z", 1, zc(0), True)
    own_x("y", 1, yc(0), True)
    here0 = SHIFT + gather(0, 4.0, 5.5, 10.0, 10.0, 4.0, 3.0, 4.0, nop, lambda: own_group(0))
    here1 = SHIFT + gather(1, 6.0, 7.5, 14.0, 14.0, 4.0, 3.2, 4.2, nop, lambda: own_group(1))

    def swap_w():
        loads[2].wait()
        mine_w = w_all.at[:, own_w]
        cps["w"] = send(mine_w, mine_w, dev(dc=1)), mine_w

    at(3.2, swap_w)
    at(3.3, spread, 1, targets)

    def weights():
        weight = jnp.zeros((8, 128), F32)
        exits = ids[0]
        for i in range(EXITS):
            weight = jnp.where(exits == float(i), scale[i], weight)
        for q in range(NX):
            weight = jnp.where((sub8 == q) & (lane >= counts[q * 2 + c]), 0.0, weight)
        for h in range(2):
            r0, n_rows, _ = HALVES[h]
            st[h, 1] = jnp.where((sub8 < NX) & (lane >= r0) & (lane < r0 + n_rows), weight, 0.0)

    at(3.4, weights)

    def logits(h, first, last):
        r0, n_rows, _ = HALVES[h]

        def one(i, carry):
            k = pl.ds(pl.multiple_of(i * 2048, 2048), 2048)
            n = n_all[:, r0 : r0 + n_rows, k].reshape(NX * n_rows, 2048)
            part = jnp.dot(n, w_all[k, :], preferred_element_type=F32)
            logit[:, r0 : r0 + n_rows, :] += part.reshape(NX, n_rows, 2 * VW)
            return carry

        lax.fori_loop(first, last, one, 0)

    def clear():
        logit[...] = jnp.zeros_like(logit)
        arrived(*cps["w"])

    def turn_w(i):
        f = pl.ds(i * 512, 512)
        w_t[:, f] = jnp.transpose(w_all[f, :], (1, 0))

    entry = lax.broadcasted_iota(jnp.int32, (CAP, 2 * VW), 1)
    base = (x * 2 * NZ * NY + v) * VW
    entry = jnp.where(entry < VW, entry + base, entry + (base + (NZ * NY - 1) * VW)).astype(F32)

    def column(ref, rel, r0, n):
        return to_col(ref[pl.ds(lax.rem(x + rel, NX), 1), :])[r0 : r0 + n]

    def local_stats(h):
        r0, n, _ = HALVES[h]
        stats = [jnp.zeros((8, 128), F32)] * 4
        for rel in range(NX):
            l = logit[rel, r0 : r0 + n, :]
            hit = entry[:n] == column(ids.at[1], rel, r0, n)
            m = jnp.max(l, axis=1, keepdims=True)
            e = jnp.exp(l - m)
            values = (
                m,
                jnp.sum(e, axis=1, keepdims=True),
                jnp.sum(e * l, axis=1, keepdims=True),
                jnp.sum(jnp.where(hit, l, 0.0), axis=1, keepdims=True),
            )
            here = sub8 == lax.rem(x + rel, NX)
            for i in range(4):
                row = jnp.broadcast_to(to_row(values[i], r0), (8, 128))
                stats[i] = jnp.where(here, row, stats[i])
        s1[h, z, 0] = jnp.where(upper, stats[0], pltpu.roll(stats[1], 4, 0))
        s1[h, z, 1] = jnp.where(upper, stats[2], pltpu.roll(stats[3], 4, 0))
        cps["s1", h] = slot()
        for i in range(1, NZ):
            send(s1.at[h, z], s1.at[h, z], dev(dz=i), cps["s1", h])

    def merge(ref, n):
        first = [ref[q, 0] for q in range(n)]
        peaks = [jnp.where(upper, a, pltpu.roll(a, 4, 0)) for a in first]
        peak = peaks[0]
        for p in peaks[1:]:
            peak = jnp.maximum(peak, p)
        f = [jnp.exp(p - peak) for p in peaks]
        total = sum(a * g for a, g in zip(first, f))
        rest = sum(ref[q, 1] * jnp.where(upper, f[q], 1.0) for q in range(n))
        return jnp.where(upper, peak, total), rest

    own = x * NY + y

    def stats_z(h):
        arrived(cps["s1", h], s1.at[h, 0 : NZ - 1])
        s2[h, own, 0], s2[h, own, 1] = merge(s1.at[h], NZ)
        cps["s2", h] = slot()
        for i in range(NX):
            for j in range(NY):
                if i or j:
                    send(s2.at[h, own], s2.at[h, own], dev(dx=i, dy=j), cps["s2", h])

    losses = []

    def stats_xy(h):
        arrived(cps["s2", h], s2.at[h, 0 : NX * NY - 1])
        peak, mean = merge(s2.at[h], NX * NY)
        total, chosen = pltpu.roll(peak, 4, 0), pltpu.roll(mean, 4, 0)
        lse = peak + jnp.log(total)
        weight = st[h, 1]
        live = weight != 0.0
        st[h, 0] = lse
        st[h, 2] = jnp.where(live, weight * (mean / total - chosen), 0.0)
        losses.append(jnp.where(live, weight * (lse - chosen), 0.0))
        if h == 1:
            own_loss = losses[0] + losses[1]
            own_loss = jnp.sum(jnp.sum(own_loss, axis=1, keepdims=True), axis=0, keepdims=True)
            loss_x[0] = jnp.broadcast_to(own_loss, (8, 128))
            cps["loss"] = send(loss_x.at[0], loss_x.at[1], dev(dc=1))
        r0, n, _ = HALVES[h]
        for rel in range(NX):
            lse_c, w_c = column(st.at[h, 0], rel, r0, n), column(st.at[h, 1], rel, r0, n)
            hit = jnp.where(entry[:n] == column(ids.at[1], rel, r0, n), 1.0, 0.0)
            p = jnp.exp(logit[rel, r0 : r0 + n, :] - lse_c)
            dl[rel, r0 : r0 + n, :] = (w_c * (p - hit)).astype(BF16)

    def grad_block(h, k, *then):
        r0, n, _ = HALVES[h]
        zz = lax.rem(z + ZORD[k], NZ)
        rows = dl[:, r0 : r0 + n, :].reshape(NX * n, 2 * VW)
        f = pl.ds(pl.multiple_of(zz * NY * VW, NY * VW), NY * VW)
        out = jnp.dot(rows, w_t[:, f], preferred_element_type=F32).astype(BF16)
        for yy in range(NY):
            ry = lax.rem(yy - y + NY, NY)
            for rx in range(NX):
                block = out[rx * n : (rx + 1) * n, yy * VW : (yy + 1) * VW]
                cut = [block[p[0] - r0 : p[0] - r0 + 16, p[1] : p[1] + p[2]] for p in PARTS[h]]
                b[f"px{h}"][rx, k, ry] = cut[0]
                b[f"pz{h}"][k, rx, ry] = cut[1]
                b[f"py{h}"][ry, rx, k] = cut[2]
        for fn in then:
            fn()

    def add_into(dst, srcs):
        def one(i, carry):
            acc = dst[i].astype(F32)
            for r in srcs:
                acc = acc + r[i].astype(F32)
            dst[i] = acc.astype(BF16)
            return carry

        lax.fori_loop(0, dst.shape[0], one, 0)

    def ring(tag, h, n, axis, block, one_way, buf_a, buf_b, times, done):
        half = n // 2
        side = {1: 0, -1: 1}
        left = [2]

        def begin(sign):
            for i in range(2):
                src = one_way(block(half, i), sign)
                cps[tag, h, sign, 1, i] = send(src, buf_a.at[side[sign], i], dev(**{axis: sign}))

        def arrive(sign, k, i):
            arrived(cps[tag, h, sign, k, i], buf_a.at[side[sign], i] if k == 1 else buf_b.at[side[sign], i, k - 2])
            d = (sign * (half - k)) % n
            if k == 1:
                add_into(one_way(block(d, i), sign), [buf_a.at[side[sign], i]])
            else:
                add_into(block(d, i), [buf_b.at[side[sign], i, k - 2]])
            cps[tag, h, sign, k + 1, i] = send(
                block(d, i), buf_b.at[side[sign], i, k - 1], dev(**{axis: sign})
            )

        def finish(i):
            for sign in (1, -1):
                arrived(cps[tag, h, sign, half, i], buf_b.at[side[sign], i, half - 2])
            add_into(block(0, i), [buf_b.at[side[sign], i, half - 2] for sign in (1, -1)])
            left[0] -= 1
            if left[0] == 0:
                done()

        for k in range(1, half):
            for i in range(2):
                for sign in (1, -1):
                    at(times[k - 1] + i * times[-1], arrive, sign, k, i)
        for i in range(2):
            at(times[half - 1] + i * times[-1], finish, i)
        return begin

    def direct(tag, h, n, axis, block, buf, time, done):
        def begin():
            cps[tag, h] = slot()
            for d in range(1, n):
                send(block(d), buf.at[d - 1], dev(**{axis: d}), cps[tag, h])

        def finish():
            arrived(cps[tag, h], buf)
            acc = block(0)[...].astype(F32)
            for d in range(1, n):
                acc = acc + buf[d - 1].astype(F32)
            done(acc)

        at(time, finish)
        return begin

    def reduce(h, t):
        px, pz, py = b[f"px{h}"], b[f"pz{h}"], b[f"py{h}"]

        def put(i):
            r, l, w = PARTS[h][i]
            def fn(acc):
                dn[r : r + 16, l : l + w] = acc
            return fn

        def back(ref, begin):
            def fn(acc):
                ref[...] = acc.astype(BF16)
                begin()
            return fn

        def cut(m):
            return lambda r, sign: r.at[0:m] if sign == 1 else r.at[m : 2 * m]

        x3 = direct("x3", h, NZ, "dz", lambda d: px.at[0, ZPOS[d], 0], b[f"ex{h}"], t["x3"], put(0))
        x2 = direct("x2", h, NY, "dy", lambda d: px.at[0, :, d], b[f"cx{h}"], t["x2"],
                    back(px.at[0, :, 0], x3))
        x1 = ring("x1", h, NX, "dx", lambda d, i: px.at[d, :, 2 * i : 2 * i + 2], cut(4),
                  b[f"ax{h}"], b[f"bx{h}"], t["x1"], x2)
        z3 = direct("z3", h, NY, "dy", lambda d: pz.at[7, 0, d], b[f"ez{h}"], t["z3"], put(1))
        z2 = direct("z2", h, NX, "dx", lambda d: pz.at[7, d], b[f"cz{h}"], t["z2"],
                    back(pz.at[7, 0], z3))
        z1 = ring("z1", h, NZ, "dz", lambda d, i: pz.at[ZPOS[d], :, 2 * i : 2 * i + 2], cut(2),
                  b[f"az{h}"], b[f"bz{h}"], t["z1"], z2)
        y3 = direct("y3", h, NZ, "dz", lambda d: py.at[0, 0, ZPOS[d]], b[f"ey{h}"], t["y3"], put(2))
        y2 = direct("y2", h, NX, "dx", lambda d: py.at[0, d], b[f"cy{h}"], t["y2"],
                    back(py.at[0, 0], y3))
        y1 = ring("y1", h, NY, "dy", lambda d, i: py.at[d, :, 4 * i : 4 * i + 4], cut(2),
                  b[f"ay{h}"], b[f"by{h}"], t["y1"], y2)
        then = {
            0: (lambda: z1(1), lambda: z1(-1)),
            3: (lambda: x1(1),),
            7: (lambda: x1(-1), lambda: y1(1), lambda: y1(-1)),
        }
        for k in range(NZ):
            at(t["g"] + t["gstep"] * k, grad_block, h, k, *then.get(k, ()))

    def head_chunk(j):
        f = pl.ds(j * 1024, 1024)
        n = n_all[:, :, f].reshape(ROWS, 1024)
        both = lax.dot_general(n, dl[...].reshape(ROWS, 2 * VW), TN, preferred_element_type=F32)
        first, second = both[:, :VW], both[:, VW:]
        mine[f, :] = jnp.where(c == 0, first, second)
        gs[f, :] = jnp.where(c == 0, second, first).astype(BF16)
        cps["g", j] = send(gs.at[f], gr.at[f], dev(dc=1))

    def head_sum(j):
        arrived(cps["g", j], gr.at[pl.ds(j * 1024, 1024)])

        def one(i, carry):
            f = pl.ds(pl.multiple_of(j * 1024 + i * 256, 256), 256)
            gr[f, :] = (mine[f, :] + gr[f, :].astype(F32)).astype(BF16)
            return carry

        lax.fori_loop(0, 4, one, 0)
        f = pl.ds(j * 1024, 1024)
        cp = pltpu.make_async_copy(gr.at[f], gw_out.at[f], lsem.at[3 + j])
        cp.start()
        outs.append(cp)

    at(7.6, clear)
    for i in range(16):
        at(8.6 + i * 0.5, turn_w, i)
    at(here0, logits, 0, 0, 4)
    at(here0, local_stats, 0)
    at(here1, logits, 1, 0, 4)
    at(here1, local_stats, 1)
    at(24.0, stats_z, 0)
    at(28.0, stats_z, 1)
    at(30.5, stats_xy, 0)
    at(34.4, stats_xy, 1)
    reduce(0, dict(
        g=31.0, gstep=0.5, z1=(34.5, 38.5, 42.5, 46.5, 0.8), x1=(38.7, 44.5, 1.5), y1=(38.8, 44.6, 1.5),
        x2=50.0, z2=50.1, y2=50.2, x3=55.0, z3=55.1, y3=55.2,
    ))
    reduce(1, dict(
        g=36.0, gstep=0.8, z1=(40.0, 44.0, 48.0, 52.0, 0.8), x1=(45.5, 52.5, 1.5), y1=(45.6, 51.6, 1.0),
        x2=57.0, z2=57.1, y2=56.0, x3=62.0, z3=62.1, y3=61.0,
    ))
    for j in range(8):
        at(42.0 + j * 1.2, head_chunk, j)
        at(53.0 + j * 0.5, head_sum, j)
    run()

    f = pl.ds(pl.multiple_of(v * VW, VW), VW)
    inner = to_col(st[0, 2, pl.ds(x, 1), :] + st[1, 2, pl.ds(x, 1), :])
    unit = hid[:, f].astype(F32) * rinv
    scaled = gain_rows(f, own_exit) * dn[...]
    gh_out[...] = (rinv * (scaled - unit * (inner / D))).astype(BF16)

    arrived(cps["loss"], loss_x.at[1])
    loss_out[...] = (loss_x[0] + loss_x[1]) / 512.0
    for cp in outs:
        cp.wait()
    for cp in pool:
        if cp is not None:
            cp.wait_send()
    assert not pending and slots[0] <= N_RECV, slots


def handover(loss, grad_weight, grad_hidden, loss_out, gw_out, gh_out, buf, small, total, sem):
    n = D // 4
    parts = [pl.ds(i * n, n) for i in range(4)]
    reads = [pltpu.make_async_copy(grad_weight.at[p], buf.at[p], sem.at[i]) for i, p in enumerate(parts)]
    writes = [pltpu.make_async_copy(buf.at[p], gw_out.at[p], sem.at[4 + i]) for i, p in enumerate(parts)]
    reads += [pltpu.make_async_copy(grad_hidden, small, sem.at[8])]
    writes += [pltpu.make_async_copy(small, gh_out, sem.at[9])]
    get_loss = pltpu.make_async_copy(loss, total, sem.at[10])
    for r in reads:
        r.start()
    get_loss.start()
    for r, w in zip(reads, writes):
        r.wait()
        w.start()
    get_loss.wait()
    loss_out[...] = total[0:1, 0:1]
    for w in writes:
        w.wait()


def body(hidden, gain, exit_scale, head_weight, targets, exit_ids, counts):
    vmem = pl.BlockSpec(memory_space=pltpu.VMEM)
    smem = pl.BlockSpec(memory_space=pltpu.SMEM)
    hbm = pl.BlockSpec(memory_space=pl.ANY)
    dma = pltpu.SemaphoreType.DMA
    big = jax.ShapeDtypeStruct((D, VW), BF16)
    small = jax.ShapeDtypeStruct((CAP, VW), BF16)
    results = pl.pallas_call(
        kernel,
        out_shape=(jax.ShapeDtypeStruct((8, 128), F32), big, small),
        in_specs=[hbm, hbm, hbm, smem, smem, smem, smem],
        out_specs=(vmem, hbm, vmem),
        scratch_shapes=[pltpu.VMEM(*v) for v in SCRATCH.values()] + [dma((N_SEND,)), dma((N_RECV,)), dma((11,))],
        compiler_params=pltpu.CompilerParams(
            collective_id=0, has_side_effects=True, vmem_limit_bytes=60 * 2**20
        ),
        name="exit_head",
    )(hidden, gain, head_weight, targets, exit_ids, counts, exit_scale)
    loss, grad_weight, grad_hidden = pl.pallas_call(
        handover,
        out_shape=(jax.ShapeDtypeStruct((1, 1), F32), big, small),
        in_specs=[hbm, hbm, hbm],
        out_specs=(vmem, hbm, hbm),
        scratch_shapes=[
            pltpu.VMEM((D, VW), BF16), pltpu.VMEM((CAP, VW), BF16), pltpu.VMEM((8, 128), F32), dma((11,)),
        ],
        compiler_params=pltpu.CompilerParams(vmem_limit_bytes=58 * 2**20),
        name="handover",
    )(*results)
    return (loss.reshape(()), grad_weight, grad_hidden)


def solution(mesh):
    in_specs = (P("section", None), P(), P(), P(None, ("section", "vocab")), P(), P(), P())
    out_specs = (P(), P(None, ("section", "vocab")), P("section", "vocab"))
    return jax.shard_map(body, mesh=mesh, in_specs=in_specs, out_specs=out_specs, check_vma=False)
```

```python
import jax
import jax.numpy as jnp
from jax import lax
from jax.experimental import pallas as pl
from jax.experimental.pallas import tpu as pltpu
from jax.sharding import PartitionSpec as P

MESH = pl.DeviceIdType.MESH
NX, NZ, NY = 4, 8, 4
CAP = 80
D = 8192
VW = 256
ROWS = NX * CAP
EXITS = 4
F32 = jnp.float32
BF16 = jnp.bfloat16
def widths(zw, yw, bw):
    return zw, yw, bw, D - NZ * zw - NY * yw - bw


WIDTHS = (widths(384, 640, 1280), widths(384, 768, 1152))
ZORD = (4, 3, 5, 2, 6, 1, 7, 0)
ZPOS = {d: k for k, d in enumerate(ZORD)}
N_SEND = 40
N_RECV = 174
HALVES = ((0, 48, 32), (48, 32, 16))
PARTS = (((0, 0, 256), (16, 0, 256), (32, 0, 256)), ((48, 0, 128), (64, 0, 256), (48, 128, 128)))
TN = (((0,), (0,)), ((), ()))
ORDER = (
    ("z", 0), ("y", 0), ("cz", 0, 1, 1, 1), ("cz", 0, 1, -1, 1), ("z", 1), ("cz", 0, 3, 1, 1),
    ("cz", 0, 3, -1, 1), ("w",), ("lg", 0, "z", 0), ("lg", 0, "y", 0), ("cz", 0, 2, 1, 1), ("cz", 0, 2, -1, 1),
    ("lg", 0, "z", 1), ("lg", 0, "z", 7), ("lg", 1, "z", 0), ("y", 1), ("cz", 0, 1, 1, 2), ("cz", 0, 1, -1, 2),
    ("lg", 1, "y", 0), ("cy", 0, 1, 1, 1), ("cy", 0, 1, -1, 1), ("cz", 1, 1, 1, 1), ("cz", 1, 1, -1, 1),
    ("turn", 0), ("turn", 1), ("cz", 1, 3, 1, 1), ("cz", 1, 3, -1, 1), ("cy", 0, 3, 1, 1), ("cy", 0, 3, -1, 1),
    ("turn", 2), ("cz", 1, 2, 1, 1), ("cz", 1, 2, -1, 1), ("b", 0), ("lg", 1, "z", 1), ("lg", 1, "z", 7),
    ("cz", 0, 3, 1, 2), ("cz", 0, 3, -1, 2), ("turn", 3), ("cy", 0, 2, 1, 1), ("cy", 0, 2, -1, 1),
    ("lg", 0, "y", 1), ("cz", 0, 2, 1, 2), ("cz", 0, 2, -1, 2), ("lg", 0, "z", 2), ("cy", 1, 1, 1, 1),
    ("cy", 1, 1, -1, 1), ("cz", 0, 1, 1, 3), ("cz", 0, 1, -1, 3), ("lg", 0, "z", 6), ("a", 0),
    ("lg", 0, "y", 3), ("cz", 1, 1, 1, 2), ("cz", 1, 1, -1, 2), ("cy", 1, 3, 1, 1), ("cy", 1, 3, -1, 1),
    ("turn", 4), ("cz", 1, 3, 1, 2), ("cz", 1, 3, -1, 2), ("turn", 5), ("cz", 1, 2, 1, 2), ("cz", 1, 2, -1, 2),
    ("lg", 1, "z", 2), ("cy", 1, 2, 1, 1), ("cy", 1, 2, -1, 1), ("b", 1), ("lg", 1, "z", 6),
    ("cy", 0, 1, -1, 2), ("cz", 0, 3, 1, 3), ("cz", 0, 3, -1, 3), ("lg", 1, "y", 1), ("cy", 0, 1, 1, 2),
    ("cy", 0, 3, -1, 2), ("cz", 0, 2, 1, 3), ("a", 1), ("cz", 0, 2, -1, 3), ("cy", 0, 2, -1, 2),
    ("lg", 0, "z", 3), ("cz", 0, 1, -1, 4), ("lg", 0, "z", 5), ("cy", 0, 3, 1, 2), ("cz", 0, 1, 1, 4),
    ("cy", 1, 1, -1, 2), ("lg", 1, "y", 3), ("cz", 1, 1, -1, 3), ("cz", 1, 1, 1, 3), ("cy", 1, 3, -1, 2),
    ("turn", 6), ("cz", 1, 3, -1, 3), ("cy", 0, 2, 1, 2), ("cz", 1, 3, 1, 3), ("lg", 0, "y", 2),
    ("cz", 1, 2, -1, 3), ("cy", 1, 1, 1, 2), ("cy", 1, 2, -1, 2), ("cz", 1, 2, 1, 3), ("cz", 0, 3, -1, 4),
    ("lg", 1, "z", 3), ("cy", 1, 3, 1, 2), ("a", 0, 2), ("cz", 0, 3, 1, 4), ("b", 0, 2), ("cz", 0, 2, -1, 4),
    ("lg", 0, "x"), ("cy", 1, 2, 1, 2), ("cz", 0, 2, 1, 4), ("lg", 0, "z", 4), ("ls", 0), ("cz", 1, 1, -1, 4),
    ("cz", 1, 1, 1, 4), ("a", 1, 2), ("b", 1, 2), ("cz", 1, 3, -1, 4), ("cz", 1, 3, 1, 4), ("cz", 1, 2, -1, 4),
    ("lg", 1, "z", 5), ("cz", 1, 2, 1, 4), ("lg", 1, "z", 4), ("lg", 1, "y", 2), ("lg", 1, "x"), ("ls", 1),
    ("turn", 7), ("turn", 8), ("turn", 9), ("turn", 10), ("turn", 11), ("turn", 12), ("turn", 13), ("sz", 0),
    ("turn", 14), ("turn", 15), ("sz", 1), ("sxy", 0), ("gb", 0, 0), ("gb", 0, 1), ("gb", 0, 2), ("gb", 0, 3),
    ("gb", 0, 4), ("sxy", 1), ("gb", 0, 5), ("gb", 0, 6), ("z1", 0, 1, 1, 0), ("z1", 0, -1, 1, 0), ("gb", 0, 7),
    ("gb", 1, 0), ("z1", 0, 1, 1, 1), ("z1", 0, -1, 1, 1), ("gb", 1, 1), ("gb", 1, 2), ("x1", 0, 1, 1, 0),
    ("gb", 1, 3), ("gb", 1, 4), ("gb", 1, 5), ("gb", 1, 6), ("x1", 0, 1, 1, 1), ("gb", 1, 7), ("head", 0),
    ("z1", 0, 1, 2, 0), ("z1", 0, -1, 2, 0), ("x1", 0, -1, 1, 0), ("y1", 0, 1, 1, 0), ("y1", 0, -1, 1, 0),
    ("z1", 1, 1, 1, 0), ("z1", 1, -1, 1, 0), ("z1", 1, 1, 1, 1), ("z1", 1, -1, 1, 1), ("head", 1),
    ("x1", 0, -1, 1, 1), ("y1", 0, 1, 1, 1), ("y1", 0, -1, 1, 1), ("z1", 0, 1, 2, 1), ("x1", 1, -1, 1, 0),
    ("z1", 0, -1, 2, 1), ("y1", 1, 1, 1, 0), ("y1", 1, -1, 1, 0), ("head", 2), ("x1", 1, -1, 1, 1),
    ("y1", 1, 1, 1, 1), ("y1", 1, -1, 1, 1), ("x1", 1, 1, 1, 0), ("z1", 0, 1, 3, 0), ("x1", 1, 1, 1, 1),
    ("z1", 0, -1, 3, 0), ("head", 3), ("head", 4), ("z1", 1, 1, 2, 0), ("z1", 1, -1, 2, 0), ("x1", 0, "fin", 0),
    ("y1", 0, "fin", 0), ("z1", 1, 1, 2, 1), ("z1", 1, -1, 2, 1), ("head", 5), ("head", 6), ("z1", 0, 1, 3, 1),
    ("z1", 0, -1, 3, 1), ("x1", 0, "fin", 1), ("y1", 0, "fin", 1), ("head", 7), ("z1", 0, "fin", 0),
    ("x1", 1, "fin", 0), ("y1", 1, "fin", 0), ("sum", 0), ("z1", 1, 1, 3, 0), ("z1", 1, -1, 3, 0),
    ("x1", 1, "fin", 1), ("y1", 1, "fin", 1), ("sum", 1), ("sum", 2), ("z1", 1, 1, 3, 1), ("z1", 1, -1, 3, 1),
    ("sum", 3), ("sum", 4), ("sum", 5), ("sum", 6), ("sum", 7), ("z1", 0, "fin", 1), ("x2", 0), ("y2", 0),
    ("z1", 1, "fin", 0), ("x2", 1), ("y2", 1), ("z1", 1, "fin", 1), ("z2", 0), ("x3", 0), ("z2", 1), ("z3", 0),
    ("y3", 0), ("x3", 1), ("y3", 1), ("z3", 1),
)
RANK = {key: i for i, key in enumerate(ORDER)}


def scratch():
    out = dict(
        hid=((CAP, D), BF16), gain=((EXITS, D), F32), n_all=((NX, CAP, D), BF16), w_all=((D, 2 * VW), BF16), w_t=((2 * VW, D), BF16),
        logit=((NX, CAP, 2 * VW), F32), dl=((NX, CAP, 2 * VW), BF16),
        s1=((2, NZ, 2, 8, 128), F32), s2=((2, NX * NY, 2, 8, 128), F32),
        st=((2, 3, 8, 128), F32), ids=((2, 8, 128), F32), loss=((2, 8, 128), F32), dn=((CAP, VW), F32),
        mine=((D, VW), F32), gs=((D, VW), BF16), gr=((D, VW), BF16),
    )
    for h in range(2):
        lx, lz, ly = [p[2] for p in PARTS[h]]
        out[f"px{h}"] = ((NX, NZ, NY, 16, lx), BF16)
        out[f"pz{h}"] = ((NZ, NX, NY, 16, lz), BF16)
        out[f"py{h}"] = ((NY, NX, NZ, 16, ly), BF16)
        out[f"ax{h}"] = ((2, 2, 4, 2, 16, lx), BF16)
        out[f"bx{h}"] = ((2, 2, 1, NZ, 2, 16, lx), BF16)
        out[f"az{h}"] = ((2, 2, 2, 2, 16, lz), BF16)
        out[f"bz{h}"] = ((2, 2, 3, NX, 2, 16, lz), BF16)
        out[f"ay{h}"] = ((2, 2, 2, 4, 16, ly), BF16)
        out[f"by{h}"] = ((2, 2, 1, NX, 4, 16, ly), BF16)
        out[f"cx{h}"] = ((NY - 1, NZ, 16, lx), BF16)
        out[f"cz{h}"] = ((NY - 1, NX, 16, lz), BF16)
        out[f"cy{h}"] = ((NX - 1, NZ, 16, ly), BF16)
        out[f"ex{h}"] = ((NZ - 1, 16, lx), BF16)
        out[f"ez{h}"] = ((NX - 1, 16, lz), BF16)
        out[f"ey{h}"] = ((NZ - 1, 16, ly), BF16)
    return out


SCRATCH = scratch()


def kernel(hidden, gain_in, head, targets, exit_ids, counts, scale, loss_out, gw_out, gh_out, *refs):
    b = dict(zip(SCRATCH, refs))
    ssem, rsem, lsem = refs[len(SCRATCH) :]
    hid, gain, n_all, w_all, w_t = b["hid"], b["gain"], b["n_all"], b["w_all"], b["w_t"]
    logit, dl, s1, s2, st, ids = b["logit"], b["dl"], b["s1"], b["s2"], b["st"], b["ids"]
    dn, mine, gs, gr, loss_x = b["dn"], b["mine"], b["gs"], b["gr"], b["loss"]
    s = lax.axis_index("section")
    v = lax.axis_index("vocab")
    x, c = lax.div(s, 2), lax.rem(s, 2)
    z, y = lax.div(v, NY), lax.rem(v, NY)

    def dev(dx=0, dc=0, dz=0, dy=0):
        return (
            lax.rem(x + dx + NX, NX) * 2 + lax.rem(c + dc, 2),
            lax.rem(z + dz + NZ, NZ) * NY + lax.rem(y + dy + NY, NY),
        )

    slots = [0]
    pool = [None] * N_SEND
    count = [0]
    pending = {}
    outs = []
    cps = {}
    events = []

    def slot():
        slots[0] += 1
        return slots[0] - 1

    def send(src, dst, device, at_slot=None):
        at_slot = slot() if at_slot is None else at_slot
        i = count[0] % N_SEND
        count[0] += 1
        if pool[i] is not None:
            pool[i].wait_send()
        cp = pltpu.make_async_remote_copy(
            src_ref=src, dst_ref=dst, send_sem=ssem.at[i], recv_sem=rsem.at[at_slot],
            device_id=device, device_id_type=MESH,
        )
        cp.start()
        pool[i] = cp
        pending.setdefault(at_slot, []).append(cp)
        return at_slot

    def arrived(at_slot, ref):
        pltpu.make_async_copy(ref, ref, rsem.at[at_slot]).wait()
        del pending[at_slot]

    def at(key, fn, *args):
        events.append((RANK[key], lambda: fn(*args)))

    def run():
        assert len(events) == len(RANK)
        for t_, fn in sorted(events, key=lambda e: e[0]):
            fn()

    barrier = pltpu.get_barrier_semaphore()
    friends = [dict(dc=1)]
    friends += [dict(dz=i) for i in range(1, NZ)]
    friends += [dict(dx=i, dy=j) for i in range(NX) for j in range(NY) if i or j]
    for f in friends:
        pl.semaphore_signal(barrier, inc=1, device_id=dev(**f), device_id_type=MESH)
    own_w = pl.ds(pl.multiple_of(c * VW, VW), VW)
    loads = [
        pltpu.make_async_copy(hidden, hid, lsem.at[0]),
        pltpu.make_async_copy(gain_in, gain, lsem.at[1]),
        pltpu.make_async_copy(head, w_all.at[:, own_w], lsem.at[2]),
    ]
    for cp in loads:
        cp.start()

    diag = lax.broadcasted_iota(jnp.int32, (CAP, 128), 0) == lax.broadcasted_iota(
        jnp.int32, (CAP, 128), 1
    )
    lane = lax.broadcasted_iota(jnp.int32, (8, 128), 1)
    sub8 = lax.broadcasted_iota(jnp.int32, (8, 128), 0)
    flat = sub8 * 128 + lane
    upper = sub8 < 4

    def to_col(row):
        return jnp.sum(jnp.where(diag, jnp.broadcast_to(row, (CAP, 128)), 0.0), axis=1, keepdims=True)

    def to_row(col, r0):
        n = col.shape[0]
        return jnp.sum(
            jnp.where(diag[r0 : r0 + n], jnp.broadcast_to(col, (n, 128)), 0.0), axis=0, keepdims=True
        )

    def spread(slot, ref):
        def one(r, acc):
            for q in range(NX):
                acc = jnp.where(flat == q * 128 + r, ref[(q * 2 + c) * CAP + r], acc)
            return acc

        acc = lax.fori_loop(0, CAP, one, jnp.zeros((8, 128), jnp.int32), unroll=4)
        ids[slot] = acc.astype(F32)

    spread(0, exit_ids)
    own_exit = to_col(ids[0, pl.ds(x, 1), :])

    def gain_rows(cols, e):
        g = jnp.broadcast_to(gain[0:1, cols], (CAP, cols.size))
        for i in range(1, EXITS):
            g = jnp.where(e == float(i), gain[i : i + 1, cols], g)
        return g

    def squares(i, acc):
        xs = hid[:, pl.ds(pl.multiple_of(i * 512, 512), 512)].astype(F32)
        xs = xs * xs
        for j in range(4):
            acc = acc + xs[:, j * 128 : (j + 1) * 128]
        return acc

    loads[0].wait()
    total_sq = lax.fori_loop(0, D // 512, squares, jnp.zeros((CAP, 128), F32))
    rinv = lax.rsqrt(jnp.sum(total_sq, axis=1, keepdims=True) / D + 1e-05)

    def norm_chunk(i, carry):
        cols = pl.ds(pl.multiple_of(i * 512, 512), 512)
        xs = hid[:, cols].astype(F32)
        n_all[0, :, cols] = (xs * rinv * gain_rows(cols, own_exit)).astype(BF16)
        return carry

    loads[1].wait()
    lax.fori_loop(0, D // 512, norm_chunk, 0)
    pl.semaphore_wait(barrier, len(friends))

    def columns(h, tag, d=0):
        zw, yw, bw, aw = WIDTHS[h]
        if tag == "z":
            return pl.ds(pl.multiple_of(lax.rem(z + d + NZ, NZ) * zw, 128), zw)
        if tag == "y":
            return pl.ds(pl.multiple_of(NZ * zw + lax.rem(y + d + NY, NY) * yw, 128), yw)
        return pl.ds(D - aw - bw, bw) if tag == "b" else pl.ds(D - aw, aw)

    def own_x(tag, h):
        rows, cols, far = pl.ds(*HALVES[h][:2]), columns(h, tag), tag in "zy"
        src = n_all.at[0, rows, cols]
        k = slot()
        send(src, n_all.at[3, rows, cols], dev(dx=1), k)
        send(src, n_all.at[1, rows, cols], dev(dx=-1), k)
        if far:
            send(src, n_all.at[2, rows, cols], dev(dx=2), k)
        cps[tag, h] = k, n_all.at[0 : 3 if far else 2, rows, cols]

    def chain(tag, h, n, axis, rel):
        half = n // 2
        r0, n_rows, n_low = HALVES[h]
        full, low, high = pl.ds(r0, n_rows), pl.ds(r0, n_low), pl.ds(r0 + n_low, n_rows - n_low)

        def begin():
            for sign in (1, -1):
                ref = n_all.at[rel, full, columns(h, tag)]
                cps[tag, h, rel, sign, 1] = send(ref, ref, dev(**{axis: sign})), ref

        def arrive(sign, k):
            arrived(*cps[tag, h, rel, sign, k])
            if k < half:
                rows = full if k < half - 1 else (low if sign == 1 else high)
                ref = n_all.at[rel, rows, columns(h, tag, -sign * k)]
                cps[tag, h, rel, sign, k + 1] = send(ref, ref, dev(**{axis: sign})), ref

        for k in range(1, half + 1):
            for sign in (1, -1):
                at(("c" + tag, h, rel, sign, k), arrive, sign, k)
        return begin

    def gather(h):
        def got(tag, then):
            arrived(*cps[tag, h])
            for fn in then:
                fn()

        def got_x(tag):
            arrived(*cps[tag, h])
            rows, cols = pl.ds(*HALVES[h][:2]), columns(h, tag)
            rel, dx = (1, -1) if tag == "b" else (3, 1)
            dst = n_all.at[2, rows, cols]
            cps[tag, h, 2] = send(n_all.at[rel, rows, cols], dst, dev(dx=dx)), dst

        own_rest = [lambda: own_x("b", h), lambda: own_x("a", h)]
        for tag, n, axis, more in (("z", NZ, "dz", []), ("y", NY, "dy", own_rest)):
            at((tag, h), got, tag, [chain(tag, h, n, axis, rel) for rel in (1, 3, 2)] + more)
            for d in range(n):
                at(("lg", h, tag, d), logits, h, tag, d)
        for tag in "ba":
            at((tag, h), got_x, tag)
            at((tag, h, 2), lambda tag=tag: arrived(*cps[tag, h, 2]))
        at(("lg", h, "x"), logits, h, "x", 0)

    def logits(h, tag, d):
        r0, n_rows, _ = HALVES[h]
        first = D - sum(WIDTHS[h][2:])
        k = pl.ds(first, D - first) if tag == "x" else columns(h, tag, d)
        n = n_all[:, r0 : r0 + n_rows, k].reshape(NX * n_rows, k.size)
        part = jnp.dot(n, w_all[k, :], preferred_element_type=F32)
        logit[:, r0 : r0 + n_rows, :] += part.reshape(NX, n_rows, 2 * VW)

    def take_w():
        arrived(*cps["w"])
        logit[...] = jnp.zeros_like(logit)

    def turn_w(i):
        f = pl.ds(i * 512, 512)
        w_t[:, f] = jnp.transpose(w_all[f, :], (1, 0))

    for h in range(2):
        own_x("z", h)
        own_x("y", h)
    for h in range(2):
        gather(h)
    loads[2].wait()
    mine_w = w_all.at[:, own_w]
    cps["w"] = send(mine_w, mine_w, dev(dc=1)), mine_w
    at(("w",), take_w)
    for i in range(16):
        at(("turn", i), turn_w, i)

    def weights():
        spread(1, targets)
        weight = jnp.zeros((8, 128), F32)
        exits = ids[0]
        for i in range(EXITS):
            weight = jnp.where(exits == float(i), scale[i], weight)
        for q in range(NX):
            weight = jnp.where((sub8 == q) & (lane >= counts[q * 2 + c]), 0.0, weight)
        for h in range(2):
            r0, n_rows, _ = HALVES[h]
            st[h, 1] = jnp.where((sub8 < NX) & (lane >= r0) & (lane < r0 + n_rows), weight, 0.0)

    weights()

    entry = lax.broadcasted_iota(jnp.int32, (CAP, 2 * VW), 1)
    base = (x * 2 * NZ * NY + v) * VW
    entry = jnp.where(entry < VW, entry + base, entry + (base + (NZ * NY - 1) * VW)).astype(F32)

    def column(ref, rel, r0, n):
        return to_col(ref[pl.ds(lax.rem(x + rel, NX), 1), :])[r0 : r0 + n]

    def local_stats(h):
        r0, n, _ = HALVES[h]
        stats = [jnp.zeros((8, 128), F32)] * 4
        for rel in range(NX):
            l = logit[rel, r0 : r0 + n, :]
            hit = entry[:n] == column(ids.at[1], rel, r0, n)
            m = jnp.max(l, axis=1, keepdims=True)
            e = jnp.exp(l - m)
            values = (
                m,
                jnp.sum(e, axis=1, keepdims=True),
                jnp.sum(e * l, axis=1, keepdims=True),
                jnp.sum(jnp.where(hit, l, 0.0), axis=1, keepdims=True),
            )
            here = sub8 == lax.rem(x + rel, NX)
            for i in range(4):
                row = jnp.broadcast_to(to_row(values[i], r0), (8, 128))
                stats[i] = jnp.where(here, row, stats[i])
        s1[h, z, 0] = jnp.where(upper, stats[0], pltpu.roll(stats[1], 4, 0))
        s1[h, z, 1] = jnp.where(upper, stats[2], pltpu.roll(stats[3], 4, 0))
        cps["s1", h] = slot()
        for i in range(1, NZ):
            send(s1.at[h, z], s1.at[h, z], dev(dz=i), cps["s1", h])

    def merge(ref, n):
        first = [ref[q, 0] for q in range(n)]
        peaks = [jnp.where(upper, a, pltpu.roll(a, 4, 0)) for a in first]
        peak = peaks[0]
        for p in peaks[1:]:
            peak = jnp.maximum(peak, p)
        f = [jnp.exp(p - peak) for p in peaks]
        total = sum(a * g for a, g in zip(first, f))
        rest = sum(ref[q, 1] * jnp.where(upper, f[q], 1.0) for q in range(n))
        return jnp.where(upper, peak, total), rest

    own = x * NY + y

    def stats_z(h):
        arrived(cps["s1", h], s1.at[h, 0 : NZ - 1])
        s2[h, own, 0], s2[h, own, 1] = merge(s1.at[h], NZ)
        cps["s2", h] = slot()
        for i in range(NX):
            for j in range(NY):
                if i or j:
                    send(s2.at[h, own], s2.at[h, own], dev(dx=i, dy=j), cps["s2", h])

    losses = []

    def stats_xy(h):
        arrived(cps["s2", h], s2.at[h, 0 : NX * NY - 1])
        peak, mean = merge(s2.at[h], NX * NY)
        total, chosen = pltpu.roll(peak, 4, 0), pltpu.roll(mean, 4, 0)
        lse = peak + jnp.log(total)
        weight = st[h, 1]
        live = weight != 0.0
        st[h, 0] = lse
        st[h, 2] = jnp.where(live, weight * (mean / total - chosen), 0.0)
        losses.append(jnp.where(live, weight * (lse - chosen), 0.0))
        if h == 1:
            own_loss = losses[0] + losses[1]
            own_loss = jnp.sum(jnp.sum(own_loss, axis=1, keepdims=True), axis=0, keepdims=True)
            loss_x[0] = jnp.broadcast_to(own_loss, (8, 128))
            cps["loss"] = send(loss_x.at[0], loss_x.at[1], dev(dc=1))
        r0, n, _ = HALVES[h]
        for rel in range(NX):
            lse_c, w_c = column(st.at[h, 0], rel, r0, n), column(st.at[h, 1], rel, r0, n)
            hit = jnp.where(entry[:n] == column(ids.at[1], rel, r0, n), 1.0, 0.0)
            p = jnp.exp(logit[rel, r0 : r0 + n, :] - lse_c)
            dl[rel, r0 : r0 + n, :] = (w_c * (p - hit)).astype(BF16)

    def grad_block(h, k, *then):
        r0, n, _ = HALVES[h]
        zz = lax.rem(z + ZORD[k], NZ)
        rows = dl[:, r0 : r0 + n, :].reshape(NX * n, 2 * VW)
        f = pl.ds(pl.multiple_of(zz * NY * VW, NY * VW), NY * VW)
        out = jnp.dot(rows, w_t[:, f], preferred_element_type=F32).astype(BF16)
        for yy in range(NY):
            ry = lax.rem(yy - y + NY, NY)
            for rx in range(NX):
                block = out[rx * n : (rx + 1) * n, yy * VW : (yy + 1) * VW]
                cut = [block[p[0] - r0 : p[0] - r0 + 16, p[1] : p[1] + p[2]] for p in PARTS[h]]
                b[f"px{h}"][rx, k, ry] = cut[0]
                b[f"pz{h}"][k, rx, ry] = cut[1]
                b[f"py{h}"][ry, rx, k] = cut[2]
        for fn in then:
            fn()

    def add_into(dst, srcs):
        def one(i, carry):
            acc = dst[i].astype(F32)
            for r in srcs:
                acc = acc + r[i].astype(F32)
            dst[i] = acc.astype(BF16)
            return carry

        lax.fori_loop(0, dst.shape[0], one, 0)

    def ring(tag, h, n, axis, block, one_way, buf_a, buf_b, done):
        half = n // 2
        side = {1: 0, -1: 1}
        left = [2]

        def begin(sign):
            for i in range(2):
                src = one_way(block(half, i), sign)
                cps[tag, h, sign, 1, i] = send(src, buf_a.at[side[sign], i], dev(**{axis: sign}))

        def arrive(sign, k, i):
            arrived(cps[tag, h, sign, k, i], buf_a.at[side[sign], i] if k == 1 else buf_b.at[side[sign], i, k - 2])
            d = (sign * (half - k)) % n
            if k == 1:
                add_into(one_way(block(d, i), sign), [buf_a.at[side[sign], i]])
            else:
                add_into(block(d, i), [buf_b.at[side[sign], i, k - 2]])
            cps[tag, h, sign, k + 1, i] = send(
                block(d, i), buf_b.at[side[sign], i, k - 1], dev(**{axis: sign})
            )

        def finish(i):
            for sign in (1, -1):
                arrived(cps[tag, h, sign, half, i], buf_b.at[side[sign], i, half - 2])
            add_into(block(0, i), [buf_b.at[side[sign], i, half - 2] for sign in (1, -1)])
            left[0] -= 1
            if left[0] == 0:
                done()

        for k in range(1, half):
            for i in range(2):
                for sign in (1, -1):
                    at((tag, h, sign, k, i), arrive, sign, k, i)
        for i in range(2):
            at((tag, h, "fin", i), finish, i)
        return begin

    def direct(tag, h, n, axis, block, buf, done):
        def begin():
            cps[tag, h] = slot()
            for d in range(1, n):
                send(block(d), buf.at[d - 1], dev(**{axis: d}), cps[tag, h])

        def finish():
            arrived(cps[tag, h], buf)
            acc = block(0)[...].astype(F32)
            for d in range(1, n):
                acc = acc + buf[d - 1].astype(F32)
            done(acc)

        at((tag, h), finish)
        return begin

    def reduce(h):
        px, pz, py = b[f"px{h}"], b[f"pz{h}"], b[f"py{h}"]

        def put(i):
            r, l, w = PARTS[h][i]
            def fn(acc):
                dn[r : r + 16, l : l + w] = acc
            return fn

        def back(ref, begin):
            def fn(acc):
                ref[...] = acc.astype(BF16)
                begin()
            return fn

        def cut(m):
            return lambda r, sign: r.at[0:m] if sign == 1 else r.at[m : 2 * m]

        x3 = direct("x3", h, NZ, "dz", lambda d: px.at[0, ZPOS[d], 0], b[f"ex{h}"], put(0))
        x2 = direct("x2", h, NY, "dy", lambda d: px.at[0, :, d], b[f"cx{h}"], back(px.at[0, :, 0], x3))
        x1 = ring("x1", h, NX, "dx", lambda d, i: px.at[d, :, 2 * i : 2 * i + 2], cut(4),
                  b[f"ax{h}"], b[f"bx{h}"], x2)
        z3 = direct("z3", h, NX, "dx", lambda d: pz.at[7, d, 0], b[f"ez{h}"], put(1))
        z2 = direct("z2", h, NY, "dy", lambda d: pz.at[7, :, d], b[f"cz{h}"], back(pz.at[7, :, 0], z3))
        z1 = ring("z1", h, NZ, "dz", lambda d, i: pz.at[ZPOS[d], :, 2 * i : 2 * i + 2], cut(2),
                  b[f"az{h}"], b[f"bz{h}"], z2)
        y3 = direct("y3", h, NZ, "dz", lambda d: py.at[0, 0, ZPOS[d]], b[f"ey{h}"], put(2))
        y2 = direct("y2", h, NX, "dx", lambda d: py.at[0, d], b[f"cy{h}"], back(py.at[0, 0], y3))
        y1 = ring("y1", h, NY, "dy", lambda d, i: py.at[d, :, 4 * i : 4 * i + 4], cut(2),
                  b[f"ay{h}"], b[f"by{h}"], y2)
        then = {
            0: (lambda: z1(1), lambda: z1(-1)),
            3: (lambda: x1(1),),
            7: (lambda: x1(-1), lambda: y1(1), lambda: y1(-1)),
        }
        for k in range(NZ):
            at(("gb", h, k), grad_block, h, k, *then.get(k, ()))

    def head_chunk(j):
        f = pl.ds(j * 1024, 1024)
        n = n_all[:, :, f].reshape(ROWS, 1024)
        both = lax.dot_general(n, dl[...].reshape(ROWS, 2 * VW), TN, preferred_element_type=F32)
        first, second = both[:, :VW], both[:, VW:]
        mine[f, :] = jnp.where(c == 0, first, second)
        gs[f, :] = jnp.where(c == 0, second, first).astype(BF16)
        cps["g", j] = send(gs.at[f], gr.at[f], dev(dc=1))

    def head_sum(j):
        arrived(cps["g", j], gr.at[pl.ds(j * 1024, 1024)])

        def one(i, carry):
            f = pl.ds(pl.multiple_of(j * 1024 + i * 256, 256), 256)
            gr[f, :] = (mine[f, :] + gr[f, :].astype(F32)).astype(BF16)
            return carry

        lax.fori_loop(0, 4, one, 0)
        f = pl.ds(j * 1024, 1024)
        cp = pltpu.make_async_copy(gr.at[f], gw_out.at[f], lsem.at[3 + j])
        cp.start()
        outs.append(cp)

    for h in range(2):
        at(("ls", h), local_stats, h)
        at(("sz", h), stats_z, h)
        at(("sxy", h), stats_xy, h)
        reduce(h)
    for j in range(8):
        at(("head", j), head_chunk, j)
        at(("sum", j), head_sum, j)
    run()

    f = pl.ds(pl.multiple_of(v * VW, VW), VW)
    inner = to_col(st[0, 2, pl.ds(x, 1), :] + st[1, 2, pl.ds(x, 1), :])
    unit = hid[:, f].astype(F32) * rinv
    scaled = gain_rows(f, own_exit) * dn[...]
    gh_out[...] = (rinv * (scaled - unit * (inner / D))).astype(BF16)

    arrived(cps["loss"], loss_x.at[1])
    loss_out[...] = (loss_x[0] + loss_x[1]) / 512.0
    for cp in outs:
        cp.wait()
    for cp in pool:
        if cp is not None:
            cp.wait_send()
    assert not pending and slots[0] <= N_RECV, slots


def handover(loss, grad_weight, grad_hidden, loss_out, gw_out, gh_out, buf, small, total, sem):
    n = D // 4
    parts = [pl.ds(i * n, n) for i in range(4)]
    reads = [pltpu.make_async_copy(grad_weight.at[p], buf.at[p], sem.at[i]) for i, p in enumerate(parts)]
    writes = [pltpu.make_async_copy(buf.at[p], gw_out.at[p], sem.at[4 + i]) for i, p in enumerate(parts)]
    reads += [pltpu.make_async_copy(grad_hidden, small, sem.at[8])]
    writes += [pltpu.make_async_copy(small, gh_out, sem.at[9])]
    get_loss = pltpu.make_async_copy(loss, total, sem.at[10])
    for r in reads:
        r.start()
    get_loss.start()
    for r, w in zip(reads, writes):
        r.wait()
        w.start()
    get_loss.wait()
    loss_out[...] = total[0:1, 0:1]
    for w in writes:
        w.wait()


def body(hidden, gain, exit_scale, head_weight, targets, exit_ids, counts):
    vmem = pl.BlockSpec(memory_space=pltpu.VMEM)
    smem = pl.BlockSpec(memory_space=pltpu.SMEM)
    hbm = pl.BlockSpec(memory_space=pl.ANY)
    dma = pltpu.SemaphoreType.DMA
    big = jax.ShapeDtypeStruct((D, VW), BF16)
    small = jax.ShapeDtypeStruct((CAP, VW), BF16)
    results = pl.pallas_call(
        kernel,
        out_shape=(jax.ShapeDtypeStruct((8, 128), F32), big, small),
        in_specs=[hbm, hbm, hbm, smem, smem, smem, smem],
        out_specs=(vmem, hbm, vmem),
        scratch_shapes=[pltpu.VMEM(*v) for v in SCRATCH.values()] + [dma((N_SEND,)), dma((N_RECV,)), dma((11,))],
        compiler_params=pltpu.CompilerParams(
            collective_id=0, has_side_effects=True, vmem_limit_bytes=60 * 2**20
        ),
        name="exit_head",
    )(hidden, gain, head_weight, targets, exit_ids, counts, exit_scale)
    loss, grad_weight, grad_hidden = pl.pallas_call(
        handover,
        out_shape=(jax.ShapeDtypeStruct((1, 1), F32), big, small),
        in_specs=[hbm, hbm, hbm],
        out_specs=(vmem, hbm, hbm),
        scratch_shapes=[
            pltpu.VMEM((D, VW), BF16), pltpu.VMEM((CAP, VW), BF16), pltpu.VMEM((8, 128), F32), dma((11,)),
        ],
        compiler_params=pltpu.CompilerParams(vmem_limit_bytes=58 * 2**20),
        name="handover",
    )(*results)
    return (loss.reshape(()), grad_weight, grad_hidden)


def solution(mesh):
    in_specs = (P("section", None), P(), P(), P(None, ("section", "vocab")), P(), P(), P())
    out_specs = (P(), P(None, ("section", "vocab")), P("section", "vocab"))
    return jax.shard_map(body, mesh=mesh, in_specs=in_specs, out_specs=out_specs, check_vma=False)
```

```python
import jax
import jax.numpy as jnp
from jax import lax
from jax.experimental import pallas as pl
from jax.experimental.pallas import tpu as pltpu
from jax.sharding import PartitionSpec as P

MESH = pl.DeviceIdType.MESH
NX, NZ, NY = 4, 8, 4
CAP = 80
D = 8192
VW = 256
ROWS = NX * CAP
EXITS = 4
F32 = jnp.float32
BF16 = jnp.bfloat16
def widths(zw, yw, bw):
    return zw, yw, bw, D - NZ * zw - NY * yw - bw


WIDTHS = (widths(384, 768, 1152), widths(384, 768, 1408))
ZORD = (4, 3, 5, 2, 6, 1, 7, 0)
ZPOS = {d: k for k, d in enumerate(ZORD)}
N_SEND = 40
N_RECV = 176
HALVES = ((0, 48, 32), (48, 32, 16))
PARTS = (((0, 0, 256), (16, 0, 256), (32, 0, 256)), ((48, 0, 128), (64, 0, 256), (48, 128, 128)))
FIRST = (('z', 0), ('y', 0), ('z', 1))
AFTER = {('z', 0): (('b', 0), ('a', 0)), ('y', 0): (('y', 1), ('b', 1), ('a', 1))}
CHAINS = ((4, 1, 2), (1, 2, 4))
Z_AT_ONCE = (0, 1)
TN = (((0,), (0,)), ((), ()))
ORDER = (
    ("z", 0), ("cz", 0, 1, 1, 1), ("cz", 0, 1, -1, 1), ("y", 0), ("cz", 0, 3, 1, 1), ("w",),
    ("cz", 0, 3, -1, 1), ("z", 1), ("lg", 0, "z", 0), ("cz", 0, 2, 1, 1), ("cz", 0, 2, -1, 1),
    ("lg", 0, "z", 1), ("lg", 0, "z", 7), ("lg", 0, "y", 0), ("lg", 1, "z", 0), ("b", 0), ("turn", 0),
    ("cz", 0, 1, 1, 2), ("cz", 0, 1, -1, 2), ("turn", 1), ("turn", 2), ("cz", 0, 3, 1, 2), ("cy", 0, 1, 1, 1),
    ("cy", 0, 1, -1, 1), ("cz", 0, 3, -1, 2), ("turn", 3), ("cz", 1, 1, 1, 1), ("a", 0), ("cz", 1, 1, -1, 1),
    ("turn", 4), ("cz", 1, 3, 1, 1), ("turn", 5), ("cz", 1, 3, -1, 1), ("cz", 1, 2, 1, 1), ("cy", 0, 3, 1, 1),
    ("cy", 0, 3, -1, 1), ("lg", 1, "z", 7), ("cz", 1, 2, -1, 1), ("lg", 1, "z", 1), ("cz", 0, 2, 1, 2),
    ("lg", 0, "z", 6), ("cz", 0, 2, -1, 2), ("lg", 0, "z", 2), ("cz", 0, 1, 1, 3), ("cy", 0, 2, 1, 1),
    ("cy", 0, 2, -1, 1), ("lg", 0, "y", 1), ("cz", 0, 1, -1, 3), ("y", 1), ("cy", 0, 1, -1, 2),
    ("lg", 0, "y", 3), ("cz", 0, 3, 1, 3), ("cy", 0, 1, 1, 2), ("cz", 0, 3, -1, 3), ("lg", 1, "y", 0),
    ("cz", 1, 1, 1, 2), ("cy", 0, 3, -1, 2), ("cz", 1, 1, -1, 2), ("b", 1), ("cz", 1, 3, 1, 2), ("turn", 6),
    ("cy", 0, 3, 1, 2), ("cz", 1, 3, -1, 2), ("turn", 7), ("cz", 1, 2, 1, 2), ("a", 1), ("cz", 1, 2, -1, 2),
    ("lg", 1, "z", 2), ("cy", 0, 2, -1, 2), ("lg", 1, "z", 6), ("cz", 0, 2, 1, 3), ("lg", 0, "z", 5),
    ("cy", 0, 2, 1, 2), ("cz", 0, 2, -1, 3), ("cz", 0, 1, 1, 4), ("cz", 0, 1, -1, 4), ("lg", 0, "z", 3),
    ("cy", 1, 1, -1, 1), ("cz", 0, 3, -1, 4), ("lg", 0, "y", 2), ("cz", 0, 3, 1, 4), ("a", 0, 2),
    ("cy", 1, 1, 1, 1), ("cz", 1, 1, -1, 3), ("turn", 8), ("cz", 1, 1, 1, 3), ("b", 0, 2), ("cy", 1, 3, -1, 1),
    ("cz", 1, 3, -1, 3), ("lg", 0, "x"), ("cz", 1, 3, 1, 3), ("cy", 1, 3, 1, 1), ("cz", 1, 2, -1, 3),
    ("cz", 1, 2, 1, 3), ("a", 1, 2), ("lg", 1, "z", 3), ("cy", 1, 2, -1, 1), ("cz", 0, 2, 1, 4),
    ("cz", 0, 2, -1, 4), ("lg", 0, "z", 4), ("ls", 0), ("cy", 1, 2, 1, 1), ("b", 1, 2), ("cy", 1, 1, -1, 2),
    ("cz", 1, 1, -1, 4), ("cy", 1, 1, 1, 2), ("cz", 1, 1, 1, 4), ("cz", 1, 3, -1, 4), ("lg", 1, "z", 5),
    ("cy", 1, 3, -1, 2), ("lg", 1, "y", 1), ("cz", 1, 3, 1, 4), ("cz", 1, 2, -1, 4), ("lg", 1, "y", 3),
    ("cz", 1, 2, 1, 4), ("cy", 1, 3, 1, 2), ("lg", 1, "z", 4), ("cy", 1, 2, -1, 2), ("lg", 1, "x"), ("turn", 9),
    ("turn", 10), ("cy", 1, 2, 1, 2), ("lg", 1, "y", 2), ("ls", 1), ("turn", 11), ("sz", 0), ("turn", 12),
    ("turn", 13), ("turn", 14), ("turn", 15), ("sz", 1), ("sxy", 0), ("gb", 0, 0), ("gb", 0, 1), ("gb", 0, 2),
    ("gb", 0, 3), ("gb", 0, 4), ("gb", 0, 5), ("gb", 0, 6), ("gb", 0, 7), ("sxy", 1), ("gb", 1, 0),
    ("z1", 0, 1, 1, 0), ("z1", 0, -1, 1, 0), ("x1", 0, 1, 1, 0), ("gb", 1, 1), ("gb", 1, 2), ("x1", 0, 1, 1, 1),
    ("gb", 1, 3), ("x1", 0, 1, 1, 2), ("x1", 0, -1, 1, 0), ("gb", 1, 4), ("gb", 1, 5), ("x1", 0, 1, 1, 3),
    ("x1", 0, -1, 1, 1), ("y1", 0, 1, 1, 0), ("y1", 0, -1, 1, 0), ("gb", 1, 6), ("z1", 1, 1, 1, 0),
    ("z1", 1, -1, 1, 0), ("x1", 0, -1, 1, 2), ("gb", 1, 7), ("z1", 1, 1, 1, 1), ("z1", 1, -1, 1, 1),
    ("x1", 0, -1, 1, 3), ("y1", 0, 1, 1, 1), ("y1", 0, -1, 1, 1), ("head", 0), ("x1", 0, "fin", 0), ("head", 1),
    ("z1", 0, 1, 2, 0), ("z1", 0, -1, 2, 0), ("x1", 0, "fin", 1), ("x1", 1, 1, 1, 0), ("head", 2),
    ("z1", 1, 1, 2, 0), ("z1", 1, -1, 2, 0), ("y1", 0, "fin", 0), ("y1", 1, 1, 1, 0), ("x1", 0, "fin", 2),
    ("y1", 1, -1, 1, 0), ("y1", 1, 1, 1, 1), ("y1", 1, -1, 1, 1), ("y1", 1, 1, 1, 2), ("y1", 1, -1, 1, 2),
    ("y1", 1, 1, 1, 3), ("z1", 1, 1, 2, 1), ("z1", 1, -1, 2, 1), ("y1", 1, -1, 1, 3), ("x1", 1, -1, 1, 0),
    ("head", 3), ("x1", 0, "fin", 3), ("head", 4), ("z1", 0, 1, 3, 0), ("z1", 0, -1, 3, 0), ("y1", 0, "fin", 1),
    ("y1", 1, "fin", 0), ("head", 5), ("z1", 1, 1, 3, 0), ("z1", 1, -1, 3, 0), ("y1", 1, "fin", 1),
    ("y1", 1, "fin", 2), ("head", 6), ("z1", 1, 1, 3, 1), ("z1", 1, -1, 3, 1), ("y1", 1, "fin", 3),
    ("x1", 1, "fin", 0), ("head", 7), ("sum", 0), ("sum", 1), ("sum", 2), ("z1", 0, "fin", 0), ("x2", 0),
    ("y2", 0), ("sum", 3), ("z1", 1, "fin", 0), ("sum", 4), ("sum", 5), ("sum", 6), ("y2", 1), ("x2", 1),
    ("z1", 1, "fin", 1), ("sum", 7), ("z2", 0), ("x3", 0), ("y3", 0), ("y3", 1), ("z2", 1), ("x3", 1),
)
RANK = {key: i for i, key in enumerate(ORDER)}


def scratch():
    out = dict(
        hid=((CAP, D), BF16), gain=((EXITS, D), F32), n_all=((NX, CAP, D), BF16), w_all=((D, 2 * VW), BF16), w_t=((2 * VW, D), BF16),
        logit=((NX, CAP, 2 * VW), F32), dl=((NX, CAP, 2 * VW), BF16),
        s1=((2, NZ, 8, 128), F32), s2=((2, NX * NY, 8, 128), F32),
        st=((2, 3, 8, 128), F32), ids=((2, 8, 128), F32), loss=((2, 8, 128), F32), dn=((CAP, VW), F32),
        mine=((D, VW), F32), gs=((D, VW), BF16), gr=((D, VW), BF16),
    )
    for h in range(2):
        lx, lz, ly = [p[2] for p in PARTS[h]]
        out[f"ownz{h}"] = ((HALVES[h][1], WIDTHS[h][0]), BF16)
        out[f"owny{h}"] = ((HALVES[h][1], WIDTHS[h][1]), BF16)
        out[f"px{h}"] = ((NX, NZ, NY, 16, lx), BF16)
        out[f"pz{h}"] = ((NZ, NX, NY, 16, lz), BF16)
        out[f"py{h}"] = ((NY, NX, NZ, 16, ly), BF16)
        cx, cz, cy = CHAINS[h]
        out[f"ax{h}"] = ((2, cx, 4, NY // cx, 16, lx), BF16)
        out[f"bx{h}"] = ((2, cx, 1, NZ, NY // cx, 16, lx), BF16)
        out[f"az{h}"] = ((2, cz, 2, NY // cz, 16, lz), BF16)
        out[f"bz{h}"] = ((2, cz, 3, NX, NY // cz, 16, lz), BF16)
        out[f"ay{h}"] = ((2, cy, 2, NZ // cy, 16, ly), BF16)
        out[f"by{h}"] = ((2, cy, 1, NX, NZ // cy, 16, ly), BF16)
        out[f"cx{h}"] = ((NY - 1, NZ, 16, lx), BF16)
        if h not in Z_AT_ONCE:
            out[f"cz{h}"] = ((NY - 1, NX, 16, lz), BF16)
        out[f"cy{h}"] = ((NX - 1, NZ, 16, ly), BF16)
        out[f"ex{h}"] = ((NZ - 1, 16, lx), BF16)
        out[f"ez{h}"] = (((NX * NY if h in Z_AT_ONCE else NX) - 1, 16, lz), BF16)
        out[f"ey{h}"] = ((NZ - 1, 16, ly), BF16)
    return out


SCRATCH = scratch()


def kernel(hidden, gain_in, head, targets, exit_ids, counts, scale, loss_out, gw_out, gh_out, *refs):
    b = dict(zip(SCRATCH, refs))
    ssem, rsem, lsem = refs[len(SCRATCH) :]
    hid, gain, n_all, w_all, w_t = b["hid"], b["gain"], b["n_all"], b["w_all"], b["w_t"]
    logit, dl, s1, s2, st, ids = b["logit"], b["dl"], b["s1"], b["s2"], b["st"], b["ids"]
    dn, mine, gs, gr, loss_x = b["dn"], b["mine"], b["gs"], b["gr"], b["loss"]
    s = lax.axis_index("section")
    v = lax.axis_index("vocab")
    x, c = lax.div(s, 2), lax.rem(s, 2)
    z, y = lax.div(v, NY), lax.rem(v, NY)

    def dev(dx=0, dc=0, dz=0, dy=0):
        return (
            lax.rem(x + dx + NX, NX) * 2 + lax.rem(c + dc, 2),
            lax.rem(z + dz + NZ, NZ) * NY + lax.rem(y + dy + NY, NY),
        )

    slots = [0]
    pool = [None] * N_SEND
    count = [0]
    pending = {}
    outs = []
    cps = {}
    events = []

    def slot():
        slots[0] += 1
        return slots[0] - 1

    def send(src, dst, device, at_slot=None):
        at_slot = slot() if at_slot is None else at_slot
        i = count[0] % N_SEND
        count[0] += 1
        if pool[i] is not None:
            pool[i].wait_send()
        cp = pltpu.make_async_remote_copy(
            src_ref=src, dst_ref=dst, send_sem=ssem.at[i], recv_sem=rsem.at[at_slot],
            device_id=device, device_id_type=MESH,
        )
        cp.start()
        pool[i] = cp
        pending.setdefault(at_slot, []).append(cp)
        return at_slot

    def arrived(at_slot, ref):
        pltpu.make_async_copy(ref, ref, rsem.at[at_slot]).wait()
        del pending[at_slot]

    def at(key, fn, *args):
        events.append((RANK[key], lambda: fn(*args)))

    def run():
        assert len(events) == len(RANK)
        for t_, fn in sorted(events, key=lambda e: e[0]):
            fn()

    barrier = pltpu.get_barrier_semaphore()
    friends = [dict(dc=1)]
    friends += [dict(dx=i) for i in range(1, NX)] + [{a: i} for a in ("dy", "dz") for i in (1, -1)]
    for f in friends:
        pl.semaphore_signal(barrier, inc=1, device_id=dev(**f), device_id_type=MESH)
    own_w = pl.ds(pl.multiple_of(c * VW, VW), VW)
    loads = [
        pltpu.make_async_copy(hidden, hid, lsem.at[0]),
        pltpu.make_async_copy(gain_in, gain, lsem.at[1]),
        pltpu.make_async_copy(head, w_all.at[:, own_w], lsem.at[2]),
    ]
    for cp in loads:
        cp.start()

    diag = lax.broadcasted_iota(jnp.int32, (CAP, 128), 0) == lax.broadcasted_iota(
        jnp.int32, (CAP, 128), 1
    )
    lane = lax.broadcasted_iota(jnp.int32, (8, 128), 1)
    sub8 = lax.broadcasted_iota(jnp.int32, (8, 128), 0)
    flat = sub8 * 128 + lane
    upper = sub8 < 4

    def to_col(row):
        return jnp.sum(jnp.where(diag, jnp.broadcast_to(row, (CAP, 128)), 0.0), axis=1, keepdims=True)

    def to_row(col, r0):
        n = col.shape[0]
        return jnp.sum(
            jnp.where(diag[r0 : r0 + n], jnp.broadcast_to(col, (n, 128)), 0.0), axis=0, keepdims=True
        )

    def spread(slot, ref):
        def one(r, acc):
            for q in range(NX):
                acc = jnp.where(flat == q * 128 + r, ref[(q * 2 + c) * CAP + r], acc)
            return acc

        acc = lax.fori_loop(0, CAP, one, jnp.zeros((8, 128), jnp.int32), unroll=4)
        ids[slot] = acc.astype(F32)

    spread(0, exit_ids)
    own_exit = to_col(ids[0, pl.ds(x, 1), :])

    def gain_rows(cols, e):
        g = jnp.broadcast_to(gain[0:1, cols], (CAP, cols.size))
        for i in range(1, EXITS):
            g = jnp.where(e == float(i), gain[i : i + 1, cols], g)
        return g

    def squares(i, acc):
        xs = hid[:, pl.ds(pl.multiple_of(i * 512, 512), 512)].astype(F32)
        xs = xs * xs
        for j in range(4):
            acc = acc + xs[:, j * 128 : (j + 1) * 128]
        return acc

    loads[0].wait()
    total_sq = lax.fori_loop(0, D // 512, squares, jnp.zeros((CAP, 128), F32))
    rinv = lax.rsqrt(jnp.sum(total_sq, axis=1, keepdims=True) / D + 1e-05)

    def norm_chunk(i, carry):
        cols = pl.ds(pl.multiple_of(i * 512, 512), 512)
        xs = hid[:, cols].astype(F32)
        n_all[0, :, cols] = (xs * rinv * gain_rows(cols, own_exit)).astype(BF16)
        return carry

    loads[1].wait()

    def columns(h, tag, d=0):
        zw, yw, bw, aw = WIDTHS[h]
        if tag == "z":
            return pl.ds(pl.multiple_of(lax.rem(z + d + NZ, NZ) * zw, 128), zw)
        if tag == "y":
            return pl.ds(pl.multiple_of(NZ * zw + lax.rem(y + d + NY, NY) * yw, 128), yw)
        return pl.ds(D - aw - bw, bw) if tag == "b" else pl.ds(D - aw, aw)

    def own_x(tag, h):
        rows, cols, far = pl.ds(*HALVES[h][:2]), columns(h, tag), tag in "zy"
        src = b[f"own{tag}{h}"] if far else n_all.at[0, rows, cols]
        k = slot()
        send(src, n_all.at[3, rows, cols], dev(dx=1), k)
        send(src, n_all.at[1, rows, cols], dev(dx=-1), k)
        if far:
            send(src, n_all.at[2, rows, cols], dev(dx=2), k)
        cps[tag, h] = k, n_all.at[0 : 3 if far else 2, rows, cols]

    def chain(tag, h, n, axis, rel):
        half = n // 2
        r0, n_rows, n_low = HALVES[h]
        full, low, high = pl.ds(r0, n_rows), pl.ds(r0, n_low), pl.ds(r0 + n_low, n_rows - n_low)

        def begin():
            for sign in (1, -1):
                ref = n_all.at[rel, full, columns(h, tag)]
                cps[tag, h, rel, sign, 1] = send(ref, ref, dev(**{axis: sign})), ref

        def arrive(sign, k):
            arrived(*cps[tag, h, rel, sign, k])
            if k < half:
                rows = full if k < half - 1 else (low if sign == 1 else high)
                ref = n_all.at[rel, rows, columns(h, tag, -sign * k)]
                cps[tag, h, rel, sign, k + 1] = send(ref, ref, dev(**{axis: sign})), ref

        for k in range(1, half + 1):
            for sign in (1, -1):
                at(("c" + tag, h, rel, sign, k), arrive, sign, k)
        return begin

    def gather(h):
        def got(tag, then):
            arrived(*cps[tag, h])
            for fn in then:
                fn()

        def got_x(tag):
            arrived(*cps[tag, h])
            rows, cols = pl.ds(*HALVES[h][:2]), columns(h, tag)
            rel, dx = (1, -1) if tag == "b" else (3, 1)
            dst = n_all.at[2, rows, cols]
            cps[tag, h, 2] = send(n_all.at[rel, rows, cols], dst, dev(dx=dx)), dst

        for tag, n, axis in (("z", NZ, "dz"), ("y", NY, "dy")):
            more = [lambda k=k: own_x(*k) for k in AFTER.get((tag, h), ())]
            at((tag, h), got, tag, [chain(tag, h, n, axis, rel) for rel in (1, 3, 2)] + more)
            for d in range(n):
                at(("lg", h, tag, d), logits, h, tag, d)
        for tag in "ba":
            at((tag, h), got_x, tag)
            at((tag, h, 2), lambda tag=tag: arrived(*cps[tag, h, 2]))
        at(("lg", h, "x"), logits, h, "x", 0)

    def logits(h, tag, d):
        r0, n_rows, _ = HALVES[h]
        first = D - sum(WIDTHS[h][2:])
        k = pl.ds(first, D - first) if tag == "x" else columns(h, tag, d)
        n = n_all[:, r0 : r0 + n_rows, k].reshape(NX * n_rows, k.size)
        part = jnp.dot(n, w_all[k, :], preferred_element_type=F32)
        logit[:, r0 : r0 + n_rows, :] += part.reshape(NX, n_rows, 2 * VW)

    def take_w():
        arrived(*cps["w"])
        logit[...] = jnp.zeros_like(logit)

    def turn_w(i):
        f = pl.ds(i * 512, 512)
        w_t[:, f] = jnp.transpose(w_all[f, :], (1, 0))

    def own_first(tag, h):
        (r0, n, _), cols = HALVES[h], columns(h, tag)
        rows = pl.ds(r0, n)
        xs = hid[rows, cols].astype(F32)
        g = jnp.broadcast_to(gain[0:1, cols], xs.shape)
        for i in range(1, EXITS):
            g = jnp.where(own_exit[r0 : r0 + n] == float(i), gain[i : i + 1, cols], g)
        b[f"own{tag}{h}"][...] = (xs * rinv[r0 : r0 + n] * g).astype(BF16)

    for h in range(2):
        for tag in "zy":
            own_first(tag, h)
    pl.semaphore_wait(barrier, len(friends))
    for tag, h in FIRST:
        own_x(tag, h)
    lax.fori_loop(0, D // 512, norm_chunk, 0)
    for h in range(2):
        gather(h)
    loads[2].wait()
    mine_w = w_all.at[:, own_w]
    cps["w"] = send(mine_w, mine_w, dev(dc=1)), mine_w
    at(("w",), take_w)
    for i in range(16):
        at(("turn", i), turn_w, i)

    def weights():
        spread(1, targets)
        weight = jnp.zeros((8, 128), F32)
        exits = ids[0]
        for i in range(EXITS):
            weight = jnp.where(exits == float(i), scale[i], weight)
        for q in range(NX):
            weight = jnp.where((sub8 == q) & (lane >= counts[q * 2 + c]), 0.0, weight)
        for h in range(2):
            r0, n_rows, _ = HALVES[h]
            st[h, 1] = jnp.where((sub8 < NX) & (lane >= r0) & (lane < r0 + n_rows), weight, 0.0)

    weights()

    entry = lax.broadcasted_iota(jnp.int32, (CAP, 2 * VW), 1)
    base = (x * 2 * NZ * NY + v) * VW
    entry = jnp.where(entry < VW, entry + base, entry + (base + (NZ * NY - 1) * VW)).astype(F32)

    def column(ref, rel, r0, n):
        return to_col(ref[pl.ds(lax.rem(x + rel, NX), 1), :])[r0 : r0 + n]

    def local_stats(h):
        r0, n, _ = HALVES[h]
        stats = [jnp.zeros((8, 128), F32)] * 4
        for rel in range(NX):
            l = logit[rel, r0 : r0 + n, :]
            hit = entry[:n] == column(ids.at[1], rel, r0, n)
            m = jnp.max(l, axis=1, keepdims=True)
            e = jnp.exp(l - m)
            values = (
                m,
                jnp.sum(e, axis=1, keepdims=True),
                jnp.sum(e * l, axis=1, keepdims=True),
                jnp.sum(jnp.where(hit, l, 0.0), axis=1, keepdims=True),
            )
            here = sub8 == lax.rem(x + rel, NX)
            for i in range(4):
                row = jnp.broadcast_to(to_row(values[i], r0), (8, 128))
                stats[i] = jnp.where(here, row, stats[i])
        first = jnp.where(upper, stats[0], pltpu.roll(stats[1], 4, 0))
        rest = jnp.where(upper, stats[2], pltpu.roll(stats[3], 4, 0))
        s1[h, z] = jnp.where(mine_lanes(h), first, pltpu.roll(rest, 64, 1))
        cps["s1", h] = slot()
        for i in range(1, NZ):
            send(s1.at[h, z], s1.at[h, z], dev(dz=i), cps["s1", h])

    def mine_lanes(h):
        r0, n, _ = HALVES[h]
        return (lane >= r0) & (lane < r0 + n)

    def merge(h, ref, n):
        own_lanes = mine_lanes(h)
        sets = [ref[q] for q in range(n)]
        peaks = [jnp.where(upper, a, pltpu.roll(a, 4, 0)) for a in sets]
        peak = peaks[0]
        for p in peaks[1:]:
            peak = jnp.maximum(peak, p)
        total = jnp.zeros((8, 128), F32)
        for a, p in zip(sets, peaks):
            f = jnp.exp(p - peak)
            total = total + a * jnp.where(own_lanes, f, jnp.where(upper, pltpu.roll(f, 64, 1), 1.0))
        return jnp.where(own_lanes & upper, peak, total)

    own = x * NY + y

    def stats_z(h):
        arrived(cps["s1", h], s1.at[h, 0 : NZ - 1])
        s2[h, own] = merge(h, s1.at[h], NZ)
        cps["s2", h] = slot()
        for i in range(NX):
            for j in range(NY):
                if i or j:
                    send(s2.at[h, own], s2.at[h, own], dev(dx=i, dy=j), cps["s2", h])

    losses = []

    def stats_xy(h):
        arrived(cps["s2", h], s2.at[h, 0 : NX * NY - 1])
        peak = merge(h, s2.at[h], NX * NY)
        mean = pltpu.roll(peak, 64, 1)
        total, chosen = pltpu.roll(peak, 4, 0), pltpu.roll(mean, 4, 0)
        lse = peak + jnp.log(total)
        weight = st[h, 1]
        live = weight != 0.0
        st[h, 0] = lse
        st[h, 2] = jnp.where(live, weight * (mean / total - chosen), 0.0)
        losses.append(jnp.where(live, weight * (lse - chosen), 0.0))
        if h == 1:
            own_loss = losses[0] + losses[1]
            own_loss = jnp.sum(jnp.sum(own_loss, axis=1, keepdims=True), axis=0, keepdims=True)
            loss_x[0] = jnp.broadcast_to(own_loss, (8, 128))
            cps["loss"] = send(loss_x.at[0], loss_x.at[1], dev(dc=1))
        r0, n, _ = HALVES[h]
        for rel in range(NX):
            lse_c, w_c = column(st.at[h, 0], rel, r0, n), column(st.at[h, 1], rel, r0, n)
            hit = jnp.where(entry[:n] == column(ids.at[1], rel, r0, n), 1.0, 0.0)
            p = jnp.exp(logit[rel, r0 : r0 + n, :] - lse_c)
            dl[rel, r0 : r0 + n, :] = (w_c * (p - hit)).astype(BF16)

    def grad_block(h, k, *then):
        r0, n, _ = HALVES[h]
        zz = lax.rem(z + ZORD[k], NZ)
        rows = dl[:, r0 : r0 + n, :].reshape(NX * n, 2 * VW)
        f = pl.ds(pl.multiple_of(zz * NY * VW, NY * VW), NY * VW)
        out = jnp.dot(rows, w_t[:, f], preferred_element_type=F32).astype(BF16)
        for yy in range(NY):
            ry = lax.rem(yy - y + NY, NY)
            for rx in range(NX):
                block = out[rx * n : (rx + 1) * n, yy * VW : (yy + 1) * VW]
                cut = [block[p[0] - r0 : p[0] - r0 + 16, p[1] : p[1] + p[2]] for p in PARTS[h]]
                b[f"px{h}"][rx, k, ry] = cut[0]
                b[f"pz{h}"][k, rx, ry] = cut[1]
                b[f"py{h}"][ry, rx, k] = cut[2]
        for fn in then:
            fn()

    def add_into(dst, srcs):
        def one(i, carry):
            acc = dst[i].astype(F32)
            for r in srcs:
                acc = acc + r[i].astype(F32)
            dst[i] = acc.astype(BF16)
            return carry

        lax.fori_loop(0, dst.shape[0], one, 0)

    def ring(tag, h, n, axis, n_chains, block, one_way, buf_a, buf_b, done):
        half = n // 2
        side = {1: 0, -1: 1}
        left = [n_chains]

        def begin(sign):
            for i in range(n_chains):
                src = one_way(block(half, i), sign)
                cps[tag, h, sign, 1, i] = send(src, buf_a.at[side[sign], i], dev(**{axis: sign}))

        def arrive(sign, k, i):
            arrived(cps[tag, h, sign, k, i], buf_a.at[side[sign], i] if k == 1 else buf_b.at[side[sign], i, k - 2])
            d = (sign * (half - k)) % n
            if k == 1:
                add_into(one_way(block(d, i), sign), [buf_a.at[side[sign], i]])
            else:
                add_into(block(d, i), [buf_b.at[side[sign], i, k - 2]])
            cps[tag, h, sign, k + 1, i] = send(
                block(d, i), buf_b.at[side[sign], i, k - 1], dev(**{axis: sign})
            )

        def finish(i):
            for sign in (1, -1):
                arrived(cps[tag, h, sign, half, i], buf_b.at[side[sign], i, half - 2])
            add_into(block(0, i), [buf_b.at[side[sign], i, half - 2] for sign in (1, -1)])
            left[0] -= 1
            if left[0] == 0:
                done()

        for k in range(1, half):
            for i in range(n_chains):
                for sign in (1, -1):
                    at((tag, h, sign, k, i), arrive, sign, k, i)
        for i in range(n_chains):
            at((tag, h, "fin", i), finish, i)
        return begin

    def direct(tag, h, n, axis, block, buf, done):
        def begin():
            cps[tag, h] = slot()
            for d in range(1, n):
                send(block(d), buf.at[d - 1], dev(**{axis: d}), cps[tag, h])

        def finish():
            arrived(cps[tag, h], buf)
            acc = block(0)[...].astype(F32)
            for d in range(1, n):
                acc = acc + buf[d - 1].astype(F32)
            done(acc)

        at((tag, h), finish)
        return begin

    def direct2(tag, h, axes, sizes, block, buf, done):
        pairs = [(i, j) for i in range(sizes[0]) for j in range(sizes[1]) if i or j]

        def begin():
            cps[tag, h] = slot()
            for q, (i, j) in enumerate(pairs):
                send(block(i, j), buf.at[q], dev(**{axes[0]: i, axes[1]: j}), cps[tag, h])

        def finish():
            arrived(cps[tag, h], buf)
            acc = block(0, 0)[...].astype(F32)
            for q in range(len(pairs)):
                acc = acc + buf[q].astype(F32)
            done(acc)

        at((tag, h), finish)
        return begin

    def reduce(h):
        px, pz, py = b[f"px{h}"], b[f"pz{h}"], b[f"py{h}"]
        cx, cz, cy = CHAINS[h]

        def put(i):
            r, l, w = PARTS[h][i]
            def fn(acc):
                dn[r : r + 16, l : l + w] = acc
            return fn

        def back(ref, begin):
            def fn(acc):
                ref[...] = acc.astype(BF16)
                begin()
            return fn

        def cut(m):
            return lambda r, sign: r.at[0:m] if sign == 1 else r.at[m : 2 * m]

        x3 = direct("x3", h, NZ, "dz", lambda d: px.at[0, ZPOS[d], 0], b[f"ex{h}"], put(0))
        x2 = direct("x2", h, NY, "dy", lambda d: px.at[0, :, d], b[f"cx{h}"], back(px.at[0, :, 0], x3))
        x1 = ring("x1", h, NX, "dx", cx, lambda d, i: px.at[d, :, i * NY // cx : (i + 1) * NY // cx], cut(4),
                  b[f"ax{h}"], b[f"bx{h}"], x2)
        if h in Z_AT_ONCE:
            z2 = direct2("z2", h, ("dy", "dx"), (NY, NX), lambda i, j: pz.at[7, j, i], b[f"ez{h}"], put(1))
        else:
            z3 = direct("z3", h, NX, "dx", lambda d: pz.at[7, d, 0], b[f"ez{h}"], put(1))
            z2 = direct("z2", h, NY, "dy", lambda d: pz.at[7, :, d], b[f"cz{h}"], back(pz.at[7, :, 0], z3))
        z1 = ring("z1", h, NZ, "dz", cz, lambda d, i: pz.at[ZPOS[d], :, i * NY // cz : (i + 1) * NY // cz], cut(2),
                  b[f"az{h}"], b[f"bz{h}"], z2)
        y3 = direct("y3", h, NZ, "dz", lambda d: py.at[0, 0, ZPOS[d]], b[f"ey{h}"], put(2))
        y2 = direct("y2", h, NX, "dx", lambda d: py.at[0, d], b[f"cy{h}"], back(py.at[0, 0], y3))
        y1 = ring("y1", h, NY, "dy", cy, lambda d, i: py.at[d, :, i * NZ // cy : (i + 1) * NZ // cy], cut(2),
                  b[f"ay{h}"], b[f"by{h}"], y2)
        then = {
            0: (lambda: z1(1), lambda: z1(-1)),
            3: (lambda: x1(1),),
            7: (lambda: x1(-1), lambda: y1(1), lambda: y1(-1)),
        }
        for k in range(NZ):
            at(("gb", h, k), grad_block, h, k, *then.get(k, ()))

    def head_chunk(j):
        f = pl.ds(j * 1024, 1024)
        n = n_all[:, :, f].reshape(ROWS, 1024)
        both = lax.dot_general(n, dl[...].reshape(ROWS, 2 * VW), TN, preferred_element_type=F32)
        first, second = both[:, :VW], both[:, VW:]
        mine[f, :] = jnp.where(c == 0, first, second)
        gs[f, :] = jnp.where(c == 0, second, first).astype(BF16)
        cps["g", j] = send(gs.at[f], gr.at[f], dev(dc=1))

    def head_sum(j):
        arrived(cps["g", j], gr.at[pl.ds(j * 1024, 1024)])

        def one(i, carry):
            f = pl.ds(pl.multiple_of(j * 1024 + i * 256, 256), 256)
            gr[f, :] = (mine[f, :] + gr[f, :].astype(F32)).astype(BF16)
            return carry

        lax.fori_loop(0, 4, one, 0)
        f = pl.ds(j * 1024, 1024)
        cp = pltpu.make_async_copy(gr.at[f], gw_out.at[f], lsem.at[3 + j])
        cp.start()
        outs.append(cp)

    for h in range(2):
        at(("ls", h), local_stats, h)
        at(("sz", h), stats_z, h)
        at(("sxy", h), stats_xy, h)
        reduce(h)
    for j in range(8):
        at(("head", j), head_chunk, j)
        at(("sum", j), head_sum, j)
    run()

    f = pl.ds(pl.multiple_of(v * VW, VW), VW)
    inner = to_col(st[0, 2, pl.ds(x, 1), :] + st[1, 2, pl.ds(x, 1), :])
    unit = hid[:, f].astype(F32) * rinv
    scaled = gain_rows(f, own_exit) * dn[...]
    gh_out[...] = (rinv * (scaled - unit * (inner / D))).astype(BF16)

    arrived(cps["loss"], loss_x.at[1])
    loss_out[...] = (loss_x[0] + loss_x[1]) / 512.0
    for cp in outs:
        cp.wait()
    for cp in pool:
        if cp is not None:
            cp.wait_send()
    assert not pending and slots[0] <= N_RECV, slots


def handover(loss, grad_weight, grad_hidden, loss_out, gw_out, gh_out, buf, small, total, sem):
    n = D // 4
    parts = [pl.ds(i * n, n) for i in range(4)]
    reads = [pltpu.make_async_copy(grad_weight.at[p], buf.at[p], sem.at[i]) for i, p in enumerate(parts)]
    writes = [pltpu.make_async_copy(buf.at[p], gw_out.at[p], sem.at[4 + i]) for i, p in enumerate(parts)]
    reads += [pltpu.make_async_copy(grad_hidden, small, sem.at[8])]
    writes += [pltpu.make_async_copy(small, gh_out, sem.at[9])]
    get_loss = pltpu.make_async_copy(loss, total, sem.at[10])
    for r in reads:
        r.start()
    get_loss.start()
    for r, w in zip(reads, writes):
        r.wait()
        w.start()
    get_loss.wait()
    loss_out[...] = total[0:1, 0:1]
    for w in writes:
        w.wait()


def body(hidden, gain, exit_scale, head_weight, targets, exit_ids, counts):
    vmem = pl.BlockSpec(memory_space=pltpu.VMEM)
    smem = pl.BlockSpec(memory_space=pltpu.SMEM)
    hbm = pl.BlockSpec(memory_space=pl.ANY)
    dma = pltpu.SemaphoreType.DMA
    big = jax.ShapeDtypeStruct((D, VW), BF16)
    small = jax.ShapeDtypeStruct((CAP, VW), BF16)
    results = pl.pallas_call(
        kernel,
        out_shape=(jax.ShapeDtypeStruct((8, 128), F32), big, small),
        in_specs=[hbm, hbm, hbm, smem, smem, smem, smem],
        out_specs=(vmem, hbm, vmem),
        scratch_shapes=[pltpu.VMEM(*v) for v in SCRATCH.values()] + [dma((N_SEND,)), dma((N_RECV,)), dma((11,))],
        compiler_params=pltpu.CompilerParams(
            collective_id=0, has_side_effects=True, vmem_limit_bytes=60 * 2**20
        ),
        name="exit_head",
    )(hidden, gain, head_weight, targets, exit_ids, counts, exit_scale)
    loss, grad_weight, grad_hidden = pl.pallas_call(
        handover,
        out_shape=(jax.ShapeDtypeStruct((1, 1), F32), big, small),
        in_specs=[hbm, hbm, hbm],
        out_specs=(vmem, hbm, hbm),
        scratch_shapes=[
            pltpu.VMEM((D, VW), BF16), pltpu.VMEM((CAP, VW), BF16), pltpu.VMEM((8, 128), F32), dma((11,)),
        ],
        compiler_params=pltpu.CompilerParams(vmem_limit_bytes=58 * 2**20),
        name="handover",
    )(*results)
    return (loss.reshape(()), grad_weight, grad_hidden)


def solution(mesh):
    in_specs = (P("section", None), P(), P(), P(None, ("section", "vocab")), P(), P(), P())
    out_specs = (P(), P(None, ("section", "vocab")), P("section", "vocab"))
    return jax.shard_map(body, mesh=mesh, in_specs=in_specs, out_specs=out_specs, check_vma=False)
```

```python
import jax
import jax.numpy as jnp
from jax import lax
from jax.experimental import pallas as pl
from jax.experimental.pallas import tpu as pltpu
from jax.sharding import PartitionSpec as P

MESH = pl.DeviceIdType.MESH
NX, NZ, NY = 4, 8, 4
CAP = 80
D = 8192
VW = 256
ROWS = NX * CAP
EXITS = 4
F32 = jnp.float32
BF16 = jnp.bfloat16
def widths(zw, yw, bw):
    return zw, yw, bw, D - NZ * zw - NY * yw - bw


WIDTHS = (widths(384, 768, 1152), widths(384, 768, 1408))
ZORD = (4, 3, 5, 2, 6, 1, 7, 0)
ZPOS = {d: k for k, d in enumerate(ZORD)}
N_SEND = 40
N_RECV = 180
HALVES = ((0, 48, 32), (48, 32, 16))
PARTS = (((0, 0, 256), (16, 0, 256), (32, 0, 256)), ((48, 0, 128), (64, 0, 256), (48, 128, 128)))
FIRST = (('z', 0), ('y', 0), ('z', 1))
AFTER = {('z', 0): (('b', 0), ('a', 0)), ('y', 0): (('y', 1), ('b', 1), ('a', 1))}
CHAINS = ((4, 1, 2), (1, 2, 4))
Z_AT_ONCE = (0, 1)
TN = (((0,), (0,)), ((), ()))
ORDER = (
    ("z", 0), ("z", 0, "far"), ("y", 0), ("cz", 0, 1, 1, 1), ("cz", 0, 1, -1, 1), ("cz", 0, 3, 1, 1),
    ("cz", 0, 3, -1, 1), ("z", 1), ("y", 0, "far"), ("cz", 0, 2, 1, 1), ("cz", 0, 2, -1, 1), ("w",),
    ("z", 1, "far"), ("lg", 0, "z", 0), ("lg", 0, "z", 1), ("cz", 0, 1, 1, 2), ("cz", 0, 1, -1, 2),
    ("cy", 0, 1, 1, 1), ("cy", 0, 1, -1, 1), ("lg", 0, "z", 7), ("lg", 0, "y", 0), ("cz", 0, 3, 1, 2),
    ("cz", 0, 3, -1, 2), ("lg", 1, "z", 0), ("b", 0), ("cz", 1, 1, 1, 1), ("cz", 1, 1, -1, 1), ("turn", 0),
    ("cy", 0, 3, 1, 1), ("cy", 0, 3, -1, 1), ("turn", 1), ("cz", 1, 3, 1, 1), ("cz", 1, 3, -1, 1), ("turn", 2),
    ("cz", 0, 2, 1, 2), ("cz", 0, 2, -1, 2), ("lg", 0, "z", 2), ("lg", 0, "z", 6), ("a", 0), ("cz", 1, 2, 1, 1),
    ("cz", 1, 2, -1, 1), ("cy", 0, 2, 1, 1), ("cy", 0, 2, -1, 1), ("lg", 0, "y", 1), ("cy", 0, 1, -1, 2),
    ("cz", 0, 1, 1, 3), ("cz", 0, 1, -1, 3), ("lg", 0, "y", 3), ("y", 1), ("cy", 0, 1, 1, 2), ("lg", 1, "z", 1),
    ("cy", 0, 3, -1, 2), ("cz", 0, 3, 1, 3), ("cz", 0, 3, -1, 3), ("lg", 1, "z", 7), ("turn", 3),
    ("cz", 1, 1, 1, 2), ("cz", 1, 1, -1, 2), ("cy", 0, 3, 1, 2), ("y", 1, "far"), ("lg", 1, "y", 0),
    ("cz", 1, 3, 1, 2), ("cz", 1, 3, -1, 2), ("turn", 4), ("cy", 0, 2, -1, 2), ("cz", 0, 2, 1, 3),
    ("cz", 0, 2, -1, 3), ("lg", 0, "z", 3), ("cy", 0, 2, 1, 2), ("lg", 0, "z", 5), ("b", 1), ("cz", 1, 2, 1, 2),
    ("cz", 1, 2, -1, 2), ("cz", 0, 1, -1, 4), ("lg", 0, "y", 2), ("cz", 0, 1, 1, 4), ("cz", 0, 3, -1, 4),
    ("cy", 1, 1, 1, 1), ("cy", 1, 1, -1, 1), ("a", 1), ("lg", 1, "z", 2), ("cz", 0, 3, 1, 4), ("lg", 1, "z", 6),
    ("cz", 1, 1, -1, 3), ("cz", 1, 1, 1, 3), ("turn", 5), ("cy", 1, 3, 1, 1), ("cy", 1, 3, -1, 1),
    ("cz", 1, 3, -1, 3), ("turn", 6), ("cz", 1, 3, 1, 3), ("cz", 0, 2, -1, 4), ("turn", 7), ("cz", 0, 2, 1, 4),
    ("a", 0, 2), ("cy", 1, 2, 1, 1), ("cy", 1, 2, -1, 1), ("lg", 0, "z", 4), ("cz", 1, 2, -1, 3),
    ("cz", 1, 2, 1, 3), ("b", 0, 2), ("lg", 0, "x"), ("ls", 0), ("cy", 1, 1, 1, 2), ("cy", 1, 1, -1, 2),
    ("a", 1, 2), ("cz", 1, 1, -1, 4), ("cz", 1, 1, 1, 4), ("cz", 1, 3, -1, 4), ("cy", 1, 3, 1, 2),
    ("cy", 1, 3, -1, 2), ("cz", 1, 3, 1, 4), ("b", 1, 2), ("lg", 1, "z", 3), ("lg", 1, "z", 5),
    ("cy", 1, 2, 1, 2), ("cy", 1, 2, -1, 2), ("lg", 1, "y", 1), ("cz", 1, 2, -1, 4), ("cz", 1, 2, 1, 4),
    ("lg", 1, "z", 4), ("lg", 1, "y", 2), ("lg", 1, "y", 3), ("lg", 1, "x"), ("ls", 1), ("sz", 0), ("turn", 8),
    ("turn", 9), ("turn", 10), ("turn", 11), ("turn", 12), ("turn", 13), ("turn", 14), ("turn", 15), ("sz", 1),
    ("sxy", 0), ("gb", 0, 0), ("gb", 0, 1), ("gb", 0, 2), ("gb", 0, 3), ("gb", 0, 4), ("gb", 0, 5),
    ("gb", 0, 6), ("gb", 0, 7), ("sxy", 1), ("gb", 1, 0), ("z1", 0, 1, 1, 0), ("z1", 0, -1, 1, 0),
    ("x1", 0, 1, 1, 0), ("gb", 1, 1), ("gb", 1, 2), ("x1", 0, 1, 1, 1), ("gb", 1, 3), ("gb", 1, 4),
    ("x1", 0, 1, 1, 2), ("x1", 0, -1, 1, 0), ("gb", 1, 5), ("x1", 0, 1, 1, 3), ("x1", 0, -1, 1, 1),
    ("y1", 0, 1, 1, 0), ("y1", 0, -1, 1, 0), ("gb", 1, 6), ("z1", 1, 1, 1, 0), ("z1", 1, -1, 1, 0),
    ("x1", 0, -1, 1, 2), ("gb", 1, 7), ("z1", 1, 1, 1, 1), ("z1", 1, -1, 1, 1), ("x1", 0, -1, 1, 3),
    ("y1", 0, 1, 1, 1), ("y1", 0, -1, 1, 1), ("head", 0), ("head", 1), ("x1", 0, "fin", 0), ("z1", 0, 1, 2, 0),
    ("z1", 0, -1, 2, 0), ("x1", 1, 1, 1, 0), ("x1", 0, "fin", 1), ("head", 2), ("z1", 1, 1, 2, 0),
    ("z1", 1, -1, 2, 0), ("y1", 0, "fin", 0), ("y1", 1, 1, 1, 0), ("y1", 1, -1, 1, 0), ("x1", 0, "fin", 2),
    ("y1", 1, 1, 1, 1), ("y1", 1, -1, 1, 1), ("y1", 1, 1, 1, 2), ("y1", 1, -1, 1, 2), ("y1", 1, 1, 1, 3),
    ("z1", 1, 1, 2, 1), ("z1", 1, -1, 2, 1), ("y1", 1, -1, 1, 3), ("x1", 1, -1, 1, 0), ("head", 3), ("head", 4),
    ("x1", 0, "fin", 3), ("z1", 0, 1, 3, 0), ("z1", 0, -1, 3, 0), ("y1", 0, "fin", 1), ("y1", 1, "fin", 0),
    ("head", 5), ("z1", 1, 1, 3, 0), ("z1", 1, -1, 3, 0), ("y1", 1, "fin", 1), ("y1", 1, "fin", 2), ("head", 6),
    ("z1", 1, 1, 3, 1), ("z1", 1, -1, 3, 1), ("y1", 1, "fin", 3), ("x1", 1, "fin", 0), ("head", 7), ("sum", 0),
    ("sum", 1), ("sum", 2), ("z1", 0, "fin", 0), ("x2", 0), ("y2", 0), ("sum", 3), ("z1", 1, "fin", 0),
    ("sum", 4), ("sum", 5), ("sum", 6), ("y2", 1), ("x2", 1), ("z1", 1, "fin", 1), ("sum", 7), ("z2", 0),
    ("x3", 0), ("y3", 0), ("y3", 1), ("z2", 1), ("x3", 1),
)
RANK = {key: i for i, key in enumerate(ORDER)}


def scratch():
    out = dict(
        hid=((CAP, D), BF16), gain=((EXITS, D), F32), n_all=((NX, CAP, D), BF16), w_all=((D, 2 * VW), BF16), w_t=((2 * VW, D), BF16),
        logit=((NX, CAP, 2 * VW), F32), dl=((NX, CAP, 2 * VW), BF16),
        s1=((2, NZ, 8, 128), F32), s2=((2, NX * NY, 8, 128), F32),
        st=((2, 3, 8, 128), F32), ids=((2, 8, 128), F32), loss=((2, 8, 128), F32), dn=((CAP, VW), F32),
        mine=((D, VW), F32), gs=((D, VW), BF16), gr=((D, VW), BF16),
    )
    for h in range(2):
        lx, lz, ly = [p[2] for p in PARTS[h]]
        out[f"ownz{h}"] = ((HALVES[h][1], WIDTHS[h][0]), BF16)
        out[f"owny{h}"] = ((HALVES[h][1], WIDTHS[h][1]), BF16)
        out[f"px{h}"] = ((NX, NZ, NY, 16, lx), BF16)
        out[f"pz{h}"] = ((NZ, NX, NY, 16, lz), BF16)
        out[f"py{h}"] = ((NY, NX, NZ, 16, ly), BF16)
        cx, cz, cy = CHAINS[h]
        out[f"ax{h}"] = ((2, cx, 4, NY // cx, 16, lx), BF16)
        out[f"bx{h}"] = ((2, cx, 1, NZ, NY // cx, 16, lx), BF16)
        out[f"az{h}"] = ((2, cz, 2, NY // cz, 16, lz), BF16)
        out[f"bz{h}"] = ((2, cz, 3, NX, NY // cz, 16, lz), BF16)
        out[f"ay{h}"] = ((2, cy, 2, NZ // cy, 16, ly), BF16)
        out[f"by{h}"] = ((2, cy, 1, NX, NZ // cy, 16, ly), BF16)
        out[f"cx{h}"] = ((NY - 1, NZ, 16, lx), BF16)
        if h not in Z_AT_ONCE:
            out[f"cz{h}"] = ((NY - 1, NX, 16, lz), BF16)
        out[f"cy{h}"] = ((NX - 1, NZ, 16, ly), BF16)
        out[f"ex{h}"] = ((NZ - 1, 16, lx), BF16)
        out[f"ez{h}"] = (((NX * NY if h in Z_AT_ONCE else NX) - 1, 16, lz), BF16)
        out[f"ey{h}"] = ((NZ - 1, 16, ly), BF16)
    return out


SCRATCH = scratch()


def kernel(hidden, gain_in, head, targets, exit_ids, counts, scale, loss_out, gw_out, gh_out, *refs):
    b = dict(zip(SCRATCH, refs))
    ssem, rsem, lsem = refs[len(SCRATCH) :]
    hid, gain, n_all, w_all, w_t = b["hid"], b["gain"], b["n_all"], b["w_all"], b["w_t"]
    logit, dl, s1, s2, st, ids = b["logit"], b["dl"], b["s1"], b["s2"], b["st"], b["ids"]
    dn, mine, gs, gr, loss_x = b["dn"], b["mine"], b["gs"], b["gr"], b["loss"]
    s = lax.axis_index("section")
    v = lax.axis_index("vocab")
    x, c = lax.div(s, 2), lax.rem(s, 2)
    z, y = lax.div(v, NY), lax.rem(v, NY)

    def dev(dx=0, dc=0, dz=0, dy=0):
        return (
            lax.rem(x + dx + NX, NX) * 2 + lax.rem(c + dc, 2),
            lax.rem(z + dz + NZ, NZ) * NY + lax.rem(y + dy + NY, NY),
        )

    slots = [0]
    pool = [None] * N_SEND
    count = [0]
    pending = {}
    outs = []
    cps = {}
    events = []

    def slot():
        slots[0] += 1
        return slots[0] - 1

    def send(src, dst, device, at_slot=None):
        at_slot = slot() if at_slot is None else at_slot
        i = count[0] % N_SEND
        count[0] += 1
        if pool[i] is not None:
            pool[i].wait_send()
        cp = pltpu.make_async_remote_copy(
            src_ref=src, dst_ref=dst, send_sem=ssem.at[i], recv_sem=rsem.at[at_slot],
            device_id=device, device_id_type=MESH,
        )
        cp.start()
        pool[i] = cp
        pending.setdefault(at_slot, []).append(cp)
        return at_slot

    def arrived(at_slot, ref):
        pltpu.make_async_copy(ref, ref, rsem.at[at_slot]).wait()
        del pending[at_slot]

    def at(key, fn, *args):
        events.append((RANK[key], lambda: fn(*args)))

    def run():
        assert len(events) == len(RANK)
        for t_, fn in sorted(events, key=lambda e: e[0]):
            fn()

    barrier = pltpu.get_barrier_semaphore()
    friends = [dict(dc=1)]
    friends += [dict(dx=i) for i in range(1, NX)] + [{a: i} for a in ("dy", "dz") for i in (1, -1)]
    for f in friends:
        pl.semaphore_signal(barrier, inc=1, device_id=dev(**f), device_id_type=MESH)
    own_w = pl.ds(pl.multiple_of(c * VW, VW), VW)
    loads = [
        pltpu.make_async_copy(hidden.at[:, cols], hid.at[:, cols], lsem.at[11 + i])
        for i, cols in enumerate(pl.ds(i * D // 4, D // 4) for i in range(4))
    ]
    loads += [
        pltpu.make_async_copy(gain_in, gain, lsem.at[1]),
        pltpu.make_async_copy(head, w_all.at[:, own_w], lsem.at[2]),
    ]
    for cp in loads:
        cp.start()

    diag = lax.broadcasted_iota(jnp.int32, (CAP, 128), 0) == lax.broadcasted_iota(
        jnp.int32, (CAP, 128), 1
    )
    lane = lax.broadcasted_iota(jnp.int32, (8, 128), 1)
    sub8 = lax.broadcasted_iota(jnp.int32, (8, 128), 0)
    flat = sub8 * 128 + lane
    upper = sub8 < 4

    def to_col(row):
        return jnp.sum(jnp.where(diag, jnp.broadcast_to(row, (CAP, 128)), 0.0), axis=1, keepdims=True)

    def to_row(col, r0):
        n = col.shape[0]
        return jnp.sum(
            jnp.where(diag[r0 : r0 + n], jnp.broadcast_to(col, (n, 128)), 0.0), axis=0, keepdims=True
        )

    def spread(slot, ref):
        def one(r, acc):
            for q in range(NX):
                acc = jnp.where(flat == q * 128 + r, ref[(q * 2 + c) * CAP + r], acc)
            return acc

        acc = lax.fori_loop(0, CAP, one, jnp.zeros((8, 128), jnp.int32), unroll=4)
        ids[slot] = acc.astype(F32)

    spread(0, exit_ids)
    own_exit = to_col(ids[0, pl.ds(x, 1), :])

    def gain_rows(cols, e):
        g = jnp.broadcast_to(gain[0:1, cols], (CAP, cols.size))
        for i in range(1, EXITS):
            g = jnp.where(e == float(i), gain[i : i + 1, cols], g)
        return g

    def squares(i, acc):
        xs = hid[:, pl.ds(pl.multiple_of(i * 512, 512), 512)].astype(F32)
        xs = xs * xs
        for j in range(4):
            acc = acc + xs[:, j * 128 : (j + 1) * 128]
        return acc

    total_sq = jnp.zeros((CAP, 128), F32)
    for i in range(4):
        loads[i].wait()
        total_sq = lax.fori_loop(4 * i, 4 * i + 4, squares, total_sq)
    rinv = lax.rsqrt(jnp.sum(total_sq, axis=1, keepdims=True) / D + 1e-05)

    def norm_chunk(i, carry):
        cols = pl.ds(pl.multiple_of(i * 512, 512), 512)
        xs = hid[:, cols].astype(F32)
        n_all[0, :, cols] = (xs * rinv * gain_rows(cols, own_exit)).astype(BF16)
        return carry

    loads[4].wait()

    def columns(h, tag, d=0):
        zw, yw, bw, aw = WIDTHS[h]
        if tag == "z":
            return pl.ds(pl.multiple_of(lax.rem(z + d + NZ, NZ) * zw, 128), zw)
        if tag == "y":
            return pl.ds(pl.multiple_of(NZ * zw + lax.rem(y + d + NY, NY) * yw, 128), yw)
        return pl.ds(D - aw - bw, bw) if tag == "b" else pl.ds(D - aw, aw)

    def own_x(tag, h):
        rows, cols, far = pl.ds(*HALVES[h][:2]), columns(h, tag), tag in "zy"
        src = b[f"own{tag}{h}"] if far else n_all.at[0, rows, cols]
        k = slot()
        send(src, n_all.at[3, rows, cols], dev(dx=1), k)
        send(src, n_all.at[1, rows, cols], dev(dx=-1), k)
        cps[tag, h] = k, n_all.at[0:2, rows, cols]
        if far:
            dst = n_all.at[2, rows, cols]
            cps[tag, h, "far"] = send(src, dst, dev(dx=2)), dst

    def chain(tag, h, n, axis, rel):
        half = n // 2
        r0, n_rows, n_low = HALVES[h]
        full, low, high = pl.ds(r0, n_rows), pl.ds(r0, n_low), pl.ds(r0 + n_low, n_rows - n_low)

        def begin():
            for sign in (1, -1):
                ref = n_all.at[rel, full, columns(h, tag)]
                cps[tag, h, rel, sign, 1] = send(ref, ref, dev(**{axis: sign})), ref

        def arrive(sign, k):
            arrived(*cps[tag, h, rel, sign, k])
            if k < half:
                rows = full if k < half - 1 else (low if sign == 1 else high)
                ref = n_all.at[rel, rows, columns(h, tag, -sign * k)]
                cps[tag, h, rel, sign, k + 1] = send(ref, ref, dev(**{axis: sign})), ref

        for k in range(1, half + 1):
            for sign in (1, -1):
                at(("c" + tag, h, rel, sign, k), arrive, sign, k)
        return begin

    def gather(h):
        def got(key, then):
            arrived(*cps[key])
            for fn in then:
                fn()

        def got_x(tag):
            arrived(*cps[tag, h])
            rows, cols = pl.ds(*HALVES[h][:2]), columns(h, tag)
            rel, dx = (1, -1) if tag == "b" else (3, 1)
            dst = n_all.at[2, rows, cols]
            cps[tag, h, 2] = send(n_all.at[rel, rows, cols], dst, dev(dx=dx)), dst

        for tag, n, axis in (("z", NZ, "dz"), ("y", NY, "dy")):
            more = [lambda k=k: own_x(*k) for k in AFTER.get((tag, h), ())]
            at((tag, h), got, (tag, h), [chain(tag, h, n, axis, rel) for rel in (1, 3)] + more)
            at((tag, h, "far"), got, (tag, h, "far"), [chain(tag, h, n, axis, 2)])
            for d in range(n):
                at(("lg", h, tag, d), logits, h, tag, d)
        for tag in "ba":
            at((tag, h), got_x, tag)
            at((tag, h, 2), lambda tag=tag: arrived(*cps[tag, h, 2]))
        at(("lg", h, "x"), logits, h, "x", 0)

    def logits(h, tag, d):
        r0, n_rows, _ = HALVES[h]
        first = D - sum(WIDTHS[h][2:])
        k = pl.ds(first, D - first) if tag == "x" else columns(h, tag, d)
        n = n_all[:, r0 : r0 + n_rows, k].reshape(NX * n_rows, k.size)
        part = jnp.dot(n, w_all[k, :], preferred_element_type=F32)
        logit[:, r0 : r0 + n_rows, :] += part.reshape(NX, n_rows, 2 * VW)

    def take_w():
        arrived(*cps["w"])
        logit[...] = jnp.zeros_like(logit)

    def turn_w(i):
        f = pl.ds(i * 512, 512)
        w_t[:, f] = jnp.transpose(w_all[f, :], (1, 0))

    def own_first(tag, h):
        (r0, n, _), cols = HALVES[h], columns(h, tag)
        rows = pl.ds(r0, n)
        xs = hid[rows, cols].astype(F32)
        g = jnp.broadcast_to(gain[0:1, cols], xs.shape)
        for i in range(1, EXITS):
            g = jnp.where(own_exit[r0 : r0 + n] == float(i), gain[i : i + 1, cols], g)
        b[f"own{tag}{h}"][...] = (xs * rinv[r0 : r0 + n] * g).astype(BF16)

    for h in range(2):
        for tag in "zy":
            own_first(tag, h)
    pl.semaphore_wait(barrier, len(friends))
    for tag, h in FIRST:
        own_x(tag, h)
    lax.fori_loop(0, D // 512, norm_chunk, 0)
    for h in range(2):
        gather(h)
    loads[5].wait()
    mine_w = w_all.at[:, own_w]
    cps["w"] = send(mine_w, mine_w, dev(dc=1)), mine_w
    at(("w",), take_w)
    for i in range(16):
        at(("turn", i), turn_w, i)

    def weights():
        spread(1, targets)
        weight = jnp.zeros((8, 128), F32)
        exits = ids[0]
        for i in range(EXITS):
            weight = jnp.where(exits == float(i), scale[i], weight)
        for q in range(NX):
            weight = jnp.where((sub8 == q) & (lane >= counts[q * 2 + c]), 0.0, weight)
        for h in range(2):
            r0, n_rows, _ = HALVES[h]
            st[h, 1] = jnp.where((sub8 < NX) & (lane >= r0) & (lane < r0 + n_rows), weight, 0.0)

    weights()

    entry = lax.broadcasted_iota(jnp.int32, (CAP, 2 * VW), 1)
    base = (x * 2 * NZ * NY + v) * VW
    entry = jnp.where(entry < VW, entry + base, entry + (base + (NZ * NY - 1) * VW)).astype(F32)

    def column(ref, rel, r0, n):
        return to_col(ref[pl.ds(lax.rem(x + rel, NX), 1), :])[r0 : r0 + n]

    def local_stats(h):
        r0, n, _ = HALVES[h]
        stats = [jnp.zeros((8, 128), F32)] * 4
        for rel in range(NX):
            l = logit[rel, r0 : r0 + n, :]
            hit = entry[:n] == column(ids.at[1], rel, r0, n)
            m = jnp.max(l, axis=1, keepdims=True)
            e = jnp.exp(l - m)
            values = (
                m,
                jnp.sum(e, axis=1, keepdims=True),
                jnp.sum(e * l, axis=1, keepdims=True),
                jnp.sum(jnp.where(hit, l, 0.0), axis=1, keepdims=True),
            )
            here = sub8 == lax.rem(x + rel, NX)
            for i in range(4):
                row = jnp.broadcast_to(to_row(values[i], r0), (8, 128))
                stats[i] = jnp.where(here, row, stats[i])
        first = jnp.where(upper, stats[0], pltpu.roll(stats[1], 4, 0))
        rest = jnp.where(upper, stats[2], pltpu.roll(stats[3], 4, 0))
        s1[h, z] = jnp.where(mine_lanes(h), first, pltpu.roll(rest, 64, 1))
        cps["s1", h] = slot()
        for i in range(1, NZ):
            send(s1.at[h, z], s1.at[h, z], dev(dz=i), cps["s1", h])

    def mine_lanes(h):
        r0, n, _ = HALVES[h]
        return (lane >= r0) & (lane < r0 + n)

    def merge(h, ref, n):
        own_lanes = mine_lanes(h)
        sets = [ref[q] for q in range(n)]
        peaks = [jnp.where(upper, a, pltpu.roll(a, 4, 0)) for a in sets]
        peak = peaks[0]
        for p in peaks[1:]:
            peak = jnp.maximum(peak, p)
        total = jnp.zeros((8, 128), F32)
        for a, p in zip(sets, peaks):
            f = jnp.exp(p - peak)
            total = total + a * jnp.where(own_lanes, f, jnp.where(upper, pltpu.roll(f, 64, 1), 1.0))
        return jnp.where(own_lanes & upper, peak, total)

    own = x * NY + y

    def stats_z(h):
        arrived(cps["s1", h], s1.at[h, 0 : NZ - 1])
        s2[h, own] = merge(h, s1.at[h], NZ)
        cps["s2", h] = slot()
        for i in range(NX):
            for j in range(NY):
                if i or j:
                    send(s2.at[h, own], s2.at[h, own], dev(dx=i, dy=j), cps["s2", h])

    losses = []

    def stats_xy(h):
        arrived(cps["s2", h], s2.at[h, 0 : NX * NY - 1])
        peak = merge(h, s2.at[h], NX * NY)
        mean = pltpu.roll(peak, 64, 1)
        total, chosen = pltpu.roll(peak, 4, 0), pltpu.roll(mean, 4, 0)
        lse = peak + jnp.log(total)
        weight = st[h, 1]
        live = weight != 0.0
        st[h, 0] = lse
        st[h, 2] = jnp.where(live, weight * (mean / total - chosen), 0.0)
        losses.append(jnp.where(live, weight * (lse - chosen), 0.0))
        if h == 1:
            own_loss = losses[0] + losses[1]
            own_loss = jnp.sum(jnp.sum(own_loss, axis=1, keepdims=True), axis=0, keepdims=True)
            loss_x[0] = jnp.broadcast_to(own_loss, (8, 128))
            cps["loss"] = send(loss_x.at[0], loss_x.at[1], dev(dc=1))
        r0, n, _ = HALVES[h]
        for rel in range(NX):
            lse_c, w_c = column(st.at[h, 0], rel, r0, n), column(st.at[h, 1], rel, r0, n)
            hit = jnp.where(entry[:n] == column(ids.at[1], rel, r0, n), 1.0, 0.0)
            p = jnp.exp(logit[rel, r0 : r0 + n, :] - lse_c)
            dl[rel, r0 : r0 + n, :] = (w_c * (p - hit)).astype(BF16)

    def grad_block(h, k, *then):
        r0, n, _ = HALVES[h]
        zz = lax.rem(z + ZORD[k], NZ)
        rows = dl[:, r0 : r0 + n, :].reshape(NX * n, 2 * VW)
        f = pl.ds(pl.multiple_of(zz * NY * VW, NY * VW), NY * VW)
        out = jnp.dot(rows, w_t[:, f], preferred_element_type=F32).astype(BF16)
        for yy in range(NY):
            ry = lax.rem(yy - y + NY, NY)
            for rx in range(NX):
                block = out[rx * n : (rx + 1) * n, yy * VW : (yy + 1) * VW]
                cut = [block[p[0] - r0 : p[0] - r0 + 16, p[1] : p[1] + p[2]] for p in PARTS[h]]
                b[f"px{h}"][rx, k, ry] = cut[0]
                b[f"pz{h}"][k, rx, ry] = cut[1]
                b[f"py{h}"][ry, rx, k] = cut[2]
        for fn in then:
            fn()

    def add_into(dst, srcs):
        def one(i, carry):
            acc = dst[i].astype(F32)
            for r in srcs:
                acc = acc + r[i].astype(F32)
            dst[i] = acc.astype(BF16)
            return carry

        lax.fori_loop(0, dst.shape[0], one, 0)

    def ring(tag, h, n, axis, n_chains, block, one_way, buf_a, buf_b, done):
        half = n // 2
        side = {1: 0, -1: 1}
        left = [n_chains]

        def begin(sign):
            for i in range(n_chains):
                src = one_way(block(half, i), sign)
                cps[tag, h, sign, 1, i] = send(src, buf_a.at[side[sign], i], dev(**{axis: sign}))

        def arrive(sign, k, i):
            arrived(cps[tag, h, sign, k, i], buf_a.at[side[sign], i] if k == 1 else buf_b.at[side[sign], i, k - 2])
            d = (sign * (half - k)) % n
            if k == 1:
                add_into(one_way(block(d, i), sign), [buf_a.at[side[sign], i]])
            else:
                add_into(block(d, i), [buf_b.at[side[sign], i, k - 2]])
            cps[tag, h, sign, k + 1, i] = send(
                block(d, i), buf_b.at[side[sign], i, k - 1], dev(**{axis: sign})
            )

        def finish(i):
            for sign in (1, -1):
                arrived(cps[tag, h, sign, half, i], buf_b.at[side[sign], i, half - 2])
            add_into(block(0, i), [buf_b.at[side[sign], i, half - 2] for sign in (1, -1)])
            left[0] -= 1
            if left[0] == 0:
                done()

        for k in range(1, half):
            for i in range(n_chains):
                for sign in (1, -1):
                    at((tag, h, sign, k, i), arrive, sign, k, i)
        for i in range(n_chains):
            at((tag, h, "fin", i), finish, i)
        return begin

    def direct(tag, h, n, axis, block, buf, done):
        def begin():
            cps[tag, h] = slot()
            for d in range(1, n):
                send(block(d), buf.at[d - 1], dev(**{axis: d}), cps[tag, h])

        def finish():
            arrived(cps[tag, h], buf)
            acc = block(0)[...].astype(F32)
            for d in range(1, n):
                acc = acc + buf[d - 1].astype(F32)
            done(acc)

        at((tag, h), finish)
        return begin

    def direct2(tag, h, axes, sizes, block, buf, done):
        pairs = [(i, j) for i in range(sizes[0]) for j in range(sizes[1]) if i or j]

        def begin():
            cps[tag, h] = slot()
            for q, (i, j) in enumerate(pairs):
                send(block(i, j), buf.at[q], dev(**{axes[0]: i, axes[1]: j}), cps[tag, h])

        def finish():
            arrived(cps[tag, h], buf)
            acc = block(0, 0)[...].astype(F32)
            for q in range(len(pairs)):
                acc = acc + buf[q].astype(F32)
            done(acc)

        at((tag, h), finish)
        return begin

    def reduce(h):
        px, pz, py = b[f"px{h}"], b[f"pz{h}"], b[f"py{h}"]
        cx, cz, cy = CHAINS[h]

        def put(i):
            r, l, w = PARTS[h][i]
            def fn(acc):
                dn[r : r + 16, l : l + w] = acc
            return fn

        def back(ref, begin):
            def fn(acc):
                ref[...] = acc.astype(BF16)
                begin()
            return fn

        def cut(m):
            return lambda r, sign: r.at[0:m] if sign == 1 else r.at[m : 2 * m]

        x3 = direct("x3", h, NZ, "dz", lambda d: px.at[0, ZPOS[d], 0], b[f"ex{h}"], put(0))
        x2 = direct("x2", h, NY, "dy", lambda d: px.at[0, :, d], b[f"cx{h}"], back(px.at[0, :, 0], x3))
        x1 = ring("x1", h, NX, "dx", cx, lambda d, i: px.at[d, :, i * NY // cx : (i + 1) * NY // cx], cut(4),
                  b[f"ax{h}"], b[f"bx{h}"], x2)
        if h in Z_AT_ONCE:
            z2 = direct2("z2", h, ("dy", "dx"), (NY, NX), lambda i, j: pz.at[7, j, i], b[f"ez{h}"], put(1))
        else:
            z3 = direct("z3", h, NX, "dx", lambda d: pz.at[7, d, 0], b[f"ez{h}"], put(1))
            z2 = direct("z2", h, NY, "dy", lambda d: pz.at[7, :, d], b[f"cz{h}"], back(pz.at[7, :, 0], z3))
        z1 = ring("z1", h, NZ, "dz", cz, lambda d, i: pz.at[ZPOS[d], :, i * NY // cz : (i + 1) * NY // cz], cut(2),
                  b[f"az{h}"], b[f"bz{h}"], z2)
        y3 = direct("y3", h, NZ, "dz", lambda d: py.at[0, 0, ZPOS[d]], b[f"ey{h}"], put(2))
        y2 = direct("y2", h, NX, "dx", lambda d: py.at[0, d], b[f"cy{h}"], back(py.at[0, 0], y3))
        y1 = ring("y1", h, NY, "dy", cy, lambda d, i: py.at[d, :, i * NZ // cy : (i + 1) * NZ // cy], cut(2),
                  b[f"ay{h}"], b[f"by{h}"], y2)
        then = {
            0: (lambda: z1(1), lambda: z1(-1)),
            3: (lambda: x1(1),),
            7: (lambda: x1(-1), lambda: y1(1), lambda: y1(-1)),
        }
        for k in range(NZ):
            at(("gb", h, k), grad_block, h, k, *then.get(k, ()))

    def head_chunk(j):
        f = pl.ds(j * 1024, 1024)
        n = n_all[:, :, f].reshape(ROWS, 1024)
        both = lax.dot_general(n, dl[...].reshape(ROWS, 2 * VW), TN, preferred_element_type=F32)
        first, second = both[:, :VW], both[:, VW:]
        mine[f, :] = jnp.where(c == 0, first, second)
        gs[f, :] = jnp.where(c == 0, second, first).astype(BF16)
        cps["g", j] = send(gs.at[f], gr.at[f], dev(dc=1))

    def head_sum(j):
        arrived(cps["g", j], gr.at[pl.ds(j * 1024, 1024)])

        def one(i, carry):
            f = pl.ds(pl.multiple_of(j * 1024 + i * 256, 256), 256)
            gr[f, :] = (mine[f, :] + gr[f, :].astype(F32)).astype(BF16)
            return carry

        lax.fori_loop(0, 4, one, 0)
        f = pl.ds(j * 1024, 1024)
        cp = pltpu.make_async_copy(gr.at[f], gw_out.at[f], lsem.at[3 + j])
        cp.start()
        outs.append(cp)

    for h in range(2):
        at(("ls", h), local_stats, h)
        at(("sz", h), stats_z, h)
        at(("sxy", h), stats_xy, h)
        reduce(h)
    for j in range(8):
        at(("head", j), head_chunk, j)
        at(("sum", j), head_sum, j)
    run()

    f = pl.ds(pl.multiple_of(v * VW, VW), VW)
    inner = to_col(st[0, 2, pl.ds(x, 1), :] + st[1, 2, pl.ds(x, 1), :])
    unit = hid[:, f].astype(F32) * rinv
    scaled = gain_rows(f, own_exit) * dn[...]
    gh_out[...] = (rinv * (scaled - unit * (inner / D))).astype(BF16)

    arrived(cps["loss"], loss_x.at[1])
    loss_out[...] = (loss_x[0, 0:1, 0:1] + loss_x[1, 0:1, 0:1]) / 512.0
    for cp in outs:
        cp.wait()
    for cp in pool:
        if cp is not None:
            cp.wait_send()
    assert not pending and slots[0] <= N_RECV, slots


def handover(loss, grad_weight, grad_hidden, loss_out, gw_out, gh_out, buf, small, total, sem):
    n = D // 4
    parts = [pl.ds(i * n, n) for i in range(4)]
    reads = [pltpu.make_async_copy(grad_weight.at[p], buf.at[p], sem.at[i]) for i, p in enumerate(parts)]
    writes = [pltpu.make_async_copy(buf.at[p], gw_out.at[p], sem.at[4 + i]) for i, p in enumerate(parts)]
    extra = [
        (pltpu.make_async_copy(grad_hidden, small, sem.at[8]), pltpu.make_async_copy(small, gh_out, sem.at[9])),
        (pltpu.make_async_copy(loss, total, sem.at[10]), pltpu.make_async_copy(total, loss_out, sem.at[11])),
    ]
    for r, _ in extra:
        r.start()
    for r in reads:
        r.start()
    for r, w in extra + list(zip(reads, writes)):
        r.wait()
        w.start()
    for w in writes + [w for _, w in extra]:
        w.wait()


def body(hidden, gain, exit_scale, head_weight, targets, exit_ids, counts):
    vmem = pl.BlockSpec(memory_space=pltpu.VMEM)
    smem = pl.BlockSpec(memory_space=pltpu.SMEM)
    hbm = pl.BlockSpec(memory_space=pl.ANY)
    dma = pltpu.SemaphoreType.DMA
    big = jax.ShapeDtypeStruct((D, VW), BF16)
    small = jax.ShapeDtypeStruct((CAP, VW), BF16)
    results = pl.pallas_call(
        kernel,
        out_shape=(jax.ShapeDtypeStruct((1, 1), F32), big, small),
        in_specs=[hbm, hbm, hbm, smem, smem, smem, smem],
        out_specs=(vmem, hbm, vmem),
        scratch_shapes=[pltpu.VMEM(*v) for v in SCRATCH.values()] + [dma((N_SEND,)), dma((N_RECV,)), dma((15,))],
        compiler_params=pltpu.CompilerParams(
            collective_id=0, has_side_effects=True, vmem_limit_bytes=60 * 2**20
        ),
        name="exit_head",
    )(hidden, gain, head_weight, targets, exit_ids, counts, exit_scale)
    loss, grad_weight, grad_hidden = pl.pallas_call(
        handover,
        out_shape=(jax.ShapeDtypeStruct((1, 1), F32), big, small),
        in_specs=[hbm, hbm, hbm],
        out_specs=(hbm, hbm, hbm),
        scratch_shapes=[
            pltpu.VMEM((D, VW), BF16), pltpu.VMEM((CAP, VW), BF16), pltpu.VMEM((1, 1), F32), dma((12,)),
        ],
        compiler_params=pltpu.CompilerParams(vmem_limit_bytes=58 * 2**20),
        name="handover",
    )(*results)
    return (loss.reshape(()), grad_weight, grad_hidden)


def solution(mesh):
    in_specs = (P("section", None), P(), P(), P(None, ("section", "vocab")), P(), P(), P())
    out_specs = (P(), P(None, ("section", "vocab")), P("section", "vocab"))
    return jax.shard_map(body, mesh=mesh, in_specs=in_specs, out_specs=out_specs, check_vma=False)
```

```python
import jax
import jax.numpy as jnp
from jax import lax
from jax.experimental import pallas as pl
from jax.experimental.pallas import tpu as pltpu
from jax.sharding import PartitionSpec as P

MESH = pl.DeviceIdType.MESH
NX, NZ, NY = 4, 8, 4
CAP = 80
D = 8192
VW = 256
ROWS = NX * CAP
EXITS = 4
F32 = jnp.float32
BF16 = jnp.bfloat16
def widths(zw, yw, bw):
    return zw, yw, bw, D - NZ * zw - NY * yw - bw


WIDTHS = (widths(384, 768, 1152), widths(384, 768, 1408))
ZORD = (4, 3, 5, 2, 6, 1, 7, 0)
ZPOS = {d: k for k, d in enumerate(ZORD)}
N_SEND = 40
N_RECV = 102
HALVES = ((0, 48, 32), (48, 32, 16))
PARTS = (((0, 0, 256), (16, 0, 256), (32, 0, 256)), ((48, 0, 128), (64, 0, 256), (48, 128, 128)))
FIRST = (('z', 0), ('y', 0), ('z', 1))
AFTER = {('z', 0): (('b', 0), ('a', 0)), ('y', 0): (('y', 1), ('b', 1), ('a', 1))}
CHAINS = ((4, 1, 2), (1, 2, 4))
Z_AT_ONCE = (0, 1)
TN = (((0,), (0,)), ((), ()))
ORDER = (
    ("z", 0), ("z", 0, "far"), ("y", 0), ("cz", 0, 1, 1, 1), ("cz", 0, 1, -1, 1), ("cz", 0, 3, 1, 1),
    ("cz", 0, 3, -1, 1), ("z", 1), ("y", 0, "far"), ("cz", 0, 2, 1, 1), ("cz", 0, 2, -1, 1), ("w",),
    ("z", 1, "far"), ("lg", 0, "z", 0), ("lg", 0, "z", 1), ("cz", 0, 1, 1, 2), ("cz", 0, 1, -1, 2),
    ("cy", 0, 1, 1, 1), ("cy", 0, 1, -1, 1), ("lg", 0, "z", 7), ("lg", 0, "y", 0), ("cz", 0, 3, 1, 2),
    ("cz", 0, 3, -1, 2), ("lg", 1, "z", 0), ("b", 0), ("cz", 1, 1, 1, 1), ("cz", 1, 1, -1, 1), ("turn", 0),
    ("cy", 0, 3, 1, 1), ("cy", 0, 3, -1, 1), ("turn", 1), ("cz", 1, 3, 1, 1), ("cz", 1, 3, -1, 1), ("turn", 2),
    ("cz", 0, 2, 1, 2), ("cz", 0, 2, -1, 2), ("lg", 0, "z", 2), ("lg", 0, "z", 6), ("a", 0), ("cz", 1, 2, 1, 1),
    ("cz", 1, 2, -1, 1), ("cy", 0, 2, 1, 1), ("cy", 0, 2, -1, 1), ("lg", 0, "y", 1), ("cy", 0, 1, -1, 2),
    ("cz", 0, 1, 1, 3), ("cz", 0, 1, -1, 3), ("lg", 0, "y", 3), ("y", 1), ("cy", 0, 1, 1, 2), ("lg", 1, "z", 1),
    ("cy", 0, 3, -1, 2), ("cz", 0, 3, 1, 3), ("cz", 0, 3, -1, 3), ("lg", 1, "z", 7), ("turn", 3),
    ("cz", 1, 1, 1, 2), ("cz", 1, 1, -1, 2), ("cy", 0, 3, 1, 2), ("y", 1, "far"), ("lg", 1, "y", 0),
    ("cz", 1, 3, 1, 2), ("cz", 1, 3, -1, 2), ("turn", 4), ("cy", 0, 2, -1, 2), ("cz", 0, 2, 1, 3),
    ("cz", 0, 2, -1, 3), ("lg", 0, "z", 3), ("cy", 0, 2, 1, 2), ("lg", 0, "z", 5), ("b", 1), ("cz", 1, 2, 1, 2),
    ("cz", 1, 2, -1, 2), ("cz", 0, 1, -1, 4), ("lg", 0, "y", 2), ("cz", 0, 1, 1, 4), ("cz", 0, 3, -1, 4),
    ("cy", 1, 1, 1, 1), ("cy", 1, 1, -1, 1), ("a", 1), ("lg", 1, "z", 2), ("cz", 0, 3, 1, 4), ("lg", 1, "z", 6),
    ("cz", 1, 1, -1, 3), ("cz", 1, 1, 1, 3), ("turn", 5), ("cy", 1, 3, 1, 1), ("cy", 1, 3, -1, 1),
    ("cz", 1, 3, -1, 3), ("turn", 6), ("cz", 1, 3, 1, 3), ("cz", 0, 2, -1, 4), ("turn", 7), ("cz", 0, 2, 1, 4),
    ("a", 0, 2), ("cy", 1, 2, 1, 1), ("cy", 1, 2, -1, 1), ("lg", 0, "z", 4), ("cz", 1, 2, -1, 3),
    ("cz", 1, 2, 1, 3), ("b", 0, 2), ("lg", 0, "x"), ("ls", 0), ("cy", 1, 1, 1, 2), ("cy", 1, 1, -1, 2),
    ("a", 1, 2), ("cz", 1, 1, -1, 4), ("cz", 1, 1, 1, 4), ("cz", 1, 3, -1, 4), ("cy", 1, 3, 1, 2),
    ("cy", 1, 3, -1, 2), ("cz", 1, 3, 1, 4), ("b", 1, 2), ("lg", 1, "z", 3), ("lg", 1, "z", 5),
    ("cy", 1, 2, 1, 2), ("cy", 1, 2, -1, 2), ("lg", 1, "y", 1), ("cz", 1, 2, -1, 4), ("cz", 1, 2, 1, 4),
    ("lg", 1, "z", 4), ("lg", 1, "y", 2), ("lg", 1, "y", 3), ("lg", 1, "x"), ("ls", 1), ("sz", 0), ("turn", 8),
    ("turn", 9), ("turn", 10), ("turn", 11), ("turn", 12), ("turn", 13), ("turn", 14), ("turn", 15), ("sz", 1),
    ("sxy", 0), ("gb", 0, 0), ("gb", 0, 1), ("gb", 0, 2), ("gb", 0, 3), ("gb", 0, 4), ("gb", 0, 5),
    ("gb", 0, 6), ("gb", 0, 7), ("sxy", 1), ("gb", 1, 0), ("z1", 0, 1, 1, 0), ("z1", 0, -1, 1, 0),
    ("x1", 0, 1, 1, 0), ("gb", 1, 1), ("gb", 1, 2), ("x1", 0, 1, 1, 1), ("gb", 1, 3), ("gb", 1, 4),
    ("x1", 0, 1, 1, 2), ("x1", 0, -1, 1, 0), ("gb", 1, 5), ("x1", 0, 1, 1, 3), ("x1", 0, -1, 1, 1),
    ("y1", 0, 1, 1, 0), ("y1", 0, -1, 1, 0), ("gb", 1, 6), ("z1", 1, 1, 1, 0), ("z1", 1, -1, 1, 0),
    ("x1", 0, -1, 1, 2), ("gb", 1, 7), ("z1", 1, 1, 1, 1), ("z1", 1, -1, 1, 1), ("x1", 0, -1, 1, 3),
    ("y1", 0, 1, 1, 1), ("y1", 0, -1, 1, 1), ("head", 0), ("head", 1), ("x1", 0, "fin", 0), ("z1", 0, 1, 2, 0),
    ("z1", 0, -1, 2, 0), ("x1", 1, 1, 1, 0), ("x1", 0, "fin", 1), ("head", 2), ("z1", 1, 1, 2, 0),
    ("z1", 1, -1, 2, 0), ("y1", 0, "fin", 0), ("y1", 1, 1, 1, 0), ("y1", 1, -1, 1, 0), ("x1", 0, "fin", 2),
    ("y1", 1, 1, 1, 1), ("y1", 1, -1, 1, 1), ("y1", 1, 1, 1, 2), ("y1", 1, -1, 1, 2), ("y1", 1, 1, 1, 3),
    ("z1", 1, 1, 2, 1), ("z1", 1, -1, 2, 1), ("y1", 1, -1, 1, 3), ("x1", 1, -1, 1, 0), ("head", 3), ("head", 4),
    ("x1", 0, "fin", 3), ("z1", 0, 1, 3, 0), ("z1", 0, -1, 3, 0), ("y1", 0, "fin", 1), ("y1", 1, "fin", 0),
    ("head", 5), ("z1", 1, 1, 3, 0), ("z1", 1, -1, 3, 0), ("y1", 1, "fin", 1), ("y1", 1, "fin", 2), ("head", 6),
    ("z1", 1, 1, 3, 1), ("z1", 1, -1, 3, 1), ("y1", 1, "fin", 3), ("x1", 1, "fin", 0), ("head", 7), ("sum", 0),
    ("sum", 1), ("sum", 2), ("z1", 0, "fin", 0), ("x2", 0), ("y2", 0), ("sum", 3), ("z1", 1, "fin", 0),
    ("sum", 4), ("sum", 5), ("sum", 6), ("y2", 1), ("x2", 1), ("z1", 1, "fin", 1), ("sum", 7), ("z2", 0),
    ("x3", 0), ("y3", 0), ("y3", 1), ("z2", 1), ("x3", 1),
)
RANK = {key: i for i, key in enumerate(ORDER)}


def scratch():
    out = dict(
        hid=((CAP, D), BF16), gain=((EXITS, D), F32), n_all=((NX, CAP, D), BF16), w_all=((D, 2 * VW), BF16), w_t=((2 * VW, D), BF16),
        logit=((NX, CAP, 2 * VW), F32), dl=((NX, CAP, 2 * VW), BF16),
        s1=((2, NZ, 8, 128), F32), s2=((2, NX * NY, 8, 128), F32),
        st=((2, 3, 8, 128), F32), ids=((2, 8, 128), F32), loss=((2, 8, 128), F32), dn=((CAP, VW), F32),
        mine=((D, VW), F32), gs=((D, VW), BF16), gr=((D, VW), BF16),
    )
    for h in range(2):
        lx, lz, ly = [p[2] for p in PARTS[h]]
        out[f"ownz{h}"] = ((HALVES[h][1], WIDTHS[h][0]), BF16)
        out[f"owny{h}"] = ((HALVES[h][1], WIDTHS[h][1]), BF16)
        out[f"px{h}"] = ((NX, NZ, NY, 16, lx), BF16)
        out[f"pz{h}"] = ((NZ, NX, NY, 16, lz), BF16)
        out[f"py{h}"] = ((NY, NX, NZ, 16, ly), BF16)
        cx, cz, cy = CHAINS[h]
        out[f"ax{h}"] = ((2, cx, 4, NY // cx, 16, lx), BF16)
        out[f"bx{h}"] = ((2, cx, 1, NZ, NY // cx, 16, lx), BF16)
        out[f"az{h}"] = ((2, cz, 2, NY // cz, 16, lz), BF16)
        out[f"bz{h}"] = ((2, cz, 3, NX, NY // cz, 16, lz), BF16)
        out[f"ay{h}"] = ((2, cy, 2, NZ // cy, 16, ly), BF16)
        out[f"by{h}"] = ((2, cy, 1, NX, NZ // cy, 16, ly), BF16)
        out[f"cx{h}"] = ((NY - 1, NZ, 16, lx), BF16)
        if h not in Z_AT_ONCE:
            out[f"cz{h}"] = ((NY - 1, NX, 16, lz), BF16)
        out[f"cy{h}"] = ((NX - 1, NZ, 16, ly), BF16)
        out[f"ex{h}"] = ((NZ - 1, 16, lx), BF16)
        out[f"ez{h}"] = (((NX * NY if h in Z_AT_ONCE else NX) - 1, 16, lz), BF16)
        out[f"ey{h}"] = ((NZ - 1, 16, ly), BF16)
    return out


SCRATCH = scratch()


def kernel(hidden, gain_in, head, targets, exit_ids, counts, scale, loss_out, gw_out, gh_out, *refs):
    b = dict(zip(SCRATCH, refs))
    ssem, rsem, lsem = refs[len(SCRATCH) :]
    hid, gain, n_all, w_all, w_t = b["hid"], b["gain"], b["n_all"], b["w_all"], b["w_t"]
    logit, dl, s1, s2, st, ids = b["logit"], b["dl"], b["s1"], b["s2"], b["st"], b["ids"]
    dn, mine, gs, gr, loss_x = b["dn"], b["mine"], b["gs"], b["gr"], b["loss"]
    s = lax.axis_index("section")
    v = lax.axis_index("vocab")
    x, c = lax.div(s, 2), lax.rem(s, 2)
    z, y = lax.div(v, NY), lax.rem(v, NY)

    def dev(dx=0, dc=0, dz=0, dy=0):
        return (
            lax.rem(x + dx + NX, NX) * 2 + lax.rem(c + dc, 2),
            lax.rem(z + dz + NZ, NZ) * NY + lax.rem(y + dy + NY, NY),
        )

    slots = [0]
    pool = [None] * N_SEND
    count = [0]
    pending = {}
    outs = []
    cps = {}
    events = []

    def slot():
        slots[0] += 1
        return slots[0] - 1

    gathered = ([], [])

    def slot_of(h):
        gathered[h].append(slot())
        return gathered[h][-1]

    def spare(h):
        k = gathered[h].pop(0) if gathered[h] else slot()
        assert k not in pending
        return k

    def send(src, dst, device, at_slot=None):
        at_slot = slot() if at_slot is None else at_slot
        i = count[0] % N_SEND
        count[0] += 1
        if pool[i] is not None:
            pool[i].wait_send()
        cp = pltpu.make_async_remote_copy(
            src_ref=src, dst_ref=dst, send_sem=ssem.at[i], recv_sem=rsem.at[at_slot],
            device_id=device, device_id_type=MESH,
        )
        cp.start()
        pool[i] = cp
        pending.setdefault(at_slot, []).append(cp)
        return at_slot

    def arrived(at_slot, ref):
        pltpu.make_async_copy(ref, ref, rsem.at[at_slot]).wait()
        del pending[at_slot]

    def at(key, fn, *args):
        events.append((RANK[key], lambda: fn(*args)))

    def run():
        assert len(events) == len(RANK)
        for t_, fn in sorted(events, key=lambda e: e[0]):
            fn()

    barrier = pltpu.get_barrier_semaphore()
    friends = [dict(dc=1)]
    friends += [dict(dx=i) for i in range(1, NX)] + [{a: i} for a in ("dy", "dz") for i in (1, -1)]
    for f in friends:
        pl.semaphore_signal(barrier, inc=1, device_id=dev(**f), device_id_type=MESH)
    own_w = pl.ds(pl.multiple_of(c * VW, VW), VW)
    loads = [
        pltpu.make_async_copy(hidden.at[:, cols], hid.at[:, cols], lsem.at[11 + i])
        for i, cols in enumerate(pl.ds(i * D // 4, D // 4) for i in range(4))
    ]
    loads += [
        pltpu.make_async_copy(gain_in, gain, lsem.at[1]),
        pltpu.make_async_copy(head, w_all.at[:, own_w], lsem.at[2]),
    ]
    for cp in loads:
        cp.start()

    diag = lax.broadcasted_iota(jnp.int32, (CAP, 128), 0) == lax.broadcasted_iota(
        jnp.int32, (CAP, 128), 1
    )
    lane = lax.broadcasted_iota(jnp.int32, (8, 128), 1)
    sub8 = lax.broadcasted_iota(jnp.int32, (8, 128), 0)
    flat = sub8 * 128 + lane
    upper = sub8 < 4

    def to_col(row):
        return jnp.sum(jnp.where(diag, jnp.broadcast_to(row, (CAP, 128)), 0.0), axis=1, keepdims=True)

    def to_row(col, r0):
        n = col.shape[0]
        return jnp.sum(
            jnp.where(diag[r0 : r0 + n], jnp.broadcast_to(col, (n, 128)), 0.0), axis=0, keepdims=True
        )

    def spread(slot, ref):
        def one(r, acc):
            for q in range(NX):
                acc = jnp.where(flat == q * 128 + r, ref[(q * 2 + c) * CAP + r], acc)
            return acc

        acc = lax.fori_loop(0, CAP, one, jnp.zeros((8, 128), jnp.int32), unroll=4)
        ids[slot] = acc.astype(F32)

    spread(0, exit_ids)
    own_exit = to_col(ids[0, pl.ds(x, 1), :])

    def gain_rows(cols, e):
        g = jnp.broadcast_to(gain[0:1, cols], (CAP, cols.size))
        for i in range(1, EXITS):
            g = jnp.where(e == float(i), gain[i : i + 1, cols], g)
        return g

    def squares(i, acc):
        xs = hid[:, pl.ds(pl.multiple_of(i * 512, 512), 512)].astype(F32)
        xs = xs * xs
        for j in range(4):
            acc = acc + xs[:, j * 128 : (j + 1) * 128]
        return acc

    total_sq = jnp.zeros((CAP, 128), F32)
    for i in range(4):
        loads[i].wait()
        total_sq = lax.fori_loop(4 * i, 4 * i + 4, squares, total_sq)
    rinv = lax.rsqrt(jnp.sum(total_sq, axis=1, keepdims=True) / D + 1e-05)

    def norm_chunk(i, carry):
        cols = pl.ds(pl.multiple_of(i * 512, 512), 512)
        xs = hid[:, cols].astype(F32)
        n_all[0, :, cols] = (xs * rinv * gain_rows(cols, own_exit)).astype(BF16)
        return carry

    loads[4].wait()

    def columns(h, tag, d=0):
        zw, yw, bw, aw = WIDTHS[h]
        if tag == "z":
            return pl.ds(pl.multiple_of(lax.rem(z + d + NZ, NZ) * zw, 128), zw)
        if tag == "y":
            return pl.ds(pl.multiple_of(NZ * zw + lax.rem(y + d + NY, NY) * yw, 128), yw)
        return pl.ds(D - aw - bw, bw) if tag == "b" else pl.ds(D - aw, aw)

    def own_x(tag, h):
        rows, cols, far = pl.ds(*HALVES[h][:2]), columns(h, tag), tag in "zy"
        src = b[f"own{tag}{h}"] if far else n_all.at[0, rows, cols]
        k = slot_of(h)
        send(src, n_all.at[3, rows, cols], dev(dx=1), k)
        send(src, n_all.at[1, rows, cols], dev(dx=-1), k)
        cps[tag, h] = k, n_all.at[0:2, rows, cols]
        if far:
            dst = n_all.at[2, rows, cols]
            cps[tag, h, "far"] = send(src, dst, dev(dx=2), slot_of(h)), dst

    def chain(tag, h, n, axis, rel):
        half = n // 2
        r0, n_rows, n_low = HALVES[h]
        full, low, high = pl.ds(r0, n_rows), pl.ds(r0, n_low), pl.ds(r0 + n_low, n_rows - n_low)

        def begin():
            for sign in (1, -1):
                ref = n_all.at[rel, full, columns(h, tag)]
                cps[tag, h, rel, sign, 1] = send(ref, ref, dev(**{axis: sign}), slot_of(h)), ref

        def arrive(sign, k):
            arrived(*cps[tag, h, rel, sign, k])
            if k < half:
                rows = full if k < half - 1 else (low if sign == 1 else high)
                ref = n_all.at[rel, rows, columns(h, tag, -sign * k)]
                cps[tag, h, rel, sign, k + 1] = send(ref, ref, dev(**{axis: sign}), slot_of(h)), ref

        for k in range(1, half + 1):
            for sign in (1, -1):
                at(("c" + tag, h, rel, sign, k), arrive, sign, k)
        return begin

    def gather(h):
        def got(key, then):
            arrived(*cps[key])
            for fn in then:
                fn()

        def got_x(tag):
            arrived(*cps[tag, h])
            rows, cols = pl.ds(*HALVES[h][:2]), columns(h, tag)
            rel, dx = (1, -1) if tag == "b" else (3, 1)
            dst = n_all.at[2, rows, cols]
            cps[tag, h, 2] = send(n_all.at[rel, rows, cols], dst, dev(dx=dx), slot_of(h)), dst

        for tag, n, axis in (("z", NZ, "dz"), ("y", NY, "dy")):
            more = [lambda k=k: own_x(*k) for k in AFTER.get((tag, h), ())]
            at((tag, h), got, (tag, h), [chain(tag, h, n, axis, rel) for rel in (1, 3)] + more)
            at((tag, h, "far"), got, (tag, h, "far"), [chain(tag, h, n, axis, 2)])
            for d in range(n):
                at(("lg", h, tag, d), logits, h, tag, d)
        for tag in "ba":
            at((tag, h), got_x, tag)
            at((tag, h, 2), lambda tag=tag: arrived(*cps[tag, h, 2]))
        at(("lg", h, "x"), logits, h, "x", 0)

    def logits(h, tag, d):
        r0, n_rows, _ = HALVES[h]
        first = D - sum(WIDTHS[h][2:])
        k = pl.ds(first, D - first) if tag == "x" else columns(h, tag, d)
        n = n_all[:, r0 : r0 + n_rows, k].reshape(NX * n_rows, k.size)
        part = jnp.dot(n, w_all[k, :], preferred_element_type=F32)
        logit[:, r0 : r0 + n_rows, :] += part.reshape(NX, n_rows, 2 * VW)

    def take_w():
        arrived(*cps["w"])
        logit[...] = jnp.zeros_like(logit)

    def turn_w(i):
        f = pl.ds(i * 512, 512)
        w_t[:, f] = jnp.transpose(w_all[f, :], (1, 0))

    def own_first(tag, h):
        (r0, n, _), cols = HALVES[h], columns(h, tag)
        rows = pl.ds(r0, n)
        xs = hid[rows, cols].astype(F32)
        g = jnp.broadcast_to(gain[0:1, cols], xs.shape)
        for i in range(1, EXITS):
            g = jnp.where(own_exit[r0 : r0 + n] == float(i), gain[i : i + 1, cols], g)
        b[f"own{tag}{h}"][...] = (xs * rinv[r0 : r0 + n] * g).astype(BF16)

    for h in range(2):
        for tag in "zy":
            own_first(tag, h)
    pl.semaphore_wait(barrier, len(friends))
    for tag, h in FIRST:
        own_x(tag, h)
    lax.fori_loop(0, D // 512, norm_chunk, 0)
    for h in range(2):
        gather(h)
    loads[5].wait()
    mine_w = w_all.at[:, own_w]
    cps["w"] = send(mine_w, mine_w, dev(dc=1)), mine_w
    at(("w",), take_w)
    for i in range(16):
        at(("turn", i), turn_w, i)

    def weights():
        spread(1, targets)
        weight = jnp.zeros((8, 128), F32)
        exits = ids[0]
        for i in range(EXITS):
            weight = jnp.where(exits == float(i), scale[i], weight)
        for q in range(NX):
            weight = jnp.where((sub8 == q) & (lane >= counts[q * 2 + c]), 0.0, weight)
        for h in range(2):
            r0, n_rows, _ = HALVES[h]
            st[h, 1] = jnp.where((sub8 < NX) & (lane >= r0) & (lane < r0 + n_rows), weight, 0.0)

    weights()

    entry = lax.broadcasted_iota(jnp.int32, (CAP, 2 * VW), 1)
    base = (x * 2 * NZ * NY + v) * VW
    entry = jnp.where(entry < VW, entry + base, entry + (base + (NZ * NY - 1) * VW)).astype(F32)

    def column(ref, rel, r0, n):
        return to_col(ref[pl.ds(lax.rem(x + rel, NX), 1), :])[r0 : r0 + n]

    def local_stats(h):
        r0, n, _ = HALVES[h]
        stats = [jnp.zeros((8, 128), F32)] * 4
        for rel in range(NX):
            l = logit[rel, r0 : r0 + n, :]
            hit = entry[:n] == column(ids.at[1], rel, r0, n)
            m = jnp.max(l, axis=1, keepdims=True)
            e = jnp.exp(l - m)
            values = (
                m,
                jnp.sum(e, axis=1, keepdims=True),
                jnp.sum(e * l, axis=1, keepdims=True),
                jnp.sum(jnp.where(hit, l, 0.0), axis=1, keepdims=True),
            )
            here = sub8 == lax.rem(x + rel, NX)
            for i in range(4):
                row = jnp.broadcast_to(to_row(values[i], r0), (8, 128))
                stats[i] = jnp.where(here, row, stats[i])
        first = jnp.where(upper, stats[0], pltpu.roll(stats[1], 4, 0))
        rest = jnp.where(upper, stats[2], pltpu.roll(stats[3], 4, 0))
        s1[h, z] = jnp.where(mine_lanes(h), first, pltpu.roll(rest, 64, 1))
        cps["s1", h] = slot()
        for i in range(1, NZ):
            send(s1.at[h, z], s1.at[h, z], dev(dz=i), cps["s1", h])

    def mine_lanes(h):
        r0, n, _ = HALVES[h]
        return (lane >= r0) & (lane < r0 + n)

    def merge(h, ref, n):
        own_lanes = mine_lanes(h)
        sets = [ref[q] for q in range(n)]
        peaks = [jnp.where(upper, a, pltpu.roll(a, 4, 0)) for a in sets]
        peak = peaks[0]
        for p in peaks[1:]:
            peak = jnp.maximum(peak, p)
        total = jnp.zeros((8, 128), F32)
        for a, p in zip(sets, peaks):
            f = jnp.exp(p - peak)
            total = total + a * jnp.where(own_lanes, f, jnp.where(upper, pltpu.roll(f, 64, 1), 1.0))
        return jnp.where(own_lanes & upper, peak, total)

    own = x * NY + y

    def stats_z(h):
        arrived(cps["s1", h], s1.at[h, 0 : NZ - 1])
        s2[h, own] = merge(h, s1.at[h], NZ)
        cps["s2", h] = slot()
        for i in range(NX):
            for j in range(NY):
                if i or j:
                    send(s2.at[h, own], s2.at[h, own], dev(dx=i, dy=j), cps["s2", h])

    losses = []

    def stats_xy(h):
        arrived(cps["s2", h], s2.at[h, 0 : NX * NY - 1])
        peak = merge(h, s2.at[h], NX * NY)
        mean = pltpu.roll(peak, 64, 1)
        total, chosen = pltpu.roll(peak, 4, 0), pltpu.roll(mean, 4, 0)
        lse = peak + jnp.log(total)
        weight = st[h, 1]
        live = weight != 0.0
        st[h, 0] = lse
        st[h, 2] = jnp.where(live, weight * (mean / total - chosen), 0.0)
        losses.append(jnp.where(live, weight * (lse - chosen), 0.0))
        if h == 1:
            own_loss = losses[0] + losses[1]
            own_loss = jnp.sum(jnp.sum(own_loss, axis=1, keepdims=True), axis=0, keepdims=True)
            loss_x[0] = jnp.broadcast_to(own_loss, (8, 128))
            cps["loss"] = send(loss_x.at[0], loss_x.at[1], dev(dc=1))
        r0, n, _ = HALVES[h]
        for rel in range(NX):
            lse_c, w_c = column(st.at[h, 0], rel, r0, n), column(st.at[h, 1], rel, r0, n)
            hit = jnp.where(entry[:n] == column(ids.at[1], rel, r0, n), 1.0, 0.0)
            p = jnp.exp(logit[rel, r0 : r0 + n, :] - lse_c)
            dl[rel, r0 : r0 + n, :] = (w_c * (p - hit)).astype(BF16)

    def grad_block(h, k, *then):
        r0, n, _ = HALVES[h]
        zz = lax.rem(z + ZORD[k], NZ)
        rows = dl[:, r0 : r0 + n, :].reshape(NX * n, 2 * VW)
        f = pl.ds(pl.multiple_of(zz * NY * VW, NY * VW), NY * VW)
        out = jnp.dot(rows, w_t[:, f], preferred_element_type=F32).astype(BF16)
        for yy in range(NY):
            ry = lax.rem(yy - y + NY, NY)
            for rx in range(NX):
                block = out[rx * n : (rx + 1) * n, yy * VW : (yy + 1) * VW]
                cut = [block[p[0] - r0 : p[0] - r0 + 16, p[1] : p[1] + p[2]] for p in PARTS[h]]
                b[f"px{h}"][rx, k, ry] = cut[0]
                b[f"pz{h}"][k, rx, ry] = cut[1]
                b[f"py{h}"][ry, rx, k] = cut[2]
        for fn in then:
            fn()

    def add_into(dst, srcs):
        def one(i, carry):
            acc = dst[i].astype(F32)
            for r in srcs:
                acc = acc + r[i].astype(F32)
            dst[i] = acc.astype(BF16)
            return carry

        lax.fori_loop(0, dst.shape[0], one, 0)

    def ring(tag, h, n, axis, n_chains, block, one_way, buf_a, buf_b, done):
        half = n // 2
        side = {1: 0, -1: 1}
        left = [n_chains]

        def begin(sign):
            for i in range(n_chains):
                src = one_way(block(half, i), sign)
                cps[tag, h, sign, 1, i] = send(src, buf_a.at[side[sign], i], dev(**{axis: sign}), spare(h))

        def arrive(sign, k, i):
            arrived(cps[tag, h, sign, k, i], buf_a.at[side[sign], i] if k == 1 else buf_b.at[side[sign], i, k - 2])
            d = (sign * (half - k)) % n
            if k == 1:
                add_into(one_way(block(d, i), sign), [buf_a.at[side[sign], i]])
            else:
                add_into(block(d, i), [buf_b.at[side[sign], i, k - 2]])
            cps[tag, h, sign, k + 1, i] = send(
                block(d, i), buf_b.at[side[sign], i, k - 1], dev(**{axis: sign}), spare(h)
            )

        def finish(i):
            for sign in (1, -1):
                arrived(cps[tag, h, sign, half, i], buf_b.at[side[sign], i, half - 2])
            add_into(block(0, i), [buf_b.at[side[sign], i, half - 2] for sign in (1, -1)])
            left[0] -= 1
            if left[0] == 0:
                done()

        for k in range(1, half):
            for i in range(n_chains):
                for sign in (1, -1):
                    at((tag, h, sign, k, i), arrive, sign, k, i)
        for i in range(n_chains):
            at((tag, h, "fin", i), finish, i)
        return begin

    def direct(tag, h, n, axis, block, buf, done):
        def begin():
            cps[tag, h] = spare(h)
            for d in range(1, n):
                send(block(d), buf.at[d - 1], dev(**{axis: d}), cps[tag, h])

        def finish():
            arrived(cps[tag, h], buf)
            acc = block(0)[...].astype(F32)
            for d in range(1, n):
                acc = acc + buf[d - 1].astype(F32)
            done(acc)

        at((tag, h), finish)
        return begin

    def direct2(tag, h, axes, sizes, block, buf, done):
        pairs = [(i, j) for i in range(sizes[0]) for j in range(sizes[1]) if i or j]

        def begin():
            cps[tag, h] = spare(h)
            for q, (i, j) in enumerate(pairs):
                send(block(i, j), buf.at[q], dev(**{axes[0]: i, axes[1]: j}), cps[tag, h])

        def finish():
            arrived(cps[tag, h], buf)
            acc = block(0, 0)[...].astype(F32)
            for q in range(len(pairs)):
                acc = acc + buf[q].astype(F32)
            done(acc)

        at((tag, h), finish)
        return begin

    def reduce(h):
        px, pz, py = b[f"px{h}"], b[f"pz{h}"], b[f"py{h}"]
        cx, cz, cy = CHAINS[h]

        def put(i):
            r, l, w = PARTS[h][i]
            def fn(acc):
                dn[r : r + 16, l : l + w] = acc
            return fn

        def back(ref, begin):
            def fn(acc):
                ref[...] = acc.astype(BF16)
                begin()
            return fn

        def cut(m):
            return lambda r, sign: r.at[0:m] if sign == 1 else r.at[m : 2 * m]

        x3 = direct("x3", h, NZ, "dz", lambda d: px.at[0, ZPOS[d], 0], b[f"ex{h}"], put(0))
        x2 = direct("x2", h, NY, "dy", lambda d: px.at[0, :, d], b[f"cx{h}"], back(px.at[0, :, 0], x3))
        x1 = ring("x1", h, NX, "dx", cx, lambda d, i: px.at[d, :, i * NY // cx : (i + 1) * NY // cx], cut(4),
                  b[f"ax{h}"], b[f"bx{h}"], x2)
        if h in Z_AT_ONCE:
            z2 = direct2("z2", h, ("dy", "dx"), (NY, NX), lambda i, j: pz.at[7, j, i], b[f"ez{h}"], put(1))
        else:
            z3 = direct("z3", h, NX, "dx", lambda d: pz.at[7, d, 0], b[f"ez{h}"], put(1))
            z2 = direct("z2", h, NY, "dy", lambda d: pz.at[7, :, d], b[f"cz{h}"], back(pz.at[7, :, 0], z3))
        z1 = ring("z1", h, NZ, "dz", cz, lambda d, i: pz.at[ZPOS[d], :, i * NY // cz : (i + 1) * NY // cz], cut(2),
                  b[f"az{h}"], b[f"bz{h}"], z2)
        y3 = direct("y3", h, NZ, "dz", lambda d: py.at[0, 0, ZPOS[d]], b[f"ey{h}"], put(2))
        y2 = direct("y2", h, NX, "dx", lambda d: py.at[0, d], b[f"cy{h}"], back(py.at[0, 0], y3))
        y1 = ring("y1", h, NY, "dy", cy, lambda d, i: py.at[d, :, i * NZ // cy : (i + 1) * NZ // cy], cut(2),
                  b[f"ay{h}"], b[f"by{h}"], y2)
        then = {
            0: (lambda: z1(1), lambda: z1(-1)),
            3: (lambda: x1(1),),
            7: (lambda: x1(-1), lambda: y1(1), lambda: y1(-1)),
        }
        for k in range(NZ):
            at(("gb", h, k), grad_block, h, k, *then.get(k, ()))

    def head_chunk(j):
        f = pl.ds(j * 1024, 1024)
        n = n_all[:, :, f].reshape(ROWS, 1024)
        both = lax.dot_general(n, dl[...].reshape(ROWS, 2 * VW), TN, preferred_element_type=F32)
        first, second = both[:, :VW], both[:, VW:]
        mine[f, :] = jnp.where(c == 0, first, second)
        gs[f, :] = jnp.where(c == 0, second, first).astype(BF16)
        cps["g", j] = send(gs.at[f], gr.at[f], dev(dc=1))

    def head_sum(j):
        arrived(cps["g", j], gr.at[pl.ds(j * 1024, 1024)])

        def one(i, carry):
            f = pl.ds(pl.multiple_of(j * 1024 + i * 256, 256), 256)
            gr[f, :] = (mine[f, :] + gr[f, :].astype(F32)).astype(BF16)
            return carry

        lax.fori_loop(0, 4, one, 0)
        f = pl.ds(j * 1024, 1024)
        cp = pltpu.make_async_copy(gr.at[f], gw_out.at[f], lsem.at[3 + j])
        cp.start()
        outs.append(cp)

    for h in range(2):
        at(("ls", h), local_stats, h)
        at(("sz", h), stats_z, h)
        at(("sxy", h), stats_xy, h)
        reduce(h)
    for j in range(8):
        at(("head", j), head_chunk, j)
        at(("sum", j), head_sum, j)
    run()

    f = pl.ds(pl.multiple_of(v * VW, VW), VW)
    inner = to_col(st[0, 2, pl.ds(x, 1), :] + st[1, 2, pl.ds(x, 1), :])
    unit = hid[:, f].astype(F32) * rinv
    scaled = gain_rows(f, own_exit) * dn[...]
    gh_out[...] = (rinv * (scaled - unit * (inner / D))).astype(BF16)

    arrived(cps["loss"], loss_x.at[1])
    loss_out[...] = (loss_x[0, 0:1, 0:1] + loss_x[1, 0:1, 0:1]) / 512.0
    for cp in outs:
        cp.wait()
    for cp in pool:
        if cp is not None:
            cp.wait_send()
    assert not pending and slots[0] <= N_RECV, slots


def handover(loss, grad_weight, grad_hidden, loss_out, gw_out, gh_out, buf, small, total, sem):
    n = D // 4
    parts = [pl.ds(i * n, n) for i in range(4)]
    reads = [pltpu.make_async_copy(grad_weight.at[p], buf.at[p], sem.at[i]) for i, p in enumerate(parts)]
    writes = [pltpu.make_async_copy(buf.at[p], gw_out.at[p], sem.at[4 + i]) for i, p in enumerate(parts)]
    extra = [
        (pltpu.make_async_copy(grad_hidden, small, sem.at[8]), pltpu.make_async_copy(small, gh_out, sem.at[9])),
        (pltpu.make_async_copy(loss, total, sem.at[10]), pltpu.make_async_copy(total, loss_out, sem.at[11])),
    ]
    for r, _ in extra:
        r.start()
    for r in reads:
        r.start()
    for r, w in extra + list(zip(reads, writes)):
        r.wait()
        w.start()
    for w in writes + [w for _, w in extra]:
        w.wait()


def body(hidden, gain, exit_scale, head_weight, targets, exit_ids, counts):
    vmem = pl.BlockSpec(memory_space=pltpu.VMEM)
    smem = pl.BlockSpec(memory_space=pltpu.SMEM)
    hbm = pl.BlockSpec(memory_space=pl.ANY)
    dma = pltpu.SemaphoreType.DMA
    big = jax.ShapeDtypeStruct((D, VW), BF16)
    small = jax.ShapeDtypeStruct((CAP, VW), BF16)
    results = pl.pallas_call(
        kernel,
        out_shape=(jax.ShapeDtypeStruct((1, 1), F32), big, small),
        in_specs=[hbm, hbm, hbm, smem, smem, smem, smem],
        out_specs=(vmem, hbm, vmem),
        scratch_shapes=[pltpu.VMEM(*v) for v in SCRATCH.values()] + [dma((N_SEND,)), dma((N_RECV,)), dma((15,))],
        compiler_params=pltpu.CompilerParams(
            collective_id=0, has_side_effects=True, vmem_limit_bytes=60 * 2**20
        ),
        name="exit_head",
    )(hidden, gain, head_weight, targets, exit_ids, counts, exit_scale)
    loss, grad_weight, grad_hidden = pl.pallas_call(
        handover,
        out_shape=(jax.ShapeDtypeStruct((1, 1), F32), big, small),
        in_specs=[hbm, hbm, hbm],
        out_specs=(hbm, hbm, hbm),
        scratch_shapes=[
            pltpu.VMEM((D, VW), BF16), pltpu.VMEM((CAP, VW), BF16), pltpu.VMEM((1, 1), F32), dma((12,)),
        ],
        compiler_params=pltpu.CompilerParams(vmem_limit_bytes=58 * 2**20),
        name="handover",
    )(*results)
    return (loss.reshape(()), grad_weight, grad_hidden)


def solution(mesh):
    in_specs = (P("section", None), P(), P(), P(None, ("section", "vocab")), P(), P(), P())
    out_specs = (P(), P(None, ("section", "vocab")), P("section", "vocab"))
    return jax.shard_map(body, mesh=mesh, in_specs=in_specs, out_specs=out_specs, check_vma=False)
```
